256 devices in a mesh: src: 8 (over y, core), tgt: 32 (over x, z).
Axes of the slice: x: 4, y: 4, z: 8, core: 2. Of those that a mesh axis runs over, the one named last changes fastest.
Arguments:
- cost: bfloat16 [8, 96, 1024, 1024], P('src', 'tgt'), may hold values from -60 to 4
- cost_scale: float32 [8, 96], P('src', 'tgt'), may hold values from 0.5 to 2
- slot_block_row: int32 [8, 96], P('src', 'tgt'), may hold values from 0 to 31, as said below
- slot_block_column: int32 [8, 96], P('src', 'tgt'), may hold values from 0 to 127, as said below
- device_block_count: int32 [8, 32], P('src', 'tgt'), may hold values from 1 to 3, as said below
- log_a: float32 [32768], P('src'), may hold values from -1 to 1
- log_b: float32 [131072], P('tgt'), may hold values from -1 to 1
- labels: bfloat16 [32768, 64], P(('src', 'tgt')), may hold values from 0 to 1
Outputs:
- f_pot: float32 [32768], P('src')
- g_pot: float32 [131072], P('tgt')
- transported: bfloat16 [131072, 64], P('tgt')
The draws below stay inside these ranges and needn't reach their ends.
Inputs may be any that keep to these rules, and one draw needn't show every extreme that they name: `device_block_count`: live slots of one device; slot 0 is always live and some device has 3. `slot_block_row`: block rows of device (i, j) lie in i * 4 to i * 4 + 3; the blocks of one device are distinct; every block row and every block column holds a live block. `slot_block_column`: block columns of device (i, j) lie in j * 4 to j * 4 + 3.
All inputs are finite; a program needn't handle non-finite values.
Results may differ from the reference program's by a relative error of at most 0.0043.
Values may be sent and summed in bfloat16 or wider, within the bound.
No kernel may reach another device: no remote copies, remote signals or barrier semaphores. Data moves between devices by JAX's collectives and lax.ppermute only.
A program may use at most 64 MiB of HBM per device.

```python
import math
import jax
import jax.numpy as jnp
from jax import lax

BLOCK = 1024
CLASSES = 64
RB = 4
CB = 4
BLK_DEV = 3
ITERS = 4
SOURCES = 32768
TARGETS = 131072
N_SRC = 8
N_TGT = 32


def pattern(key):
    key_count, key_order, key_pick = jax.random.split(key, 3)
    src_ids = jnp.arange(N_SRC, dtype=jnp.int32)[:, None]
    tgt_ids = jnp.arange(N_TGT, dtype=jnp.int32)[None, :]
    first = tgt_ids % RB * CB + src_ids % CB
    spots = RB * CB
    scores = jax.random.randint(key_order, (N_SRC, N_TGT, spots - 1), 0, 1 << 20)
    scores = scores * 64 + jnp.arange(spots - 1, dtype=jnp.int32)
    order = jnp.argsort(scores, axis=-1, stable=True).astype(jnp.int32)
    offsets = jnp.concatenate([jnp.zeros((N_SRC, N_TGT, 1), jnp.int32), 1 + order[:, :, :BLK_DEV - 1]], axis=-1)
    places = (first[:, :, None] + offsets) % spots
    rows = src_ids[:, :, None] * RB + places // CB
    cols = tgt_ids[:, :, None] * CB + places % CB
    counts = jax.random.randint(key_count, (N_SRC, N_TGT), 1, BLK_DEV + 1)
    chosen = jax.random.randint(key_pick, (), 0, N_SRC * N_TGT)
    flat_ids = jnp.arange(N_SRC * N_TGT, dtype=jnp.int32).reshape(N_SRC, N_TGT)
    counts = jnp.where(flat_ids == chosen, BLK_DEV, counts)
    return (rows.reshape(N_SRC, N_TGT * BLK_DEV), cols.reshape(N_SRC, N_TGT * BLK_DEV), counts.astype(jnp.int32))


def draw_slot_block_row(key, part):
    return pattern(key)[0]


def draw_slot_block_column(key, part):
    return pattern(key)[1]


def draw_device_block_count(key, part):
    return pattern(key)[2]


def draw_cost(key, part):
    key = jax.random.fold_in(key, 11)
    key_base = jax.random.fold_in(key, 0)
    array_dimensions = (N_SRC, N_TGT * BLK_DEV, BLOCK, BLOCK)
    base = jax.random.uniform(key_base, array_dimensions, jnp.float32, 0.0, 4.0)
    return base.astype(jnp.bfloat16)


def draw_log_b(key, part):
    key = jax.random.fold_in(key, 23)
    target = jnp.arange(TARGETS, dtype=jnp.int32)
    sign = jnp.where(target // BLOCK % 2 == 0, 1.0, -1.0).astype(jnp.float32)
    spread = jax.random.uniform(key, (TARGETS,), jnp.float32, 0.0, 1.0)
    level = 0.5 + 0.5 * spread
    return (sign * level).astype(jnp.float32)


def steps_of(own_key, dims, pieces, low, top_value):
    gain, own = 1.0, jax.random.fold_in(own_key, 6)
    for position, shards_of in pieces:
        heights = jnp.exp(jax.random.uniform(jax.random.fold_in(own, position), (shards_of,), jnp.float32, low / len(pieces), top_value / len(pieces)))
        gain = gain * jnp.repeat(heights, dims[position] // shards_of).reshape([-1 if axis == position else 1 for axis in range(len(dims))])
    return gain


def setup_inputs(seed: int = 0) -> dict:
    arg_keys = jax.random.split(jax.random.key(seed), 9)
    return {
        "cost": draw_cost(jax.random.fold_in(arg_keys[8], 71), 0),
        "cost_scale": jnp.clip(jnp.exp(math.log(2.0) - 1.3862944 * jax.random.uniform(arg_keys[1], (N_SRC, N_TGT * BLK_DEV), jnp.float32) ** steps_of(arg_keys[1], (N_SRC, N_TGT * BLK_DEV), ((0, 8), (1, 32)), -0.2, 0.2)), 0.5, 2.0),
        "slot_block_row": draw_slot_block_row(jax.random.fold_in(arg_keys[8], 71), 0),
        "slot_block_column": draw_slot_block_column(jax.random.fold_in(arg_keys[8], 71), 0),
        "device_block_count": draw_device_block_count(jax.random.fold_in(arg_keys[8], 71), 0),
        "log_a": jnp.clip(jax.random.uniform(arg_keys[5], (SOURCES,), jnp.float32, -1.0, 1.0) * steps_of(arg_keys[5], (SOURCES,), ((0, 8),), -0.4, 0.0), -1.0, 1.0),
        "log_b": draw_log_b(jax.random.fold_in(arg_keys[8], 71), 0),
        "labels": jnp.clip(1.0 * jax.random.uniform(arg_keys[7], (SOURCES, CLASSES), jnp.float32) ** steps_of(arg_keys[7], (SOURCES, CLASSES), ((0, 256),), -0.2, 0.2), 0.0, 1.0).astype(jnp.bfloat16),
    }


EPS = 0.5
NEG = -1.0e30


def flat_blocks(cost, cost_scale, slot_block_row, slot_block_column, device_block_count):
    nblk = N_SRC * N_TGT * BLK_DEV
    slot_ids = jnp.arange(N_TGT * BLK_DEV, dtype=jnp.int32) % BLK_DEV
    counts = jnp.repeat(device_block_count, BLK_DEV, axis=1)
    live = (slot_ids[None, :] < counts).reshape(nblk)
    return (cost.reshape(nblk, BLOCK, BLOCK), cost_scale.reshape(nblk),
            slot_block_row.reshape(nblk).astype(jnp.int32), slot_block_column.reshape(nblk).astype(jnp.int32), live)


def merge_into(m_all, s_all, start, block_max, block_sum, live):
    old_m = lax.dynamic_slice(m_all, (start,), (BLOCK,))
    old_s = lax.dynamic_slice(s_all, (start,), (BLOCK,))
    new_m = jnp.maximum(old_m, block_max)
    new_s = old_s * jnp.exp(old_m - new_m) + block_sum * jnp.exp(block_max - new_m)
    new_m = jnp.where(live, new_m, old_m)
    new_s = jnp.where(live, new_s, old_s)
    return lax.dynamic_update_slice(m_all, new_m, (start,)), lax.dynamic_update_slice(s_all, new_s, (start,))


def reduce_lse(blocks, other, count, along_rows):
    def step(carry, item):
        m_all, s_all = carry
        block_tile, scale, row, col, live = item
        dense = scale * block_tile.astype(jnp.float32)
        if along_rows:
            part = lax.dynamic_slice(other, (col * BLOCK,), (BLOCK,))
            z = (part[None, :] - dense) / EPS
            axis_id = 1
            start = row * BLOCK
        else:
            part = lax.dynamic_slice(other, (row * BLOCK,), (BLOCK,))
            z = (part[:, None] - dense) / EPS
            axis_id = 0
            start = col * BLOCK
        block_max = jnp.max(z, axis=axis_id)
        expand = jnp.expand_dims(block_max, axis_id)
        block_sum = jnp.sum(jnp.exp(z - expand), axis=axis_id)
        return merge_into(m_all, s_all, start, block_max, block_sum, live), None

    init = (jnp.full((count,), NEG, jnp.float32), jnp.zeros((count,), jnp.float32))
    (m_all, s_all), _ = lax.scan(step, init, blocks)
    return m_all + jnp.log(s_all)


def reference(cost, cost_scale, slot_block_row, slot_block_column, device_block_count, log_a, log_b, labels):
    blocks = flat_blocks(cost, cost_scale, slot_block_row, slot_block_column, device_block_count)
    g_pot = jnp.zeros((TARGETS,), jnp.float32)
    f_pot = jnp.zeros((SOURCES,), jnp.float32)
    for step_id in range(ITERS):
        f_pot = EPS * log_a - EPS * reduce_lse(blocks, g_pot, SOURCES, True)
        g_pot = EPS * log_b - EPS * reduce_lse(blocks, f_pot, TARGETS, False)

    def carry_labels(acc, item):
        block_tile, scale, row, col, live = item
        f_part = lax.dynamic_slice(f_pot, (row * BLOCK,), (BLOCK,))
        g_part = lax.dynamic_slice(g_pot, (col * BLOCK,), (BLOCK,))
        plan = jnp.exp((f_part[:, None] + g_part[None, :] - scale * block_tile.astype(jnp.float32)) / EPS).astype(jnp.bfloat16)
        lab = lax.dynamic_slice(labels, (row * BLOCK, jnp.int32(0)), (BLOCK, CLASSES))
        term = jnp.dot(plan.T, lab, preferred_element_type=jnp.float32)
        old = lax.dynamic_slice(acc, (col * BLOCK, jnp.int32(0)), (BLOCK, CLASSES))
        new = old + jnp.where(live, term, jnp.zeros_like(term))
        return lax.dynamic_update_slice(acc, new, (col * BLOCK, jnp.int32(0))), None

    acc, _ = lax.scan(carry_labels, jnp.zeros((TARGETS, CLASSES), jnp.float32), blocks)
    return f_pot, g_pot, acc.astype(jnp.bfloat16)
```

```python
import functools

import jax
import jax.numpy as jnp
from jax import lax
from jax.experimental import pallas as pl
from jax.experimental.pallas import tpu as pltpu
from jax.sharding import PartitionSpec as P

ITERS = 4
EPS = 0.5
NEG = -1e30
LOG2E = 1.4426950408889634
TO2 = LOG2E / EPS
INNER = 8
LIMIT = 40 * 1024 * 1024
F32, BF16 = jnp.float32, jnp.bfloat16


def tree_sum(parts):
    while len(parts) > 1:
        parts = [a + b for a, b in zip(parts[0::2], parts[1::2])]
    return parts[0]


def lse(parts):
    top = functools.reduce(jnp.maximum, parts)
    return top + jnp.log(tree_sum([jnp.exp(p - top) for p in parts]))


def xor_exchange(x, axis, size, steps):
    return [x] + [lax.ppermute(x, axis, [(i, i ^ k) for i in range(size)]) for k in steps]


class Slots:
    def __init__(self, scale, row, col, count, rb, cb, total):
        src, tgt = lax.axis_index("src"), lax.axis_index("tgt")
        self.total = total
        self.scale = [scale[0, s] for s in range(total)]
        self.row = [row[0, s] - src * rb for s in range(total)]
        self.col = [col[0, s] - tgt * cb for s in range(total)]
        self.live = [s < count[0, 0] for s in range(total)]
        self.src, self.tgt = src, tgt


def split_rows(x):
    x = jnp.broadcast_to(x, (16, x.shape[1]))
    hi = x.astype(BF16).astype(F32)
    rest = x - hi
    mid = rest.astype(BF16).astype(F32)
    low = (rest - mid).astype(BF16).astype(F32)
    at = lax.broadcasted_iota(jnp.int32, x.shape, 0)
    zero = jnp.zeros_like(x)
    return jnp.where(at == 0, hi, jnp.where(at == 1, mid, jnp.where(at == 2, low, zero))).astype(BF16)


def k_row(lhs, k_block):
    return lax.dot_general(lhs, k_block, (((1,), (1,)), ((), ())), preferred_element_type=F32)


def k_col(lhs, k_block):
    return lax.dot_general(lhs, k_block, (((1,), (0,)), ((), ())), preferred_element_type=F32)


def chunked(row, out_ref):
    for c in range(out_ref.shape[0]):
        out_ref[c : c + 1, :] = row[:, c * 128 : (c + 1) * 128]


def tile_z(cost_v, scale, other8, out_chunk, red_chunk, rows_mode):
    mine = pl.ds(pl.multiple_of(out_chunk * 128, 128), 128)
    summed = pl.ds(pl.multiple_of(red_chunk * 128, 128), 128)
    other = jnp.broadcast_to(other8[pl.ds(red_chunk, 1), :], (128, 128)).T
    if rows_mode:
        tile = cost_v[mine, summed].astype(F32).T
    else:
        tile = cost_v[summed, mine].astype(F32)
    return (other - scale * tile) / EPS


def slow_lse(slots, cost_hbm, cost_v, sem, other8, out8, other_ref, l_ref, rows_mode):
    l_ref[...] = jnp.full(l_ref.shape, NEG, F32)
    chunks = out8.shape[0]
    for s in range(slots.total):
        out_at, other_at = (slots.row[s], slots.col[s]) if rows_mode else (slots.col[s], slots.row[s])

        @pl.when(slots.live[s])
        def _():
            copy = pltpu.make_async_copy(cost_hbm.at[0, s], cost_v, sem)
            copy.start()
            copy.wait()
            chunked(other_ref[pl.ds(other_at, 1), :], other8)

            @pl.loop(0, chunks)
            def _(i):
                def step(j, carry):
                    m, total = carry
                    z = tile_z(cost_v, slots.scale[s], other8, i, j, rows_mode)
                    top = jnp.maximum(m, jnp.max(z, axis=0, keepdims=True))
                    total = total * jnp.exp(m - top) + jnp.sum(jnp.exp(z - top), axis=0, keepdims=True)
                    return top, total

                first = (jnp.full((1, 128), NEG, F32), jnp.zeros((1, 128), F32))
                m, total = lax.fori_loop(0, chunks, step, first)
                out8[pl.ds(i, 1), :] = m + jnp.log(total)

            new = jnp.concatenate([out8[c : c + 1, :] for c in range(chunks)], axis=1)
            old = l_ref[pl.ds(out_at, 1), :]
            top = jnp.maximum(old, new)
            l_ref[pl.ds(out_at, 1), :] = top + jnp.log(jnp.exp(old - top) + jnp.exp(new - top))


def piece_of(ref, piece, width):
    per = ref.shape[1] // width
    row = ref[pl.ds(piece // per, 1), :]
    out = row[:, :width]
    for c in range(1, per):
        out = jnp.where(piece % per == c, row[:, c * width : (c + 1) * width], out)
    return out


def to_log(total, shift):
    return jnp.where(total > 0, jnp.log(jnp.maximum(total, 1e-38)) - shift / EPS, NEG)


def sums_fine(low, high, others):
    return (low >= 2.0**-80 * jnp.maximum(others, 1.0)) & (high <= 2.0**100)


def build_kernel(dims, scale, row, col, count, cost_hbm, k_ref, l_ref, ref_ref, cost_v, sums, zero, other8, out8, sems):
    slots = Slots(scale, row, col, count, *dims)
    total = slots.total
    half = cost_v.shape[1] // 2
    copies = [
        [
            pltpu.make_async_copy(
                cost_hbm.at[0, s, pl.ds(h * half, half)], cost_v.at[s, pl.ds(h * half, half)], sems.at[s, h]
            )
            for h in range(2)
        ]
        for s in range(total)
    ]
    for s in range(total):

        @pl.when(slots.live[s])
        def _():
            for h in range(2):
                copies[s][h].start()

    chunk = 32
    ones = jnp.ones((16, cost_v.shape[2]), BF16)

    def build(shift, wait):
        sums[...] = jnp.zeros(sums.shape, F32)
        ref_ref[0, 0] = shift
        ref_ref[0, 1] = 0.0
        ref_ref[0, 2] = jnp.float32(jnp.inf)
        for s in range(total):

            @pl.when(slots.live[s])
            def _():
                for h in range(2):
                    if wait:
                        copies[s][h].wait()

                    @pl.loop(0, half // chunk, unroll=2)
                    def _(i):
                        here = pl.ds(pl.multiple_of(h * half + i * chunk, chunk), chunk)
                        x = cost_v[s, here, :].astype(F32)
                        x = x * (-TO2 * slots.scale[s]) + shift * TO2
                        k_ref[s, here, :] = jnp.exp2(x).astype(BF16)

                part = k_row(ones, k_ref[s])[0:1]
                at = pl.ds(slots.row[s], 1)
                sums[at, :] = sums[at, :] + part
                ref_ref[0, 1] = jnp.maximum(ref_ref[0, 1], jnp.max(part))
                ref_ref[0, 2] = jnp.minimum(ref_ref[0, 2], jnp.min(part))

        l_ref[...] = to_log(sums[...], shift)
        return sums_fine(ref_ref[0, 2], ref_ref[0, 1], ref_ref[0, 1])

    fine = build(jnp.float32(0.0), True)

    @pl.when(jnp.logical_not(fine))
    def _():
        ref_ref[0, 3] = jnp.float32(jnp.inf)
        for s in range(total):

            @pl.when(slots.live[s])
            def _():
                def lowest(i, low):
                    here = pl.ds(pl.multiple_of(i * chunk, chunk), chunk)
                    return jnp.minimum(low, jnp.min(cost_v[s, here, :].astype(F32)))

                low = lax.fori_loop(0, 2 * half // chunk, lowest, jnp.float32(jnp.inf))
                ref_ref[0, 3] = jnp.minimum(ref_ref[0, 3], low * slots.scale[s])

        shifted = build(ref_ref[0, 3], False)

        @pl.when(jnp.logical_not(shifted))
        def _():
            zero[...] = jnp.zeros(zero.shape, F32)
            slow_lse(slots, cost_hbm, cost_v.at[0], sems.at[0, 0], other8, out8, zero, l_ref, True)


def row_kernel(dims, n_parts, scale, row, col, count, ref, log_b, cost_hbm, k_ref, *rest):
    parts, (l_ref, g, sums, stat, cost_v, other8, out8, sem) = rest[:n_parts], rest[n_parts:]
    slots = Slots(scale, row, col, count, *dims)
    g[...] = EPS * log_b[...] - EPS * lse([p[...] for p in parts])
    sums[...] = jnp.zeros(sums.shape, F32)
    stat[0] = jnp.float32(0.0)
    stat[1] = jnp.float32(jnp.inf)
    stat[2] = ref[0, 1]
    for s in range(slots.total):

        @pl.when(slots.live[s])
        def _():
            v = jnp.exp2(g[pl.ds(slots.col[s], 1), :] * TO2)
            part = jnp.sum(k_row(split_rows(v), k_ref[s]), axis=0, keepdims=True)
            at = pl.ds(slots.row[s], 1)
            sums[at, :] = sums[at, :] + part
            stat[0] = jnp.maximum(stat[0], jnp.max(part))
            stat[1] = jnp.minimum(stat[1], jnp.min(part))
            stat[2] = jnp.maximum(stat[2], jnp.max(v))

    l_ref[...] = to_log(sums[...], ref[0, 0])

    @pl.when(jnp.logical_not(sums_fine(stat[1], stat[0], stat[2])))
    def _():
        slow_lse(slots, cost_hbm, cost_v, sem, other8, out8, g, l_ref, True)


def col_kernel(dims, n_parts, scale, row, col, count, ref, log_a, cost_hbm, k_ref, *rest):
    parts, (l_ref, f, sums, stat, cost_v, other8, out8, sem) = rest[:n_parts], rest[n_parts:]
    slots = Slots(scale, row, col, count, *dims)
    f[...] = EPS * log_a[...] - EPS * lse([p[...] for p in parts])
    sums[...] = jnp.zeros(sums.shape, F32)
    stat[0] = jnp.float32(0.0)
    stat[1] = jnp.float32(jnp.inf)
    stat[2] = ref[0, 1]
    for s in range(slots.total):

        @pl.when(slots.live[s])
        def _():
            u = jnp.exp2(f[pl.ds(slots.row[s], 1), :] * TO2)
            part = jnp.sum(k_col(split_rows(u), k_ref[s]), axis=0, keepdims=True)
            at = pl.ds(slots.col[s], 1)
            sums[at, :] = sums[at, :] + part
            stat[0] = jnp.maximum(stat[0], jnp.max(part))
            stat[1] = jnp.minimum(stat[1], jnp.min(part))
            stat[2] = jnp.maximum(stat[2], jnp.max(u))

    l_ref[...] = to_log(sums[...], ref[0, 0])

    @pl.when(jnp.logical_not(sums_fine(stat[1], stat[0], stat[2])))
    def _():
        slow_lse(slots, cost_hbm, cost_v, sem, other8, out8, f, l_ref, False)


def label_kernel(dims, n_parts, n_out, scale, row, col, count, ref, log_a, cost_hbm, k_ref, labels, *rest):
    parts, rest = rest[:n_parts], rest[n_parts:]
    l_ref, f_out, outs, rest = rest[0], rest[1], rest[2 : 2 + n_out], rest[2 + n_out :]
    acc, sums, stat, cost_v, other8, out8, sem = rest
    slots = Slots(scale, row, col, count, *dims)
    classes = acc.shape[1]
    f_out[...] = EPS * log_a[...] - EPS * lse([p[...] for p in parts])
    sums[...] = jnp.zeros(sums.shape, F32)
    acc[...] = jnp.zeros(acc.shape, F32)
    stat[0] = jnp.float32(0.0)
    stat[1] = jnp.float32(jnp.inf)
    stat[2] = ref[0, 1]
    my_outer, my_inner = slots.tgt // INNER, slots.tgt % INNER
    for s in range(slots.total):

        @pl.when(slots.live[s])
        def _():
            u = jnp.exp2(f_out[pl.ds(slots.row[s], 1), :] * TO2)
            outer = slots.row[s] ^ my_outer
            lab = jnp.concatenate([labels[outer, z ^ my_inner] for z in range(INNER)], axis=1)
            weighted = lab.astype(F32) * u
            hi = weighted.astype(BF16)
            low = (weighted - hi.astype(F32)).astype(BF16)
            res = k_col(jnp.concatenate([hi, low, split_rows(u)], axis=0), k_ref[s])
            part = jnp.sum(res[2 * classes :], axis=0, keepdims=True)
            at = pl.ds(slots.col[s], 1)
            sums[at, :] = sums[at, :] + part
            acc[slots.col[s]] = acc[slots.col[s]] + (res[:classes] + res[classes : 2 * classes])
            stat[0] = jnp.maximum(stat[0], jnp.max(part))
            stat[1] = jnp.minimum(stat[1], jnp.min(part))
            stat[2] = jnp.maximum(stat[2], jnp.max(u))

    l_ref[...] = to_log(sums[...], ref[0, 0])

    @pl.when(jnp.logical_not(sums_fine(stat[1], stat[0], stat[2])))
    def _():
        slow_lse(slots, cost_hbm, cost_v, sem, other8, out8, f_out, l_ref, False)
        acc[...] = jnp.zeros(acc.shape, F32)
        sums[...] = jnp.ones(sums.shape, F32)
        chunks = cost_v.shape[0] // 128
        for s in range(slots.total):

            @pl.when(slots.live[s])
            def _():
                copy = pltpu.make_async_copy(cost_hbm.at[0, s], cost_v, sem)
                copy.start()
                copy.wait()
                chunked(f_out[pl.ds(slots.row[s], 1), :], other8)
                chunked(l_ref[pl.ds(slots.col[s], 1), :], out8)

                @pl.loop(0, chunks * chunks)
                def _(ij):
                    i, j = ij // chunks, ij % chunks
                    here = pl.ds(pl.multiple_of(i * 128, 128), 128)
                    z = tile_z(cost_v, slots.scale[s], other8, i, j, False)
                    p = jnp.exp(z - out8[pl.ds(i, 1), :]).astype(BF16)
                    lab = labels[slots.row[s] ^ my_outer, j ^ my_inner]
                    term = jnp.dot(lab, p, preferred_element_type=F32)
                    acc[slots.col[s], :, here] = acc[slots.col[s], :, here] + term

    width = outs[0].shape[1]
    per = acc.shape[2] // width
    for k in range(n_out):
        piece = slots.src ^ k
        here = pl.ds(pl.multiple_of((piece % per) * width, width), width)
        total = piece_of(sums, piece, width)
        inv = jnp.where(total > 0, 1.0 / jnp.maximum(total, 1e-38), 0.0)
        outs[k][...] = (acc[piece // per, :, here] * inv).astype(BF16)


def combine_kernel(n_src, log_b, *rest):
    means, parts, (g_out, out) = rest[:n_src], rest[n_src : 2 * n_src], rest[2 * n_src :]
    src = lax.axis_index("src")
    total = lse([p[...] for p in parts])
    g_out[...] = EPS * log_b[...] - EPS * total
    width = out.shape[1]
    ls = [piece_of(p, src, width) for p in parts]
    top = lse(ls) - piece_of(log_b, src, width)
    out[...] = tree_sum([means[k][...].astype(F32) * jnp.exp(ls[k] - top) for k in range(n_src)]).astype(BF16)


def assemble_kernel(n_src, *refs):
    pieces, out = refs[:n_src], refs[n_src]
    src = lax.axis_index("src")
    width = pieces[0].shape[1]
    for k in range(n_src):
        out[:, pl.ds(pl.multiple_of((src ^ k) * width, width), width)] = pieces[k][...]


VM = pl.BlockSpec(memory_space=pltpu.VMEM)
SM = pl.BlockSpec(memory_space=pltpu.SMEM)
HB = pl.BlockSpec(memory_space=pltpu.HBM)
PARAMS = pltpu.CompilerParams(vmem_limit_bytes=LIMIT)


def local(cost, cost_scale, slot_block_row, slot_block_column, device_block_count, log_a, log_b, labels):
    n_src, n_tgt = lax.axis_size("src"), lax.axis_size("tgt")
    slots, tile = cost.shape[1], cost.shape[2]
    rb, cb = log_a.shape[0] // tile, log_b.shape[0] // tile
    classes = labels.shape[1]
    dims = (rb, cb, slots)
    scalars = (cost_scale, slot_block_row, slot_block_column, device_block_count)
    log_a = log_a.reshape(rb, tile)
    log_b = log_b.reshape(cb, tile)
    outer = n_tgt // INNER

    lab = jnp.stack(xor_exchange(labels.T, "tgt", n_tgt, range(1, INNER)))
    lab = jnp.stack(xor_exchange(lab, "tgt", n_tgt, [k * INNER for k in range(1, outer)]))

    k_type = pltpu.VMEM((slots, tile, tile), BF16)
    vec = functools.partial(jax.ShapeDtypeStruct, dtype=F32)
    chunks = pltpu.VMEM((tile // 128, 128), F32)
    slow = [pltpu.VMEM((tile, tile), BF16), chunks, chunks, pltpu.SemaphoreType.DMA]
    work = [pltpu.SMEM((3,), F32)] + slow

    k_all, row_l, ref = pl.pallas_call(
        functools.partial(build_kernel, dims),
        out_shape=(k_type, vec((rb, tile)), vec((1, 4))),
        in_specs=[SM] * 4 + [HB],
        out_specs=(VM, VM, SM),
        scratch_shapes=[
            pltpu.VMEM((slots, tile, tile), BF16),
            pltpu.VMEM((rb, tile), F32),
            pltpu.VMEM((cb, tile), F32),
            chunks,
            chunks,
            pltpu.SemaphoreType.DMA((slots, 2)),
        ],
        compiler_params=PARAMS,
    )(*scalars, cost)
    k_all = pltpu.with_memory_space_constraint(k_all, pltpu.VMEM)
    common = [SM] * 5 + [VM, HB, VM]

    def row_exchange(part):
        part = lse(xor_exchange(part, "tgt", n_tgt, range(1, INNER)))
        return xor_exchange(part, "tgt", n_tgt, [k * INNER for k in range(1, outer)])

    for step in range(ITERS):
        row_parts = row_exchange(row_l)
        if step == ITERS - 1:
            break
        col_l = pl.pallas_call(
            functools.partial(col_kernel, dims, outer),
            out_shape=vec((cb, tile)),
            in_specs=common + [VM] * outer,
            out_specs=VM,
            scratch_shapes=[pltpu.VMEM((rb, tile), F32), pltpu.VMEM((cb, tile), F32)] + work,
            compiler_params=PARAMS,
        )(*scalars, ref, log_a, cost, k_all, *row_parts)
        col_parts = xor_exchange(col_l, "src", n_src, range(1, n_src))
        row_l = pl.pallas_call(
            functools.partial(row_kernel, dims, n_src),
            out_shape=vec((rb, tile)),
            in_specs=common + [VM] * n_src,
            out_specs=VM,
            scratch_shapes=[pltpu.VMEM((cb, tile), F32), pltpu.VMEM((rb, tile), F32)] + work,
            compiler_params=PARAMS,
        )(*scalars, ref, log_b, cost, k_all, *col_parts)

    width = cb * tile // n_src
    piece = jax.ShapeDtypeStruct((classes, width), BF16)
    col_l, f_pot, *means = pl.pallas_call(
        functools.partial(label_kernel, dims, outer, n_src),
        out_shape=(vec((cb, tile)), vec((rb, tile))) + (piece,) * n_src,
        in_specs=common + [VM] + [VM] * outer,
        out_specs=(VM,) * (2 + n_src),
        scratch_shapes=[pltpu.VMEM((cb, classes, tile), F32), pltpu.VMEM((cb, tile), F32)] + work,
        compiler_params=PARAMS,
    )(*scalars, ref, log_a, cost, k_all, lab, *row_parts)
    col_parts = xor_exchange(col_l, "src", n_src, range(1, n_src))
    means = [means[0]] + [
        lax.ppermute(means[k], "src", [(i, i ^ k) for i in range(n_src)]) for k in range(1, n_src)
    ]
    g_pot, out = pl.pallas_call(
        functools.partial(combine_kernel, n_src),
        out_shape=(vec((cb, tile)), piece),
        in_specs=[VM] * (1 + 2 * n_src),
        out_specs=(VM, VM),
        compiler_params=PARAMS,
    )(log_b, *means, *col_parts)
    out = pl.pallas_call(
        functools.partial(assemble_kernel, n_src),
        out_shape=jax.ShapeDtypeStruct((classes, cb * tile), BF16),
        in_specs=[VM] * n_src,
        out_specs=VM,
        compiler_params=PARAMS,
    )(*xor_exchange(out, "src", n_src, range(1, n_src)))
    return f_pot.reshape(-1), g_pot.reshape(-1), out.T


def solution(mesh):
    in_specs = (
        P("src", "tgt", None, None),
        P("src", "tgt"),
        P("src", "tgt"),
        P("src", "tgt"),
        P("src", "tgt"),
        P("src"),
        P("tgt"),
        P(("src", "tgt"), None),
    )
    out_specs = (P("src"), P("tgt"), P("tgt", None))
    return jax.shard_map(local, mesh=mesh, in_specs=in_specs, out_specs=out_specs, check_vma=False)
```

```python
import functools

import jax
import jax.numpy as jnp
from jax import lax
from jax.experimental import pallas as pl
from jax.experimental.pallas import tpu as pltpu
from jax.sharding import PartitionSpec as P

ITERS = 4
EPS = 0.5
NEG = -1e30
LOG2E = 1.4426950408889634
TO2 = LOG2E / EPS
INNER = 8
LIMIT = 40 * 1024 * 1024
F32, BF16 = jnp.float32, jnp.bfloat16


def tree_sum(parts):
    while len(parts) > 1:
        parts = [a + b for a, b in zip(parts[0::2], parts[1::2])]
    return parts[0]


def lse(parts):
    top = functools.reduce(jnp.maximum, parts)
    return top + jnp.log(tree_sum([jnp.exp(p - top) for p in parts]))


class Slots:
    def __init__(self, ints, floats, total):
        self.total = total
        self.row = [ints[0, s] for s in range(total)]
        self.col = [ints[0, total + s] for s in range(total)]
        self.count = ints[0, 2 * total]
        self.live = [s < self.count for s in range(total)]
        self.scale = [floats[0, s] for s in range(total)]
        self.shift, self.high = floats[0, total], floats[0, total + 1]
        self.src, self.tgt = lax.axis_index("src"), lax.axis_index("tgt")


def split_rows(x):
    x = jnp.broadcast_to(x, (16, x.shape[1]))
    hi = x.astype(BF16).astype(F32)
    rest = x - hi
    mid = rest.astype(BF16).astype(F32)
    low = (rest - mid).astype(BF16).astype(F32)
    at = lax.broadcasted_iota(jnp.int32, x.shape, 0)
    zero = jnp.zeros_like(x)
    return jnp.where(at == 0, hi, jnp.where(at == 1, mid, jnp.where(at == 2, low, zero))).astype(BF16)


def k_row(lhs, k_block):
    return lax.dot_general(lhs, k_block, (((1,), (1,)), ((), ())), preferred_element_type=F32)


def k_col(lhs, k_block):
    return lax.dot_general(lhs, k_block, (((1,), (0,)), ((), ())), preferred_element_type=F32)


def chunked(row, out_ref):
    for c in range(out_ref.shape[0]):
        out_ref[c : c + 1, :] = row[:, c * 128 : (c + 1) * 128]


def tile_z(cost_v, scale, other8, out_chunk, red_chunk, rows_mode):
    mine = pl.ds(pl.multiple_of(out_chunk * 128, 128), 128)
    summed = pl.ds(pl.multiple_of(red_chunk * 128, 128), 128)
    other = jnp.broadcast_to(other8[pl.ds(red_chunk, 1), :], (128, 128)).T
    if rows_mode:
        tile = cost_v[mine, summed].astype(F32).T
    else:
        tile = cost_v[summed, mine].astype(F32)
    return (other - scale * tile) / EPS


def slow_lse(slots, cost_hbm, cost_v, sem, other8, out8, other_ref, l_ref, rows_mode):
    l_ref[...] = jnp.full(l_ref.shape, NEG, F32)
    chunks = out8.shape[0]
    for s in range(slots.total):
        out_at, other_at = (slots.row[s], slots.col[s]) if rows_mode else (slots.col[s], slots.row[s])

        @pl.when(slots.live[s])
        def _():
            copy = pltpu.make_async_copy(cost_hbm.at[0, s], cost_v, sem)
            copy.start()
            copy.wait()
            chunked(other_ref[pl.ds(other_at, 1), :], other8)

            @pl.loop(0, chunks)
            def _(i):
                def step(j, carry):
                    m, total = carry
                    z = tile_z(cost_v, slots.scale[s], other8, i, j, rows_mode)
                    top = jnp.maximum(m, jnp.max(z, axis=0, keepdims=True))
                    total = total * jnp.exp(m - top) + jnp.sum(jnp.exp(z - top), axis=0, keepdims=True)
                    return top, total

                first = (jnp.full((1, 128), NEG, F32), jnp.zeros((1, 128), F32))
                m, total = lax.fori_loop(0, chunks, step, first)
                out8[pl.ds(i, 1), :] = m + jnp.log(total)

            new = jnp.concatenate([out8[c : c + 1, :] for c in range(chunks)], axis=1)
            old = l_ref[pl.ds(out_at, 1), :]
            top = jnp.maximum(old, new)
            l_ref[pl.ds(out_at, 1), :] = top + jnp.log(jnp.exp(old - top) + jnp.exp(new - top))


def piece_of(ref, piece, width):
    per = ref.shape[1] // width
    row = ref[pl.ds(piece // per, 1), :]
    out = row[:, :width]
    for c in range(1, per):
        out = jnp.where(piece % per == c, row[:, c * width : (c + 1) * width], out)
    return out


def to_log(total, shift):
    return jnp.where(total > 0, jnp.log(jnp.maximum(total, 1e-38)) - shift / EPS, NEG)


def send_copies(l_ref, copies_ref):
    for k in range(copies_ref.shape[0]):
        copies_ref[k] = l_ref[...]


def sums_fine(low, high, others):
    return (low >= 2.0**-80 * jnp.maximum(others, 1.0)) & (high <= 2.0**100)


def build_kernel(
    dims, scale, row, col, count, log_a, log_b, cost_hbm,
    k_ref, copies_ref, ints, floats, a_ref, b_ref,
    l_ref, cost_v, sums, zero, other8, out8, stat, sems,
):
    rb, cb, total = dims
    src, tgt = lax.axis_index("src"), lax.axis_index("tgt")
    for s in range(total):
        ints[0, s] = row[0, s] - src * rb
        ints[0, total + s] = col[0, s] - tgt * cb
        floats[0, s] = scale[0, s]
    ints[0, 2 * total] = count[0, 0]
    slots = Slots(ints, floats, total)
    half = cost_v.shape[1] // 2
    copies = [
        [
            pltpu.make_async_copy(
                cost_hbm.at[0, s, pl.ds(h * half, half)], cost_v.at[s, pl.ds(h * half, half)], sems.at[s, h]
            )
            for h in range(2)
        ]
        for s in range(total)
    ]
    for s in range(total):

        @pl.when(slots.live[s])
        def _():
            for h in range(2):
                copies[s][h].start()

    tile = cost_v.shape[2]
    for r in range(rb):
        a_ref[r : r + 1, :] = log_a[r * tile : (r + 1) * tile].reshape(1, tile)
    for c in range(cb):
        b_ref[c : c + 1, :] = log_b[c * tile : (c + 1) * tile].reshape(1, tile)
    chunk = 32
    ones = jnp.ones((16, cost_v.shape[2]), BF16)

    def build(shift, wait):
        sums[...] = jnp.zeros(sums.shape, F32)
        floats[0, total] = shift
        stat[1] = jnp.float32(0.0)
        stat[2] = jnp.float32(jnp.inf)
        for s in range(total):

            @pl.when(slots.live[s])
            def _():
                for h in range(2):
                    if wait:
                        copies[s][h].wait()

                    @pl.loop(0, half // chunk, unroll=2)
                    def _(i):
                        here = pl.ds(pl.multiple_of(h * half + i * chunk, chunk), chunk)
                        x = cost_v[s, here, :].astype(F32)
                        x = x * (-TO2 * slots.scale[s]) + shift * TO2
                        k_ref[s, here, :] = jnp.exp2(x).astype(BF16)

                part = k_row(ones, k_ref[s])[0:1]
                at = pl.ds(slots.row[s], 1)
                sums[at, :] = sums[at, :] + part
                stat[1] = jnp.maximum(stat[1], jnp.max(part))
                stat[2] = jnp.minimum(stat[2], jnp.min(part))

        l_ref[...] = to_log(sums[...], shift)
        floats[0, total + 1] = stat[1]
        return sums_fine(stat[2], stat[1], stat[1])

    fine = build(jnp.float32(0.0), True)

    @pl.when(jnp.logical_not(fine))
    def _():
        stat[0] = jnp.float32(jnp.inf)
        for s in range(total):

            @pl.when(slots.live[s])
            def _():
                def lowest(i, low):
                    here = pl.ds(pl.multiple_of(i * chunk, chunk), chunk)
                    return jnp.minimum(low, jnp.min(cost_v[s, here, :].astype(F32)))

                low = lax.fori_loop(0, 2 * half // chunk, lowest, jnp.float32(jnp.inf))
                stat[0] = jnp.minimum(stat[0], low * slots.scale[s])

        shifted = build(stat[0], False)

        @pl.when(jnp.logical_not(shifted))
        def _():
            zero[...] = jnp.zeros(zero.shape, F32)
            slow_lse(slots, cost_hbm, cost_v.at[0], sems.at[0, 0], other8, out8, zero, l_ref, True)

    send_copies(l_ref, copies_ref)


def row_kernel(total, n_parts, ints, floats, log_b, cost_hbm, k_ref, _, *rest):
    parts, (copies_ref, _, l_ref, g, sums, stat, cost_v, other8, out8, sem) = rest[:n_parts], rest[n_parts:]
    slots = Slots(ints, floats, total)
    g[...] = EPS * log_b[...] - EPS * lse([p[...] for p in parts])
    sums[...] = jnp.zeros(sums.shape, F32)
    stat[0] = jnp.float32(0.0)
    stat[1] = jnp.float32(jnp.inf)
    stat[2] = slots.high
    for s in range(slots.total):

        @pl.when(slots.live[s])
        def _():
            v = jnp.exp2(g[pl.ds(slots.col[s], 1), :] * TO2)
            part = jnp.sum(k_row(split_rows(v), k_ref[s]), axis=0, keepdims=True)
            at = pl.ds(slots.row[s], 1)
            sums[at, :] = sums[at, :] + part
            stat[0] = jnp.maximum(stat[0], jnp.max(part))
            stat[1] = jnp.minimum(stat[1], jnp.min(part))
            stat[2] = jnp.maximum(stat[2], jnp.max(v))

    l_ref[...] = to_log(sums[...], slots.shift)

    @pl.when(jnp.logical_not(sums_fine(stat[1], stat[0], stat[2])))
    def _():
        slow_lse(slots, cost_hbm, cost_v, sem, other8, out8, g, l_ref, True)

    send_copies(l_ref, copies_ref)


def col_kernel(total, ints, floats, log_a, cost_hbm, k_ref, _, parts, *rest):
    l_ref, _, f, sums, stat, cost_v, other8, out8, sem = rest
    slots = Slots(ints, floats, total)
    f[...] = EPS * log_a[...] - EPS * lse([parts[k] for k in range(parts.shape[0])])
    sums[...] = jnp.zeros(sums.shape, F32)
    stat[0] = jnp.float32(0.0)
    stat[1] = jnp.float32(jnp.inf)
    stat[2] = slots.high
    for s in range(slots.total):

        @pl.when(slots.live[s])
        def _():
            u = jnp.exp2(f[pl.ds(slots.row[s], 1), :] * TO2)
            part = jnp.sum(k_col(split_rows(u), k_ref[s]), axis=0, keepdims=True)
            at = pl.ds(slots.col[s], 1)
            sums[at, :] = sums[at, :] + part
            stat[0] = jnp.maximum(stat[0], jnp.max(part))
            stat[1] = jnp.minimum(stat[1], jnp.min(part))
            stat[2] = jnp.maximum(stat[2], jnp.max(u))

    l_ref[...] = to_log(sums[...], slots.shift)

    @pl.when(jnp.logical_not(sums_fine(stat[1], stat[0], stat[2])))
    def _():
        slow_lse(slots, cost_hbm, cost_v, sem, other8, out8, f, l_ref, False)


def label_kernel(total, ints, floats, log_a, cost_hbm, k_ref, labels, parts, *rest):
    f_out, keep, send, acc, l_ref, sums, stat, cost_v, other8, out8, sem = rest
    slots = Slots(ints, floats, total)
    classes = acc.shape[1]
    f_out[...] = EPS * log_a[...] - EPS * lse([parts[k] for k in range(parts.shape[0])])
    sums[...] = jnp.zeros(sums.shape, F32)
    acc[...] = jnp.zeros(acc.shape, F32)
    stat[0] = jnp.float32(0.0)
    stat[1] = jnp.float32(jnp.inf)
    stat[2] = slots.high
    my_outer, my_inner = slots.tgt // INNER, slots.tgt % INNER
    for s in range(slots.total):

        @pl.when(slots.live[s])
        def _():
            u = jnp.exp2(f_out[pl.ds(slots.row[s], 1), :] * TO2)
            outer = slots.row[s] ^ my_outer
            lab = jnp.concatenate([labels[outer, z ^ my_inner] for z in range(INNER)], axis=1)
            weighted = lab.astype(F32) * u
            hi = weighted.astype(BF16)
            low = (weighted - hi.astype(F32)).astype(BF16)
            res = k_col(jnp.concatenate([hi, low, split_rows(u)], axis=0), k_ref[s])
            part = jnp.sum(res[2 * classes :], axis=0, keepdims=True)
            at = pl.ds(slots.col[s], 1)
            sums[at, :] = sums[at, :] + part
            acc[slots.col[s]] = acc[slots.col[s]] + (res[:classes] + res[classes : 2 * classes])
            stat[0] = jnp.maximum(stat[0], jnp.max(part))
            stat[1] = jnp.minimum(stat[1], jnp.min(part))
            stat[2] = jnp.maximum(stat[2], jnp.max(u))

    l_ref[...] = to_log(sums[...], slots.shift)

    @pl.when(jnp.logical_not(sums_fine(stat[1], stat[0], stat[2])))
    def _():
        slow_lse(slots, cost_hbm, cost_v, sem, other8, out8, f_out, l_ref, False)
        acc[...] = jnp.zeros(acc.shape, F32)
        sums[...] = jnp.ones(sums.shape, F32)
        chunks = cost_v.shape[0] // 128
        for s in range(slots.total):

            @pl.when(slots.live[s])
            def _():
                copy = pltpu.make_async_copy(cost_hbm.at[0, s], cost_v, sem)
                copy.start()
                copy.wait()
                chunked(f_out[pl.ds(slots.row[s], 1), :], other8)
                chunked(l_ref[pl.ds(slots.col[s], 1), :], out8)

                @pl.loop(0, chunks * chunks)
                def _(ij):
                    i, j = ij // chunks, ij % chunks
                    here = pl.ds(pl.multiple_of(i * 128, 128), 128)
                    z = tile_z(cost_v, slots.scale[s], other8, i, j, False)
                    p = jnp.exp(z - out8[pl.ds(i, 1), :]).astype(BF16)
                    lab = labels[slots.row[s] ^ my_outer, j ^ my_inner]
                    term = jnp.dot(lab, p, preferred_element_type=F32)
                    acc[slots.col[s], :, here] = acc[slots.col[s], :, here] + term

    core = slots.src % 2
    width = keep.shape[2]
    for c in range(acc.shape[0]):
        total = sums[c : c + 1, :]
        inv = jnp.where(total > 0, 1.0 / jnp.maximum(total, 1e-38), 0.0)
        for half in range(2):
            here = slice(half * width, (half + 1) * width)
            mean = acc[c, :, here] * inv[:, here]
            tail = jnp.broadcast_to(l_ref[c : c + 1, here], (8, width))

            @pl.when(core == half)
            def _():
                keep[c, :classes] = mean
                keep[c, classes:] = tail

            @pl.when(core != half)
            def _():
                send[c, :classes] = mean
                send[c, classes:] = tail


def merge_kernel(keep, got, *outs):
    src = lax.axis_index("src")
    classes = keep.shape[1] - 8
    for q, out in enumerate(outs):
        block = (src // 2) ^ q
        mine, other = keep[block], got[block]
        first, second = mine[classes : classes + 1], other[classes : classes + 1]
        both = lse([first, second])
        mean = mine[:classes] * jnp.exp(first - both) + other[:classes] * jnp.exp(second - both)
        out[:classes] = mean.astype(BF16)
        out[classes:] = split_rows(both)


def tail_row(piece):
    return jnp.sum(piece[piece.shape[0] - 16 :].astype(F32), axis=0, keepdims=True)


def combine_kernel(log_b, *rest):
    pieces, out = rest[:-1], rest[-1]
    src = lax.axis_index("src")
    classes, width = out.shape[0] - 16, out.shape[1]
    ls = [tail_row(p[...]) for p in pieces]
    total = lse(ls)
    mass = piece_of(log_b, src, width)
    top = total - mass
    out[:classes] = tree_sum([p[:classes].astype(F32) * jnp.exp(l - top) for p, l in zip(pieces, ls)]).astype(BF16)
    out[classes:] = split_rows(EPS * mass - EPS * total)


def assemble_kernel(order, *refs):
    pieces, (g_out, out, row) = refs[: len(order)], refs[len(order) :]
    src = lax.axis_index("src")
    classes, width = out.shape[0], pieces[0].shape[1]
    for k, piece in zip(order, pieces):
        here = pl.ds(pl.multiple_of((src ^ k) * width, width), width)
        out[:, here] = piece[:classes]
        row[:, here] = tail_row(piece[...])
    g_out[...] = row[...].reshape(g_out.shape)


VM = pl.BlockSpec(memory_space=pltpu.VMEM)
SM = pl.BlockSpec(memory_space=pltpu.SMEM)
HB = pl.BlockSpec(memory_space=pltpu.HBM)
PARAMS = pltpu.CompilerParams(vmem_limit_bytes=LIMIT)


def local(cost, cost_scale, slot_block_row, slot_block_column, device_block_count, log_a, log_b, labels):
    n_src, n_tgt = lax.axis_size("src"), lax.axis_size("tgt")
    slots, tile = cost.shape[1], cost.shape[2]
    rb, cb = log_a.shape[0] // tile, log_b.shape[0] // tile
    classes = labels.shape[1]
    dims = (rb, cb, slots)
    in_hbm = functools.partial(pltpu.with_memory_space_constraint, memory_space=pltpu.HBM)
    in_vmem = functools.partial(pltpu.with_memory_space_constraint, memory_space=pltpu.VMEM)
    in_smem = functools.partial(pltpu.with_memory_space_constraint, memory_space=pltpu.SMEM)

    def xor(x, axis, k):
        return lax.ppermute(x, axis, [(i, i ^ k) for i in range(lax.axis_size(axis))])

    def doubled(part, axis):
        k = 1
        while 2 * k < lax.axis_size(axis):
            part = lse([part, xor(part, axis, k)])
            k *= 2
        return [part, xor(part, axis, k)]

    outer = n_tgt // INNER
    along_z = [[x * INNER + z for z in range(INNER)] for x in range(outer)]
    along_x = [[x * INNER + z for x in range(outer)] for z in range(INNER)]

    def over_tgt(copies):
        parts = lax.all_to_all(copies, "tgt", 0, 0, axis_index_groups=along_z, tiled=True)
        part = lse([parts[z] for z in range(INNER)])
        copies = jnp.broadcast_to(part[None], (outer,) + part.shape)
        return lax.all_to_all(copies, "tgt", 0, 0, axis_index_groups=along_x, tiled=True)

    def grow(lab):
        return jnp.concatenate([lab, xor(lab, "tgt", lab.shape[0])])

    cost = in_hbm(cost)
    vec = functools.partial(jax.ShapeDtypeStruct, dtype=F32)
    chunks = pltpu.VMEM((tile // 128, 128), F32)
    work = [pltpu.SMEM((3,), F32), pltpu.VMEM((tile, tile), BF16), chunks, chunks, pltpu.SemaphoreType.DMA]
    rows, cols = pltpu.VMEM((rb, tile), F32), pltpu.VMEM((cb, tile), F32)

    k_all, row_l, ints, floats, log_a, log_b = pl.pallas_call(
        functools.partial(build_kernel, dims),
        out_shape=(
            pltpu.VMEM((slots, tile, tile), BF16),
            vec((INNER, rb, tile)),
            pltpu.SMEM((1, 2 * slots + 1), jnp.int32),
            pltpu.SMEM((1, slots + 2), F32),
            pltpu.VMEM((rb, tile), F32),
            pltpu.VMEM((cb, tile), F32),
        ),
        in_specs=[SM] * 4 + [VM] * 2 + [HB],
        out_specs=(VM, VM, SM, SM, VM, VM),
        scratch_shapes=[
            rows,
            pltpu.VMEM((slots, tile, tile), BF16),
            rows,
            cols,
            chunks,
            chunks,
            pltpu.SMEM((3,), F32),
            pltpu.SemaphoreType.DMA((slots, 2)),
        ],
        compiler_params=PARAMS,
    )(
        in_hbm(cost_scale),
        in_hbm(slot_block_row),
        in_hbm(slot_block_column),
        device_block_count,
        in_hbm(log_a),
        in_hbm(log_b),
        cost,
    )
    k_all, log_a, log_b = in_vmem(k_all), in_vmem(log_a), in_vmem(log_b)
    scalars = (in_smem(ints), in_smem(floats))
    common = [SM] * 2 + [VM, HB, VM]

    lab = labels.T[None]
    any_spec = pl.BlockSpec(memory_space=pl.ANY)
    for step in range(ITERS):
        row_parts = over_tgt(row_l)
        if step == ITERS - 1:
            break
        col_l, lab = pl.pallas_call(
            functools.partial(col_kernel, slots),
            out_shape=(vec((cb, tile)), jax.ShapeDtypeStruct(lab.shape, BF16)),
            in_specs=common + [any_spec, VM],
            out_specs=(VM, any_spec),
            scratch_shapes=[rows, cols] + work,
            input_output_aliases={5: 1},
            compiler_params=PARAMS,
        )(*scalars, log_a, cost, k_all, lab, row_parts)
        for _ in range(2 if step < ITERS - 2 else 1):
            lab = grow(lab)
        col_parts = doubled(col_l, "src")
        row_l, lab = pl.pallas_call(
            functools.partial(row_kernel, slots, 2),
            out_shape=(vec((INNER, rb, tile)), jax.ShapeDtypeStruct(lab.shape, BF16)),
            in_specs=common + [any_spec] + [VM] * 2,
            out_specs=(VM, any_spec),
            scratch_shapes=[rows, cols, rows] + work,
            input_output_aliases={5: 1},
            compiler_params=PARAMS,
        )(*scalars, log_b, cost, k_all, lab, *col_parts)
    lab = lab.reshape(outer, INNER, classes, -1)

    width = cb * tile // n_src
    half = vec((cb, classes + 8, width))
    piece = jax.ShapeDtypeStruct((classes + 16, width), BF16)
    f_pot, keep, send = pl.pallas_call(
        functools.partial(label_kernel, slots),
        out_shape=(vec((rb, tile)), half, half),
        in_specs=common + [VM] + [VM],
        out_specs=(VM,) * 3,
        scratch_shapes=[pltpu.VMEM((cb, classes, tile), F32), cols, cols] + work,
        compiler_params=PARAMS,
    )(*scalars, log_a, cost, k_all, lab, row_parts)
    n_y = n_src // 2
    pieces = pl.pallas_call(
        merge_kernel,
        out_shape=(piece,) * n_y,
        in_specs=[VM] * 2,
        out_specs=(VM,) * n_y,
        compiler_params=PARAMS,
    )(keep, xor(send, "src", 1))
    pieces = [pieces[0]] + [xor(pieces[q], "src", 2 * q) for q in range(1, n_y)]
    done = pl.pallas_call(
        combine_kernel,
        out_shape=piece,
        in_specs=[VM] * (1 + n_y),
        out_specs=VM,
        compiler_params=PARAMS,
    )(log_b, *pieces)
    pieces = [done] + [xor(done, "src", 2 * q) for q in range(1, n_y)]
    pieces = pieces + [xor(p, "src", 1) for p in pieces]
    order = tuple(2 * q for q in range(n_y)) + tuple(2 * q + 1 for q in range(n_y))
    g_pot, out = pl.pallas_call(
        functools.partial(assemble_kernel, order),
        out_shape=(vec((cb * tile,)), jax.ShapeDtypeStruct((classes, cb * tile), BF16)),
        in_specs=[VM] * n_src,
        out_specs=(VM, VM),
        scratch_shapes=[pltpu.VMEM((1, cb * tile), F32)],
        compiler_params=PARAMS,
    )(*pieces)
    return f_pot.reshape(-1), g_pot, out.T


def solution(mesh):
    in_specs = (
        P("src", "tgt", None, None),
        P("src", "tgt"),
        P("src", "tgt"),
        P("src", "tgt"),
        P("src", "tgt"),
        P("src"),
        P("tgt"),
        P(("src", "tgt"), None),
    )
    out_specs = (P("src"), P("tgt"), P("tgt", None))
    return jax.shard_map(local, mesh=mesh, in_specs=in_specs, out_specs=out_specs, check_vma=False)
```

```python
import functools

import jax
import jax.numpy as jnp
from jax import lax
from jax.experimental import pallas as pl
from jax.experimental.pallas import tpu as pltpu
from jax.sharding import PartitionSpec as P

ITERS = 4
EPS = 0.5
NEG = -1e30
LOG2E = 1.4426950408889634
TO2 = LOG2E / EPS
LIMIT = 40 * 1024 * 1024
F32, BF16 = jnp.float32, jnp.bfloat16


def tree_sum(parts):
    while len(parts) > 1:
        parts = [a + b for a, b in zip(parts[0::2], parts[1::2])]
    return parts[0]


def lse(parts):
    top = functools.reduce(jnp.maximum, parts)
    return top + jnp.log(tree_sum([jnp.exp(p - top) for p in parts]))


class Slots:
    def __init__(self, ints, floats, total):
        self.total = total
        self.row = [ints[0, s] for s in range(total)]
        self.col = [ints[0, total + s] for s in range(total)]
        self.count = ints[0, 2 * total]
        self.live = [s < self.count for s in range(total)]
        self.scale = [floats[0, s] for s in range(total)]
        self.shift, self.high = floats[0, total], floats[0, total + 1]
        self.src, self.tgt = lax.axis_index("src"), lax.axis_index("tgt")


def split_rows(x):
    x = jnp.broadcast_to(x, (16, x.shape[1]))
    hi = x.astype(BF16).astype(F32)
    rest = x - hi
    mid = rest.astype(BF16).astype(F32)
    low = (rest - mid).astype(BF16).astype(F32)
    at = lax.broadcasted_iota(jnp.int32, x.shape, 0)
    zero = jnp.zeros_like(x)
    return jnp.where(at == 0, hi, jnp.where(at == 1, mid, jnp.where(at == 2, low, zero))).astype(BF16)


def k_row(lhs, k_block):
    return lax.dot_general(lhs, k_block, (((1,), (1,)), ((), ())), preferred_element_type=F32)


def k_col(lhs, k_block):
    return lax.dot_general(lhs, k_block, (((1,), (0,)), ((), ())), preferred_element_type=F32)


def chunked(row, out_ref):
    for c in range(out_ref.shape[0]):
        out_ref[c : c + 1, :] = row[:, c * 128 : (c + 1) * 128]


def tile_z(cost_v, scale, other8, out_chunk, red_chunk, rows_mode):
    mine = pl.ds(pl.multiple_of(out_chunk * 128, 128), 128)
    summed = pl.ds(pl.multiple_of(red_chunk * 128, 128), 128)
    other = jnp.broadcast_to(other8[pl.ds(red_chunk, 1), :], (128, 128)).T
    if rows_mode:
        tile = cost_v[mine, summed].astype(F32).T
    else:
        tile = cost_v[summed, mine].astype(F32)
    return (other - scale * tile) / EPS


def slow_lse(slots, cost_hbm, cost_v, sem, other8, out8, other_ref, l_ref, rows_mode):
    l_ref[...] = jnp.full(l_ref.shape, NEG, F32)
    chunks = out8.shape[0]
    for s in range(slots.total):
        out_at, other_at = (slots.row[s], slots.col[s]) if rows_mode else (slots.col[s], slots.row[s])

        @pl.when(slots.live[s])
        def _():
            copy = pltpu.make_async_copy(cost_hbm.at[0, s], cost_v, sem)
            copy.start()
            copy.wait()
            chunked(other_ref[pl.ds(other_at, 1), :], other8)

            @pl.loop(0, chunks)
            def _(i):
                def step(j, carry):
                    m, total = carry
                    z = tile_z(cost_v, slots.scale[s], other8, i, j, rows_mode)
                    top = jnp.maximum(m, jnp.max(z, axis=0, keepdims=True))
                    total = total * jnp.exp(m - top) + jnp.sum(jnp.exp(z - top), axis=0, keepdims=True)
                    return top, total

                first = (jnp.full((1, 128), NEG, F32), jnp.zeros((1, 128), F32))
                m, total = lax.fori_loop(0, chunks, step, first)
                out8[pl.ds(i, 1), :] = m + jnp.log(total)

            new = jnp.concatenate([out8[c : c + 1, :] for c in range(chunks)], axis=1)
            old = l_ref[pl.ds(out_at, 1), :]
            top = jnp.maximum(old, new)
            l_ref[pl.ds(out_at, 1), :] = top + jnp.log(jnp.exp(old - top) + jnp.exp(new - top))


def piece_of(ref, piece, width):
    per = ref.shape[1] // width
    row = ref[pl.ds(piece // per, 1), :]
    out = row[:, :width]
    for c in range(1, per):
        out = jnp.where(piece % per == c, row[:, c * width : (c + 1) * width], out)
    return out


def to_log(total, shift):
    return jnp.where(total > 0, jnp.log(jnp.maximum(total, 1e-38)) - shift / EPS, NEG)


def send_copies(l_ref, copies_ref):
    for k in range(copies_ref.shape[0]):
        copies_ref[k] = l_ref[...]


def sums_fine(low, high, others):
    return (low >= 2.0**-80 * jnp.maximum(others, 1.0)) & (high <= 2.0**100)


def build_kernel(
    dims, scale, row, col, count, log_a, log_b, cost_hbm,
    k_hbm, copies_ref, ints, floats, a_ref, b_ref,
    l_ref, k_ref, cost_v, sums, zero, other8, out8, stat, sems, k_sems,
):
    rb, cb, total = dims
    src, tgt = lax.axis_index("src"), lax.axis_index("tgt")
    for s in range(total):
        ints[0, s] = row[0, s] - src * rb
        ints[0, total + s] = col[0, s] - tgt * cb
        floats[0, s] = scale[0, s]
    ints[0, 2 * total] = count[0, 0]
    slots = Slots(ints, floats, total)
    half = cost_v.shape[1] // 2
    copies = [
        [
            pltpu.make_async_copy(
                cost_hbm.at[0, s, pl.ds(h * half, half)], cost_v.at[s, pl.ds(h * half, half)], sems.at[s, h]
            )
            for h in range(2)
        ]
        for s in range(total)
    ]
    for s in range(total):

        @pl.when(slots.live[s])
        def _():
            for h in range(2):
                copies[s][h].start()

    k_copies = [pltpu.make_async_copy(k_ref.at[s], k_hbm.at[s], k_sems.at[s]) for s in range(total)]
    tile = cost_v.shape[2]
    for r in range(rb):
        a_ref[r : r + 1, :] = log_a[r * tile : (r + 1) * tile].reshape(1, tile)
    for c in range(cb):
        b_ref[c : c + 1, :] = log_b[c * tile : (c + 1) * tile].reshape(1, tile)
    chunk = 32
    ones = jnp.ones((16, cost_v.shape[2]), BF16)

    def build(shift, wait):
        sums[...] = jnp.zeros(sums.shape, F32)
        floats[0, total] = shift
        stat[1] = jnp.float32(0.0)
        stat[2] = jnp.float32(jnp.inf)
        for s in range(total):

            @pl.when(slots.live[s])
            def _():
                for h in range(2):
                    if wait:
                        copies[s][h].wait()

                    @pl.loop(0, half // chunk, unroll=2)
                    def _(i):
                        here = pl.ds(pl.multiple_of(h * half + i * chunk, chunk), chunk)
                        x = cost_v[s, here, :].astype(F32)
                        x = x * (-TO2 * slots.scale[s]) + shift * TO2
                        k_ref[s, here, :] = jnp.exp2(x).astype(BF16)

                k_copies[s].start()
                part = k_row(ones, k_ref[s])[0:1]
                at = pl.ds(slots.row[s], 1)
                sums[at, :] = sums[at, :] + part
                stat[1] = jnp.maximum(stat[1], jnp.max(part))
                stat[2] = jnp.minimum(stat[2], jnp.min(part))

        for s in range(total):

            @pl.when(slots.live[s])
            def _():
                k_copies[s].wait()

        l_ref[...] = to_log(sums[...], shift)
        floats[0, total + 1] = stat[1]
        return sums_fine(stat[2], stat[1], stat[1])

    fine = build(jnp.float32(0.0), True)

    @pl.when(jnp.logical_not(fine))
    def _():
        stat[0] = jnp.float32(jnp.inf)
        for s in range(total):

            @pl.when(slots.live[s])
            def _():
                def lowest(i, low):
                    here = pl.ds(pl.multiple_of(i * chunk, chunk), chunk)
                    return jnp.minimum(low, jnp.min(cost_v[s, here, :].astype(F32)))

                low = lax.fori_loop(0, 2 * half // chunk, lowest, jnp.float32(jnp.inf))
                stat[0] = jnp.minimum(stat[0], low * slots.scale[s])

        shifted = build(stat[0], False)

        @pl.when(jnp.logical_not(shifted))
        def _():
            zero[...] = jnp.zeros(zero.shape, F32)
            slow_lse(slots, cost_hbm, cost_v.at[0], sems.at[0, 0], other8, out8, zero, l_ref, True)

    send_copies(l_ref, copies_ref)


def row_kernel(total, ints, floats, log_b, cost_hbm, k_ref, parts, *rest):
    copies_ref, l_ref, g, sums, stat, cost_v, other8, out8, sem = rest
    slots = Slots(ints, floats, total)
    g[...] = EPS * log_b[...] - EPS * lse([parts[k] for k in range(parts.shape[0])])
    sums[...] = jnp.zeros(sums.shape, F32)
    stat[0] = jnp.float32(0.0)
    stat[1] = jnp.float32(jnp.inf)
    stat[2] = slots.high
    for s in range(slots.total):

        @pl.when(slots.live[s])
        def _():
            v = jnp.exp2(g[pl.ds(slots.col[s], 1), :] * TO2)
            part = jnp.sum(k_row(split_rows(v), k_ref[s]), axis=0, keepdims=True)
            at = pl.ds(slots.row[s], 1)
            sums[at, :] = sums[at, :] + part
            stat[0] = jnp.maximum(stat[0], jnp.max(part))
            stat[1] = jnp.minimum(stat[1], jnp.min(part))
            stat[2] = jnp.maximum(stat[2], jnp.max(v))

    l_ref[...] = to_log(sums[...], slots.shift)

    @pl.when(jnp.logical_not(sums_fine(stat[1], stat[0], stat[2])))
    def _():
        slow_lse(slots, cost_hbm, cost_v, sem, other8, out8, g, l_ref, True)

    send_copies(l_ref, copies_ref)


def col_kernel(total, ints, floats, log_a, cost_hbm, k_ref, parts, *rest):
    copies_ref, l_ref, f, sums, stat, cost_v, other8, out8, sem = rest
    slots = Slots(ints, floats, total)
    f[...] = EPS * log_a[...] - EPS * lse([parts[k] for k in range(parts.shape[0])])
    sums[...] = jnp.zeros(sums.shape, F32)
    stat[0] = jnp.float32(0.0)
    stat[1] = jnp.float32(jnp.inf)
    stat[2] = slots.high
    for s in range(slots.total):

        @pl.when(slots.live[s])
        def _():
            u = jnp.exp2(f[pl.ds(slots.row[s], 1), :] * TO2)
            part = jnp.sum(k_col(split_rows(u), k_ref[s]), axis=0, keepdims=True)
            at = pl.ds(slots.col[s], 1)
            sums[at, :] = sums[at, :] + part
            stat[0] = jnp.maximum(stat[0], jnp.max(part))
            stat[1] = jnp.minimum(stat[1], jnp.min(part))
            stat[2] = jnp.maximum(stat[2], jnp.max(u))

    l_ref[...] = to_log(sums[...], slots.shift)

    @pl.when(jnp.logical_not(sums_fine(stat[1], stat[0], stat[2])))
    def _():
        slow_lse(slots, cost_hbm, cost_v, sem, other8, out8, f, l_ref, False)

    send_copies(l_ref, copies_ref)


def label_kernel(total, ints, floats, log_a, cost_hbm, k_ref, labels, parts, *rest):
    f_out, keep, send, acc, l_ref, sums, stat, cost_v, other8, out8, sem = rest
    slots = Slots(ints, floats, total)
    classes = acc.shape[1]
    f_out[...] = EPS * log_a[...] - EPS * lse([parts[k] for k in range(parts.shape[0])])
    sums[...] = jnp.zeros(sums.shape, F32)
    acc[...] = jnp.zeros(acc.shape, F32)
    stat[0] = jnp.float32(0.0)
    stat[1] = jnp.float32(jnp.inf)
    stat[2] = slots.high
    per = labels.shape[0] // acc.shape[0]
    for s in range(slots.total):

        @pl.when(slots.live[s])
        def _():
            u = jnp.exp2(f_out[pl.ds(slots.row[s], 1), :] * TO2)
            lab = jnp.concatenate([labels[slots.row[s] * per + p] for p in range(per)], axis=1)
            weighted = lab.astype(F32) * u
            hi = weighted.astype(BF16)
            low = (weighted - hi.astype(F32)).astype(BF16)
            res = k_col(jnp.concatenate([hi, low, split_rows(u)], axis=0), k_ref[s])
            part = jnp.sum(res[2 * classes :], axis=0, keepdims=True)
            at = pl.ds(slots.col[s], 1)
            sums[at, :] = sums[at, :] + part
            acc[slots.col[s]] = acc[slots.col[s]] + (res[:classes] + res[classes : 2 * classes])
            stat[0] = jnp.maximum(stat[0], jnp.max(part))
            stat[1] = jnp.minimum(stat[1], jnp.min(part))
            stat[2] = jnp.maximum(stat[2], jnp.max(u))

    l_ref[...] = to_log(sums[...], slots.shift)

    @pl.when(jnp.logical_not(sums_fine(stat[1], stat[0], stat[2])))
    def _():
        slow_lse(slots, cost_hbm, cost_v, sem, other8, out8, f_out, l_ref, False)
        acc[...] = jnp.zeros(acc.shape, F32)
        sums[...] = jnp.ones(sums.shape, F32)
        chunks = cost_v.shape[0] // 128
        for s in range(slots.total):

            @pl.when(slots.live[s])
            def _():
                copy = pltpu.make_async_copy(cost_hbm.at[0, s], cost_v, sem)
                copy.start()
                copy.wait()
                chunked(f_out[pl.ds(slots.row[s], 1), :], other8)
                chunked(l_ref[pl.ds(slots.col[s], 1), :], out8)

                @pl.loop(0, chunks * chunks)
                def _(ij):
                    i, j = ij // chunks, ij % chunks
                    here = pl.ds(pl.multiple_of(i * 128, 128), 128)
                    z = tile_z(cost_v, slots.scale[s], other8, i, j, False)
                    p = jnp.exp(z - out8[pl.ds(i, 1), :]).astype(BF16)
                    lab = labels[slots.row[s] * per + j]
                    term = jnp.dot(lab, p, preferred_element_type=F32)
                    acc[slots.col[s], :, here] = acc[slots.col[s], :, here] + term

    core = slots.src % 2
    width = keep.shape[2]
    for c in range(acc.shape[0]):
        total = sums[c : c + 1, :]
        inv = jnp.where(total > 0, 1.0 / jnp.maximum(total, 1e-38), 0.0)
        for half in range(2):
            here = slice(half * width, (half + 1) * width)
            mean = acc[c, :, here] * inv[:, here]
            tail = jnp.broadcast_to(l_ref[c : c + 1, here], (8, width))

            @pl.when(core == half)
            def _():
                keep[c, :classes] = mean
                keep[c, classes:] = tail

            @pl.when(core != half)
            def _():
                send[c, :classes] = mean
                send[c, classes:] = tail


def pass_kernel(*refs):
    pass


def merge_kernel(keep, got, *outs):
    src = lax.axis_index("src")
    classes = keep.shape[1] - 8
    for q, out in enumerate(outs):
        block = (src // 2) ^ q
        mine, other = keep[block], got[block]
        first, second = mine[classes : classes + 1], other[classes : classes + 1]
        both = lse([first, second])
        mean = mine[:classes] * jnp.exp(first - both) + other[:classes] * jnp.exp(second - both)
        out[:classes] = mean.astype(BF16)
        out[classes:] = split_rows(both)


def tail_row(piece):
    return jnp.sum(piece[piece.shape[0] - 16 :].astype(F32), axis=0, keepdims=True)


def combine_kernel(log_b, *rest):
    pieces, out = rest[:-1], rest[-1]
    src = lax.axis_index("src")
    classes, width = out.shape[0] - 16, out.shape[1]
    ls = [tail_row(p[...]) for p in pieces]
    total = lse(ls)
    mass = piece_of(log_b, src, width)
    top = total - mass
    out[:classes] = tree_sum([p[:classes].astype(F32) * jnp.exp(l - top) for p, l in zip(pieces, ls)]).astype(BF16)
    out[classes:] = split_rows(EPS * mass - EPS * total)


def assemble_kernel(order, *refs):
    pieces, (g_out, out, row) = refs[: len(order)], refs[len(order) :]
    src = lax.axis_index("src")
    classes, width = out.shape[0], pieces[0].shape[1]
    for k, piece in zip(order, pieces):
        here = pl.ds(pl.multiple_of((src ^ k) * width, width), width)
        out[:, here] = piece[:classes]
        row[:, here] = tail_row(piece[...])
    g_out[...] = row[...].reshape(g_out.shape)


VM = pl.BlockSpec(memory_space=pltpu.VMEM)
SM = pl.BlockSpec(memory_space=pltpu.SMEM)
HB = pl.BlockSpec(memory_space=pltpu.HBM)
PARAMS = pltpu.CompilerParams(vmem_limit_bytes=LIMIT)


def local(cost, cost_scale, slot_block_row, slot_block_column, device_block_count, log_a, log_b, labels):
    n_src, n_tgt = lax.axis_size("src"), lax.axis_size("tgt")
    slots, tile = cost.shape[1], cost.shape[2]
    rb, cb = log_a.shape[0] // tile, log_b.shape[0] // tile
    classes = labels.shape[1]
    dims = (rb, cb, slots)
    in_hbm = functools.partial(pltpu.with_memory_space_constraint, memory_space=pltpu.HBM)
    in_vmem = functools.partial(pltpu.with_memory_space_constraint, memory_space=pltpu.VMEM)
    in_smem = functools.partial(pltpu.with_memory_space_constraint, memory_space=pltpu.SMEM)

    def xor(x, axis, k):
        return lax.ppermute(x, axis, [(i, i ^ k) for i in range(lax.axis_size(axis))])

    def everyone(copies, axis):
        return lax.all_to_all(copies, axis, 0, 0, tiled=True)

    lab = everyone(jnp.broadcast_to(labels.T[None], (n_tgt, classes, labels.shape[0])), "tgt")

    cost = in_hbm(cost)
    vec = functools.partial(jax.ShapeDtypeStruct, dtype=F32)
    chunks = pltpu.VMEM((tile // 128, 128), F32)
    work = [pltpu.SMEM((3,), F32), pltpu.VMEM((tile, tile), BF16), chunks, chunks, pltpu.SemaphoreType.DMA]
    rows, cols = pltpu.VMEM((rb, tile), F32), pltpu.VMEM((cb, tile), F32)

    k_all, row_l, ints, floats, log_a, log_b = pl.pallas_call(
        functools.partial(build_kernel, dims),
        out_shape=(
            jax.ShapeDtypeStruct((slots, tile, tile), BF16),
            vec((n_tgt, rb, tile)),
            pltpu.SMEM((1, 2 * slots + 1), jnp.int32),
            pltpu.SMEM((1, slots + 2), F32),
            pltpu.VMEM((rb, tile), F32),
            pltpu.VMEM((cb, tile), F32),
        ),
        in_specs=[SM] * 4 + [VM] * 2 + [HB],
        out_specs=(HB, VM, SM, SM, VM, VM),
        scratch_shapes=[
            rows,
            pltpu.VMEM((slots, tile, tile), BF16),
            pltpu.VMEM((slots, tile, tile), BF16),
            rows,
            cols,
            chunks,
            chunks,
            pltpu.SMEM((3,), F32),
            pltpu.SemaphoreType.DMA((slots, 2)),
            pltpu.SemaphoreType.DMA((slots,)),
        ],
        cost_estimate=pl.CostEstimate(
            flops=40 * slots * tile * tile, bytes_accessed=4 * slots * tile * tile, transcendentals=slots * tile * tile
        ),
        compiler_params=PARAMS,
    )(
        in_hbm(cost_scale),
        in_hbm(slot_block_row),
        in_hbm(slot_block_column),
        device_block_count,
        in_hbm(log_a),
        in_hbm(log_b),
        cost,
    )
    k_all, log_a, log_b = in_vmem(k_all), in_vmem(log_a), in_vmem(log_b)
    scalars = (in_smem(ints), in_smem(floats))
    common = [SM] * 2 + [VM, HB, VM]

    any_spec = pl.BlockSpec(memory_space=pl.ANY)
    row_l, lab = pl.pallas_call(
        pass_kernel,
        out_shape=tuple(jax.ShapeDtypeStruct(x.shape, x.dtype) for x in (row_l, lab)),
        in_specs=[any_spec] * 2,
        out_specs=(any_spec,) * 2,
        input_output_aliases={0: 0, 1: 1},
        compiler_params=PARAMS,
    )(row_l, lab)
    for step in range(ITERS):
        row_parts = everyone(row_l, "tgt")
        if step == ITERS - 1:
            break
        col_l = pl.pallas_call(
            functools.partial(col_kernel, slots),
            out_shape=vec((n_src, cb, tile)),
            in_specs=common + [VM],
            out_specs=VM,
            scratch_shapes=[cols, rows, cols] + work,
            compiler_params=PARAMS,
        )(*scalars, log_a, cost, k_all, row_parts)
        row_l = pl.pallas_call(
            functools.partial(row_kernel, slots),
            out_shape=vec((n_tgt, rb, tile)),
            in_specs=common + [VM],
            out_specs=VM,
            scratch_shapes=[rows, cols, rows] + work,
            compiler_params=PARAMS,
        )(*scalars, log_b, cost, k_all, everyone(col_l, "src"))

    width = cb * tile // n_src
    half = vec((cb, classes + 8, width))
    piece = jax.ShapeDtypeStruct((classes + 16, width), BF16)
    f_pot, keep, send = pl.pallas_call(
        functools.partial(label_kernel, slots),
        out_shape=(vec((rb, tile)), half, half),
        in_specs=common + [VM] + [VM],
        out_specs=(VM,) * 3,
        scratch_shapes=[pltpu.VMEM((cb, classes, tile), F32), cols, cols] + work,
        compiler_params=PARAMS,
    )(*scalars, log_a, cost, k_all, lab, row_parts)
    n_y = n_src // 2
    pieces = pl.pallas_call(
        merge_kernel,
        out_shape=(piece,) * n_y,
        in_specs=[VM] * 2,
        out_specs=(VM,) * n_y,
        compiler_params=PARAMS,
    )(keep, xor(send, "src", 1))
    pieces = [pieces[0]] + [xor(pieces[q], "src", 2 * q) for q in range(1, n_y)]
    done = pl.pallas_call(
        combine_kernel,
        out_shape=piece,
        in_specs=[VM] * (1 + n_y),
        out_specs=VM,
        compiler_params=PARAMS,
    )(log_b, *pieces)
    pieces = [done] + [xor(done, "src", 2 * q) for q in range(1, n_y)]
    pieces = pieces + [xor(p, "src", 1) for p in pieces]
    order = tuple(2 * q for q in range(n_y)) + tuple(2 * q + 1 for q in range(n_y))
    g_pot, out = pl.pallas_call(
        functools.partial(assemble_kernel, order),
        out_shape=(vec((cb * tile,)), jax.ShapeDtypeStruct((classes, cb * tile), BF16)),
        in_specs=[VM] * n_src,
        out_specs=(VM, VM),
        scratch_shapes=[pltpu.VMEM((1, cb * tile), F32)],
        compiler_params=PARAMS,
    )(*pieces)
    return f_pot.reshape(-1), g_pot, out.T


def solution(mesh):
    in_specs = (
        P("src", "tgt", None, None),
        P("src", "tgt"),
        P("src", "tgt"),
        P("src", "tgt"),
        P("src", "tgt"),
        P("src"),
        P("tgt"),
        P(("src", "tgt"), None),
    )
    out_specs = (P("src"), P("tgt"), P("tgt", None))
    return jax.shard_map(local, mesh=mesh, in_specs=in_specs, out_specs=out_specs, check_vma=False)
```

```python
import functools

import jax
import jax.numpy as jnp
from jax import lax
from jax.experimental import pallas as pl
from jax.experimental.pallas import tpu as pltpu
from jax.sharding import PartitionSpec as P

ITERS = 4
EPS = 0.5
NEG = -1e30
LOG2E = 1.4426950408889634
TO2 = LOG2E / EPS
INNER = 8
FLAT = (16, 256)
SHARE = ((0, 1, 2), (3, 4, 5), (6, 7))
LIMIT = 40 * 1024 * 1024
F32, BF16 = jnp.float32, jnp.bfloat16


def tree_sum(parts):
    while len(parts) > 1:
        parts = [a + b for a, b in zip(parts[0::2], parts[1::2])]
    return parts[0]


def lse(parts):
    top = functools.reduce(jnp.maximum, parts)
    return top + jnp.log(tree_sum([jnp.exp(p - top) for p in parts]))


class Slots:
    def __init__(self, ints, floats, total):
        self.total = total
        self.row = [ints[0, s] for s in range(total)]
        self.col = [ints[0, total + s] for s in range(total)]
        self.count = ints[0, 2 * total]
        self.live = [s < self.count for s in range(total)]
        self.scale = [floats[0, s] for s in range(total)]
        self.shift, self.high = floats[0, total], floats[0, total + 1]
        self.src, self.tgt = lax.axis_index("src"), lax.axis_index("tgt")


def split_rows(x):
    x = jnp.broadcast_to(x, (16, x.shape[1]))
    hi = x.astype(BF16).astype(F32)
    rest = x - hi
    mid = rest.astype(BF16).astype(F32)
    low = (rest - mid).astype(BF16).astype(F32)
    at = lax.broadcasted_iota(jnp.int32, x.shape, 0)
    zero = jnp.zeros_like(x)
    return jnp.where(at == 0, hi, jnp.where(at == 1, mid, jnp.where(at == 2, low, zero))).astype(BF16)


def k_row(lhs, k_block):
    return lax.dot_general(lhs, k_block, (((1,), (1,)), ((), ())), preferred_element_type=F32)


def k_col(lhs, k_block):
    return lax.dot_general(lhs, k_block, (((1,), (0,)), ((), ())), preferred_element_type=F32)


def chunked(row, out_ref):
    for c in range(out_ref.shape[0]):
        out_ref[c : c + 1, :] = row[:, c * 128 : (c + 1) * 128]


def tile_z(cost_v, scale, other8, out_chunk, red_chunk, rows_mode):
    mine = pl.ds(pl.multiple_of(out_chunk * 128, 128), 128)
    summed = pl.ds(pl.multiple_of(red_chunk * 128, 128), 128)
    other = jnp.broadcast_to(other8[pl.ds(red_chunk, 1), :], (128, 128)).T
    if rows_mode:
        tile = cost_v[mine, summed].astype(F32).T
    else:
        tile = cost_v[summed, mine].astype(F32)
    return (other - scale * tile) / EPS


def slow_lse(slots, cost_hbm, cost_v, sem, other8, out8, other_ref, l_ref, rows_mode):
    l_ref[...] = jnp.full(l_ref.shape, NEG, F32)
    chunks = out8.shape[0]
    for s in range(slots.total):
        out_at, other_at = (slots.row[s], slots.col[s]) if rows_mode else (slots.col[s], slots.row[s])

        @pl.when(slots.live[s])
        def _():
            copy = pltpu.make_async_copy(cost_hbm.at[0, s], cost_v, sem)
            copy.start()
            copy.wait()
            chunked(other_ref[pl.ds(other_at, 1), :], other8)

            @pl.loop(0, chunks)
            def _(i):
                def step(j, carry):
                    m, total = carry
                    z = tile_z(cost_v, slots.scale[s], other8, i, j, rows_mode)
                    top = jnp.maximum(m, jnp.max(z, axis=0, keepdims=True))
                    total = total * jnp.exp(m - top) + jnp.sum(jnp.exp(z - top), axis=0, keepdims=True)
                    return top, total

                first = (jnp.full((1, 128), NEG, F32), jnp.zeros((1, 128), F32))
                m, total = lax.fori_loop(0, chunks, step, first)
                out8[pl.ds(i, 1), :] = m + jnp.log(total)

            new = jnp.concatenate([out8[c : c + 1, :] for c in range(chunks)], axis=1)
            old = l_ref[pl.ds(out_at, 1), :]
            top = jnp.maximum(old, new)
            l_ref[pl.ds(out_at, 1), :] = top + jnp.log(jnp.exp(old - top) + jnp.exp(new - top))


def piece_of(ref, piece, width):
    per = ref.shape[1] // width
    row = ref[pl.ds(piece // per, 1), :]
    out = row[:, :width]
    for c in range(1, per):
        out = jnp.where(piece % per == c, row[:, c * width : (c + 1) * width], out)
    return out


def to_log(total, shift):
    return jnp.where(total > 0, jnp.log(jnp.maximum(total, 1e-38)) - shift / EPS, NEG)


def send_copies(l_ref, copies_ref):
    for k in range(copies_ref.shape[0]):
        copies_ref[k] = l_ref[...]


def send_relative(l_ref, pot, log_mass, flat, copies_ref):
    rel = jnp.exp(l_ref[...] + pot[...] / EPS - log_mass[...])
    count, width = rel.shape[0], flat.shape[1]
    for c in range(rel.shape[1] // width):
        flat[c * count : (c + 1) * count, :] = rel[:, c * width : (c + 1) * width]
    rel = flat[...].astype(BF16)
    for k in range(copies_ref.shape[0]):
        copies_ref[k, : flat.shape[0]] = rel


def new_potential(out, log_mass, parts, prev, flat):
    if prev is None:
        out[...] = EPS * log_mass[...] - EPS * lse([parts[k] for k in range(parts.shape[0])])
        return
    flat[...] = tree_sum([parts[k, : flat.shape[0]].astype(F32) for k in range(parts.shape[0])])
    count, width = out.shape[0], flat.shape[1]
    for c in range(out.shape[1] // width):
        here = slice(c * width, (c + 1) * width)
        out[:, here] = prev[:, here] - EPS * jnp.log(flat[c * count : (c + 1) * count, :])


def sums_fine(low, high, others):
    return (low >= 2.0**-80 * jnp.maximum(others, 1.0)) & (high <= 2.0**100)


def build_kernel(
    dims, scale, row, col, count, log_a, log_b, cost_hbm,
    k_ref, copies_ref, ints, floats, a_ref, b_ref,
    l_ref, cost_v, sums, zero, other8, out8, stat, sems,
):
    rb, cb, total = dims
    src, tgt = lax.axis_index("src"), lax.axis_index("tgt")
    for s in range(total):
        ints[0, s] = row[0, s] - src * rb
        ints[0, total + s] = col[0, s] - tgt * cb
        floats[0, s] = scale[0, s]
    ints[0, 2 * total] = count[0, 0]
    slots = Slots(ints, floats, total)
    half = cost_v.shape[1] // 2
    copies = [
        [
            pltpu.make_async_copy(
                cost_hbm.at[0, s, pl.ds(h * half, half)], cost_v.at[s, pl.ds(h * half, half)], sems.at[s, h]
            )
            for h in range(2)
        ]
        for s in range(total)
    ]
    for s in range(total):

        @pl.when(slots.live[s])
        def _():
            for h in range(2):
                copies[s][h].start()

    tile = cost_v.shape[2]
    for r in range(rb):
        a_ref[r : r + 1, :] = log_a[r * tile : (r + 1) * tile].reshape(1, tile)
    for c in range(cb):
        b_ref[c : c + 1, :] = log_b[c * tile : (c + 1) * tile].reshape(1, tile)
    chunk = 32
    ones = jnp.ones((16, cost_v.shape[2]), BF16)

    def build(shift, wait):
        sums[...] = jnp.zeros(sums.shape, F32)
        floats[0, total] = shift
        stat[1] = jnp.float32(0.0)
        stat[2] = jnp.float32(jnp.inf)
        for s in range(total):

            @pl.when(slots.live[s])
            def _():
                for h in range(2):
                    if wait:
                        copies[s][h].wait()

                    @pl.loop(0, half // chunk, unroll=2)
                    def _(i):
                        here = pl.ds(pl.multiple_of(h * half + i * chunk, chunk), chunk)
                        x = cost_v[s, here, :].astype(F32)
                        x = x * (-TO2 * slots.scale[s]) + shift * TO2
                        k_ref[s, here, :] = jnp.exp2(x).astype(BF16)

                part = k_row(ones, k_ref[s])[0:1]
                at = pl.ds(slots.row[s], 1)
                sums[at, :] = sums[at, :] + part
                stat[1] = jnp.maximum(stat[1], jnp.max(part))
                stat[2] = jnp.minimum(stat[2], jnp.min(part))

        l_ref[...] = to_log(sums[...], shift)
        floats[0, total + 1] = stat[1]
        return sums_fine(stat[2], stat[1], stat[1])

    fine = build(jnp.float32(0.0), True)

    @pl.when(jnp.logical_not(fine))
    def _():
        stat[0] = jnp.float32(jnp.inf)
        for s in range(total):

            @pl.when(slots.live[s])
            def _():
                def lowest(i, low):
                    here = pl.ds(pl.multiple_of(i * chunk, chunk), chunk)
                    return jnp.minimum(low, jnp.min(cost_v[s, here, :].astype(F32)))

                low = lax.fori_loop(0, 2 * half // chunk, lowest, jnp.float32(jnp.inf))
                stat[0] = jnp.minimum(stat[0], low * slots.scale[s])

        shifted = build(stat[0], False)

        @pl.when(jnp.logical_not(shifted))
        def _():
            zero[...] = jnp.zeros(zero.shape, F32)
            slow_lse(slots, cost_hbm, cost_v.at[0], sems.at[0, 0], other8, out8, zero, l_ref, True)

    send_copies(l_ref, copies_ref)


def row_kernel(total, first, with_labels, ints, floats, log_b, cost_hbm, k_ref, parts, log_a, f, *rest):
    prev, rest = (None, rest) if first else (rest[0], rest[1:])
    lab, rest = (rest[0], rest[1:]) if with_labels else (None, rest)
    copies_ref, g, l_ref, flat, sums, stat, cost_v, other8, out8, sem = rest
    slots = Slots(ints, floats, total)
    new_potential(g, log_b, parts, prev, flat)
    sums[...] = jnp.zeros(sums.shape, F32)
    stat[0] = jnp.float32(0.0)
    stat[1] = jnp.float32(jnp.inf)
    stat[2] = slots.high
    for s in range(slots.total):

        @pl.when(slots.live[s])
        def _():
            v = jnp.exp2(g[pl.ds(slots.col[s], 1), :] * TO2)
            part = jnp.sum(k_row(split_rows(v), k_ref[s]), axis=0, keepdims=True)
            at = pl.ds(slots.row[s], 1)
            sums[at, :] = sums[at, :] + part
            stat[0] = jnp.maximum(stat[0], jnp.max(part))
            stat[1] = jnp.minimum(stat[1], jnp.min(part))
            stat[2] = jnp.maximum(stat[2], jnp.max(v))

    l_ref[...] = to_log(sums[...], slots.shift)

    @pl.when(jnp.logical_not(sums_fine(stat[1], stat[0], stat[2])))
    def _():
        slow_lse(slots, cost_hbm, cost_v, sem, other8, out8, g, l_ref, True)

    send_relative(l_ref, f, log_a, flat, copies_ref)
    if with_labels:
        half = lab.shape[0] // 2
        for k in range(copies_ref.shape[0]):
            copies_ref[k, flat.shape[0] :] = jnp.concatenate([lab[:half], lab[half:]], axis=1)


def relay_kernel(share, parts, lab, copies_ref):
    rows = FLAT[0]
    total = tree_sum([parts[k, :rows].astype(F32) for k in range(parts.shape[0])]).astype(BF16)
    high = lab.shape[1] - rows
    for k in range(copies_ref.shape[0]):
        copies_ref[k, :rows] = total
        for i, p in enumerate(share):
            copies_ref[k, rows + i * high : rows + (i + 1) * high] = lab[p, rows:]


def col_kernel(total, first, ints, floats, log_a, cost_hbm, k_ref, parts, *rest):
    (prev, log_b, g), rest = ((None, None, None), rest) if first else (rest[:3], rest[3:])
    copies_ref, f, l_ref, flat, sums, stat, cost_v, other8, out8, sem = rest
    slots = Slots(ints, floats, total)
    new_potential(f, log_a, parts, prev, flat)
    sums[...] = jnp.zeros(sums.shape, F32)
    stat[0] = jnp.float32(0.0)
    stat[1] = jnp.float32(jnp.inf)
    stat[2] = slots.high
    for s in range(slots.total):

        @pl.when(slots.live[s])
        def _():
            u = jnp.exp2(f[pl.ds(slots.row[s], 1), :] * TO2)
            part = jnp.sum(k_col(split_rows(u), k_ref[s]), axis=0, keepdims=True)
            at = pl.ds(slots.col[s], 1)
            sums[at, :] = sums[at, :] + part
            stat[0] = jnp.maximum(stat[0], jnp.max(part))
            stat[1] = jnp.minimum(stat[1], jnp.min(part))
            stat[2] = jnp.maximum(stat[2], jnp.max(u))

    l_ref[...] = to_log(sums[...], slots.shift)

    @pl.when(jnp.logical_not(sums_fine(stat[1], stat[0], stat[2])))
    def _():
        slow_lse(slots, cost_hbm, cost_v, sem, other8, out8, f, l_ref, False)

    if first:
        send_copies(l_ref, copies_ref)
    else:
        send_relative(l_ref, g, log_b, flat, copies_ref)


def label_kernel(total, ints, floats, log_a, cost_hbm, k_ref, prev, *rest):
    boxes, rest = rest[: len(SHARE)], rest[len(SHARE) :]
    f_out, keep, send, acc, l_ref, flat, lab_v, sums, stat, cost_v, other8, out8, sem = rest
    slots = Slots(ints, floats, total)
    classes = acc.shape[1]
    new_potential(f_out, log_a, boxes[-1], prev, flat)
    sums[...] = jnp.zeros(sums.shape, F32)
    acc[...] = jnp.zeros(acc.shape, F32)
    stat[0] = jnp.float32(0.0)
    stat[1] = jnp.float32(jnp.inf)
    stat[2] = slots.high
    high = classes // 2

    def label_piece(block, p):
        box = [i for i, share in enumerate(SHARE) if p in share][0]
        at = FLAT[0] + SHARE[box].index(p) * high
        both = boxes[box][block, at : at + high]
        return jnp.concatenate([both[:, :128], both[:, 128:]], axis=0)

    for s in range(slots.total):

        @pl.when(slots.live[s])
        def _():
            u = jnp.exp2(f_out[pl.ds(slots.row[s], 1), :] * TO2)
            lab = jnp.concatenate([label_piece(slots.row[s], p) for p in range(INNER)], axis=1)
            weighted = lab.astype(F32) * u
            hi = weighted.astype(BF16)
            low = (weighted - hi.astype(F32)).astype(BF16)
            res = k_col(jnp.concatenate([hi, low, split_rows(u)], axis=0), k_ref[s])
            part = jnp.sum(res[2 * classes :], axis=0, keepdims=True)
            at = pl.ds(slots.col[s], 1)
            sums[at, :] = sums[at, :] + part
            acc[slots.col[s]] = acc[slots.col[s]] + (res[:classes] + res[classes : 2 * classes])
            stat[0] = jnp.maximum(stat[0], jnp.max(part))
            stat[1] = jnp.minimum(stat[1], jnp.min(part))
            stat[2] = jnp.maximum(stat[2], jnp.max(u))

    l_ref[...] = to_log(sums[...], slots.shift)

    @pl.when(jnp.logical_not(sums_fine(stat[1], stat[0], stat[2])))
    def _():
        slow_lse(slots, cost_hbm, cost_v, sem, other8, out8, f_out, l_ref, False)
        acc[...] = jnp.zeros(acc.shape, F32)
        sums[...] = jnp.ones(sums.shape, F32)
        chunks = cost_v.shape[0] // 128
        for s in range(slots.total):

            @pl.when(slots.live[s])
            def _():
                copy = pltpu.make_async_copy(cost_hbm.at[0, s], cost_v, sem)
                copy.start()
                copy.wait()
                chunked(f_out[pl.ds(slots.row[s], 1), :], other8)
                chunked(l_ref[pl.ds(slots.col[s], 1), :], out8)
                for p in range(INNER):
                    lab_v[p] = label_piece(slots.row[s], p)

                @pl.loop(0, chunks * chunks)
                def _(ij):
                    i, j = ij // chunks, ij % chunks
                    here = pl.ds(pl.multiple_of(i * 128, 128), 128)
                    z = tile_z(cost_v, slots.scale[s], other8, i, j, False)
                    p = jnp.exp(z - out8[pl.ds(i, 1), :]).astype(BF16)
                    term = jnp.dot(lab_v[j], p, preferred_element_type=F32)
                    acc[slots.col[s], :, here] = acc[slots.col[s], :, here] + term

    core = slots.src % 2
    width = keep.shape[2]
    for c in range(acc.shape[0]):
        total = sums[c : c + 1, :]
        inv = jnp.where(total > 0, 1.0 / jnp.maximum(total, 1e-38), 0.0)
        for half in range(2):
            here = slice(half * width, (half + 1) * width)
            mean = acc[c, :, here] * inv[:, here]
            tail = jnp.broadcast_to(l_ref[c : c + 1, here], (8, width))

            @pl.when(core == half)
            def _():
                keep[c, :classes] = mean
                keep[c, classes:] = tail

            @pl.when(core != half)
            def _():
                send[c, :classes] = mean
                send[c, classes:] = tail


def merge_kernel(keep, got, *outs):
    src = lax.axis_index("src")
    classes = keep.shape[1] - 8
    for q, out in enumerate(outs):
        block = (src // 2) ^ q
        mine, other = keep[block], got[block]
        first, second = mine[classes : classes + 1], other[classes : classes + 1]
        both = lse([first, second])
        mean = mine[:classes] * jnp.exp(first - both) + other[:classes] * jnp.exp(second - both)
        out[:classes] = mean.astype(BF16)
        out[classes:] = split_rows(both)


def tail_row(piece):
    return jnp.sum(piece[piece.shape[0] - 16 :].astype(F32), axis=0, keepdims=True)


def combine_kernel(log_b, *rest):
    pieces, out = rest[:-1], rest[-1]
    src = lax.axis_index("src")
    classes, width = out.shape[0] - 16, out.shape[1]
    ls = [tail_row(p[...]) for p in pieces]
    total = lse(ls)
    mass = piece_of(log_b, src, width)
    top = total - mass
    out[:classes] = tree_sum([p[:classes].astype(F32) * jnp.exp(l - top) for p, l in zip(pieces, ls)]).astype(BF16)
    out[classes:] = split_rows(EPS * mass - EPS * total)


def assemble_kernel(order, *refs):
    pieces, (g_out, out, row) = refs[: len(order)], refs[len(order) :]
    src = lax.axis_index("src")
    classes, width = out.shape[0], pieces[0].shape[1]
    for k, piece in zip(order, pieces):
        here = pl.ds(pl.multiple_of((src ^ k) * width, width), width)
        out[:, here] = piece[:classes]
        row[:, here] = tail_row(piece[...])
    g_out[...] = row[...].reshape(g_out.shape)


VM = pl.BlockSpec(memory_space=pltpu.VMEM)
SM = pl.BlockSpec(memory_space=pltpu.SMEM)
HB = pl.BlockSpec(memory_space=pltpu.HBM)
PARAMS = pltpu.CompilerParams(vmem_limit_bytes=LIMIT)


def local(cost, cost_scale, slot_block_row, slot_block_column, device_block_count, log_a, log_b, labels):
    n_src, n_tgt = lax.axis_size("src"), lax.axis_size("tgt")
    slots, tile = cost.shape[1], cost.shape[2]
    rb, cb = log_a.shape[0] // tile, log_b.shape[0] // tile
    classes = labels.shape[1]
    dims = (rb, cb, slots)
    in_hbm = functools.partial(pltpu.with_memory_space_constraint, memory_space=pltpu.HBM)
    in_vmem = functools.partial(pltpu.with_memory_space_constraint, memory_space=pltpu.VMEM)
    in_smem = functools.partial(pltpu.with_memory_space_constraint, memory_space=pltpu.SMEM)

    def xor(x, axis, k):
        return lax.ppermute(x, axis, [(i, i ^ k) for i in range(lax.axis_size(axis))])

    def doubled(part, axis):
        k = 1
        while 2 * k < lax.axis_size(axis):
            part = lse([part, xor(part, axis, k)])
            k *= 2
        return [part, xor(part, axis, k)]

    outer = n_tgt // INNER
    along_z = [[x * INNER + z for z in range(INNER)] for x in range(outer)]
    along_x = [[x * INNER + z for x in range(outer)] for z in range(INNER)]

    def everyone(copies, axis, groups=None):
        return lax.all_to_all(copies, axis, 0, 0, axis_index_groups=groups, tiled=True)

    cost = in_hbm(cost)
    vec = functools.partial(jax.ShapeDtypeStruct, dtype=F32)
    chunks = pltpu.VMEM((tile // 128, 128), F32)
    work = [pltpu.SMEM((3,), F32), pltpu.VMEM((tile, tile), BF16), chunks, chunks, pltpu.SemaphoreType.DMA]
    rows, cols = pltpu.VMEM((rb, tile), F32), pltpu.VMEM((cb, tile), F32)

    k_all, row_l, ints, floats, log_a, log_b = pl.pallas_call(
        functools.partial(build_kernel, dims),
        out_shape=(
            pltpu.VMEM((slots, tile, tile), BF16),
            vec((INNER, rb, tile)),
            pltpu.SMEM((1, 2 * slots + 1), jnp.int32),
            pltpu.SMEM((1, slots + 2), F32),
            pltpu.VMEM((rb, tile), F32),
            pltpu.VMEM((cb, tile), F32),
        ),
        in_specs=[SM] * 4 + [VM] * 2 + [HB],
        out_specs=(VM, VM, SM, SM, VM, VM),
        scratch_shapes=[
            rows,
            pltpu.VMEM((slots, tile, tile), BF16),
            rows,
            cols,
            chunks,
            chunks,
            pltpu.SMEM((3,), F32),
            pltpu.SemaphoreType.DMA((slots, 2)),
        ],
        compiler_params=PARAMS,
    )(
        in_hbm(cost_scale),
        in_hbm(slot_block_row),
        in_hbm(slot_block_column),
        device_block_count,
        in_hbm(log_a),
        in_hbm(log_b),
        cost,
    )
    k_all, log_a, log_b = in_vmem(k_all), in_vmem(log_a), in_vmem(log_b)
    scalars = (in_smem(ints), in_smem(floats))
    common = [SM] * 2 + [VM, HB, VM]

    flat = pltpu.VMEM(FLAT, F32)
    sent = functools.partial(jax.ShapeDtypeStruct, dtype=BF16)
    lab_t, boxes = labels.T, []
    f_pot = g_pot = lab_z = None
    for step in range(ITERS):
        along = everyone(row_l, "tgt", along_z)
        if step == 0:
            part = lse([along[z] for z in range(INNER)])
            copies = jnp.broadcast_to(part[None], (outer,) + part.shape)
        else:
            lab_z = along if step == 1 else lab_z
            share = SHARE[step - 1]
            high = FLAT[0] + len(share) * (lab_z.shape[1] - FLAT[0])
            copies = pl.pallas_call(
                functools.partial(relay_kernel, share),
                out_shape=sent((outer, high, FLAT[1])),
                in_specs=[VM] * 2,
                out_specs=VM,
                compiler_params=PARAMS,
            )(along, lab_z)
        row_parts = everyone(copies, "tgt", along_x)
        if step:
            boxes.append(row_parts)
        if step == ITERS - 1:
            break
        first = step == 0
        col_l, f_pot = pl.pallas_call(
            functools.partial(col_kernel, slots, first),
            out_shape=(vec((n_src, cb, tile)) if first else sent((n_src,) + FLAT), vec((rb, tile))),
            in_specs=common + [VM] * (1 if first else 4),
            out_specs=(VM, VM),
            scratch_shapes=[cols, flat, cols] + work,
            compiler_params=PARAMS,
        )(*scalars, log_a, cost, k_all, row_parts, *(() if first else (f_pot, log_b, g_pot)))
        col_parts = everyone(col_l, "src")
        extra = FLAT[0] * lab_t.size // (FLAT[0] * FLAT[1]) if first else 0
        row_l, g_pot = pl.pallas_call(
            functools.partial(row_kernel, slots, first, first),
            out_shape=(sent((INNER, FLAT[0] + extra, FLAT[1])), vec((cb, tile))),
            in_specs=common + [VM] * 4,
            out_specs=(VM, VM),
            scratch_shapes=[rows, flat, rows] + work,
            compiler_params=PARAMS,
        )(*scalars, log_b, cost, k_all, col_parts, log_a, f_pot, lab_t if first else g_pot)

    width = cb * tile // n_src
    half = vec((cb, classes + 8, width))
    piece = jax.ShapeDtypeStruct((classes + 16, width), BF16)
    f_pot, keep, send = pl.pallas_call(
        functools.partial(label_kernel, slots),
        out_shape=(vec((rb, tile)), half, half),
        in_specs=common + [VM] * (1 + len(SHARE)),
        out_specs=(VM,) * 3,
        scratch_shapes=[
            pltpu.VMEM((cb, classes, tile), F32),
            cols,
            flat,
            pltpu.VMEM((INNER, classes, 128), BF16),
            cols,
        ] + work,
        compiler_params=PARAMS,
    )(*scalars, log_a, cost, k_all, f_pot, *boxes)
    n_y = n_src // 2
    pieces = pl.pallas_call(
        merge_kernel,
        out_shape=(piece,) * n_y,
        in_specs=[VM] * 2,
        out_specs=(VM,) * n_y,
        compiler_params=PARAMS,
    )(keep, xor(send, "src", 1))
    pieces = [pieces[0]] + [xor(pieces[q], "src", 2 * q) for q in range(1, n_y)]
    done = pl.pallas_call(
        combine_kernel,
        out_shape=piece,
        in_specs=[VM] * (1 + n_y),
        out_specs=VM,
        compiler_params=PARAMS,
    )(log_b, *pieces)
    pieces = [done] + [xor(done, "src", 2 * q) for q in range(1, n_y)]
    pieces = pieces + [xor(p, "src", 1) for p in pieces]
    order = tuple(2 * q for q in range(n_y)) + tuple(2 * q + 1 for q in range(n_y))
    g_pot, out = pl.pallas_call(
        functools.partial(assemble_kernel, order),
        out_shape=(vec((cb * tile,)), jax.ShapeDtypeStruct((classes, cb * tile), BF16)),
        in_specs=[VM] * n_src,
        out_specs=(VM, VM),
        scratch_shapes=[pltpu.VMEM((1, cb * tile), F32)],
        compiler_params=PARAMS,
    )(*pieces)
    return f_pot.reshape(-1), g_pot, out.T


def solution(mesh):
    in_specs = (
        P("src", "tgt", None, None),
        P("src", "tgt"),
        P("src", "tgt"),
        P("src", "tgt"),
        P("src", "tgt"),
        P("src"),
        P("tgt"),
        P(("src", "tgt"), None),
    )
    out_specs = (P("src"), P("tgt"), P("tgt", None))
    return jax.shard_map(local, mesh=mesh, in_specs=in_specs, out_specs=out_specs, check_vma=False)
```

```python
import functools

import jax
import jax.numpy as jnp
from jax import lax
from jax.experimental import pallas as pl
from jax.experimental.pallas import tpu as pltpu
from jax.sharding import PartitionSpec as P

ITERS = 4
EPS = 0.5
NEG = -1e30
LOG2E = 1.4426950408889634
TO2 = LOG2E / EPS
PART = 256
INNER = 8
FLAT = (16, 256)
LIMIT = 40 * 1024 * 1024
F32, BF16 = jnp.float32, jnp.bfloat16


def tree_sum(parts):
    while len(parts) > 1:
        parts = [a + b for a, b in zip(parts[0::2], parts[1::2])]
    return parts[0]


def lse(parts):
    top = functools.reduce(jnp.maximum, parts)
    return top + jnp.log(tree_sum([jnp.exp(p - top) for p in parts]))


class Slots:
    def __init__(self, ints, floats, total):
        self.total = total
        self.row = [ints[0, s] for s in range(total)]
        self.col = [ints[0, total + s] for s in range(total)]
        self.count = ints[0, 2 * total]
        self.live = [s < self.count for s in range(total)]
        self.scale = [floats[0, s] for s in range(total)]
        self.shift, self.high = floats[0, total], floats[0, total + 1]
        self.src, self.tgt = lax.axis_index("src"), lax.axis_index("tgt")


def split_rows(x):
    x = jnp.broadcast_to(x, (16, x.shape[1]))
    hi = x.astype(BF16).astype(F32)
    rest = x - hi
    mid = rest.astype(BF16).astype(F32)
    low = (rest - mid).astype(BF16).astype(F32)
    at = lax.broadcasted_iota(jnp.int32, x.shape, 0)
    zero = jnp.zeros_like(x)
    return jnp.where(at == 0, hi, jnp.where(at == 1, mid, jnp.where(at == 2, low, zero))).astype(BF16)


def k_row(lhs, k_block):
    return lax.dot_general(lhs, k_block, (((1,), (1,)), ((), ())), preferred_element_type=F32)


def k_col(lhs, k_block):
    return lax.dot_general(lhs, k_block, (((1,), (0,)), ((), ())), preferred_element_type=F32)


def chunked(row, out_ref):
    for c in range(out_ref.shape[0]):
        out_ref[c : c + 1, :] = row[:, c * 128 : (c + 1) * 128]


def tile_z(cost_v, scale, other8, out_chunk, red_chunk, rows_mode):
    mine = pl.ds(pl.multiple_of(out_chunk * 128, 128), 128)
    summed = pl.ds(pl.multiple_of(red_chunk * 128, 128), 128)
    other = jnp.broadcast_to(other8[pl.ds(red_chunk, 1), :], (128, 128)).T
    if rows_mode:
        tile = cost_v[mine, summed].astype(F32).T
    else:
        tile = cost_v[summed, mine].astype(F32)
    return (other - scale * tile) / EPS


def slow_lse(slots, cost_hbm, cost_v, sem, other8, out8, other_ref, l_ref, rows_mode, start=0):
    l_ref[...] = jnp.full(l_ref.shape, NEG, F32)
    chunks, out_chunks = other8.shape[0], out8.shape[0]
    for s in range(slots.total):
        out_at, other_at = (slots.row[s], slots.col[s]) if rows_mode else (slots.col[s], slots.row[s])

        @pl.when(slots.live[s])
        def _():
            copy = pltpu.make_async_copy(cost_hbm.at[0, s], cost_v, sem)
            copy.start()
            copy.wait()
            chunked(other_ref[pl.ds(other_at, 1), :], other8)

            @pl.loop(0, out_chunks)
            def _(i):
                def step(j, carry):
                    m, total = carry
                    z = tile_z(cost_v, slots.scale[s], other8, start + i, j, rows_mode)
                    top = jnp.maximum(m, jnp.max(z, axis=0, keepdims=True))
                    total = total * jnp.exp(m - top) + jnp.sum(jnp.exp(z - top), axis=0, keepdims=True)
                    return top, total

                first = (jnp.full((1, 128), NEG, F32), jnp.zeros((1, 128), F32))
                m, total = lax.fori_loop(0, chunks, step, first)
                out8[pl.ds(i, 1), :] = m + jnp.log(total)

            new = jnp.concatenate([out8[c : c + 1, :] for c in range(out_chunks)], axis=1)
            old = l_ref[pl.ds(out_at, 1), :]
            top = jnp.maximum(old, new)
            l_ref[pl.ds(out_at, 1), :] = top + jnp.log(jnp.exp(old - top) + jnp.exp(new - top))


def piece_of(ref, piece, width):
    per = ref.shape[1] // width
    row = ref[pl.ds(piece // per, 1), :]
    out = row[:, :width]
    for c in range(1, per):
        out = jnp.where(piece % per == c, row[:, c * width : (c + 1) * width], out)
    return out


def to_log(total, shift):
    return jnp.where(total > 0, jnp.log(jnp.maximum(total, 1e-38)) - shift / EPS, NEG)


def send_copies(l_ref, copies_ref):
    for k in range(copies_ref.shape[0]):
        copies_ref[k] = l_ref[...]


def send_relative(l_ref, pot, log_mass, flat, copies_ref):
    rel = jnp.exp(l_ref[...] + pot[...] / EPS - log_mass[...])
    count, width = rel.shape[0], flat.shape[1]
    for c in range(rel.shape[1] // width):
        flat[c * count : (c + 1) * count, :] = rel[:, c * width : (c + 1) * width]
    rel = flat[...].astype(BF16)
    for k in range(copies_ref.shape[0]):
        copies_ref[k, : flat.shape[0]] = rel


def new_potential(out, log_mass, parts, prev, flat):
    if prev is None:
        out[...] = EPS * log_mass[...] - EPS * lse([parts[k] for k in range(parts.shape[0])])
        return
    flat[...] = tree_sum([parts[k, : flat.shape[0]].astype(F32) for k in range(parts.shape[0])])
    count, width = out.shape[0], flat.shape[1]
    for c in range(out.shape[1] // width):
        here = slice(c * width, (c + 1) * width)
        out[:, here] = prev[:, here] - EPS * jnp.log(flat[c * count : (c + 1) * count, :])


def sums_fine(low, high, others):
    return (low >= 2.0**-80 * jnp.maximum(others, 1.0)) & (high <= 2.0**100)


def build_kernel(
    dims, count, scale_hbm, row_hbm, col_hbm, a_hbm, b_hbm, cost_hbm,
    k_ref, copies_ref, ints, floats, a_ref, b_ref,
    l_ref, cost_v, sums, zero, other8, out8, stat, sems,
    scale, row, col, log_a, log_b, small_sems, tall,
):
    rb, cb, total = dims
    small = [
        pltpu.make_async_copy(a, b, small_sems.at[i])
        for i, (a, b) in enumerate(
            ((scale_hbm, scale), (row_hbm, row), (col_hbm, col), (a_hbm, log_a), (b_hbm, log_b))
        )
    ]
    parts = cost_v.shape[1] // PART
    copies = [
        [
            pltpu.make_async_copy(
                cost_hbm.at[0, s, pl.ds(h * PART, PART)], cost_v.at[s, pl.ds(h * PART, PART)], sems.at[s, h]
            )
            for h in range(parts)
        ]
        for s in range(total)
    ]
    copies[0][0].start()
    for copy in small:
        copy.start()
    for s in range(total):

        @pl.when(s < count[0, 0])
        def _():
            for h in range(0 if s else 1, parts):
                copies[s][h].start()

    for copy in small[:3]:
        copy.wait()
    src, tgt = lax.axis_index("src"), lax.axis_index("tgt")
    for s in range(total):
        ints[0, s] = row[0, s] - src * rb
        ints[0, total + s] = col[0, s] - tgt * cb
        floats[0, s] = scale[0, s]
    ints[0, 2 * total] = count[0, 0]
    slots = Slots(ints, floats, total)
    chunk, tile = 32, cost_v.shape[2]

    def build(shift, wait):
        sums[...] = jnp.zeros(sums.shape, F32)
        floats[0, total] = jnp.float32(0.0) if shift is None else shift
        stat[1] = jnp.float32(0.0)
        stat[2] = jnp.float32(jnp.inf)
        for s in range(total):

            @pl.when(slots.live[s])
            def _():
                for h in range(parts):
                    if wait:
                        copies[s][h].wait()

                    @pl.loop(0, PART // chunk, unroll=2)
                    def _(i):
                        here = pl.ds(pl.multiple_of(h * PART + i * chunk, chunk), chunk)
                        x = cost_v[s, here, :].astype(F32) * (-TO2 * slots.scale[s])
                        if shift is not None:
                            x = x + shift * TO2
                        e = jnp.exp2(x)
                        k_ref[s, here, :] = e.astype(BF16)
                        tall[here, :] = tree_sum([e[:, c * 128 : (c + 1) * 128] for c in range(tile // 128)])

                wide = tall[...]
                hi = wide.astype(BF16)
                low = (wide - hi.astype(F32)).astype(BF16)
                ones = jnp.ones((16, 128), BF16)
                part = (k_row(ones, hi) + k_row(ones, low))[0:1]
                at = pl.ds(slots.row[s], 1)
                sums[at, :] = sums[at, :] + part
                stat[1] = jnp.maximum(stat[1], jnp.max(part))
                stat[2] = jnp.minimum(stat[2], jnp.min(part))

        l_ref[...] = to_log(sums[...], floats[0, total])
        floats[0, total + 1] = stat[1]
        return sums_fine(stat[2], stat[1], stat[1])

    fine = build(None, True)
    for copy in small[3:]:
        copy.wait()
    for r in range(rb):
        a_ref[r : r + 1, :] = log_a[r * tile : (r + 1) * tile].reshape(1, tile)
    for c in range(cb):
        b_ref[c : c + 1, :] = log_b[c * tile : (c + 1) * tile].reshape(1, tile)

    @pl.when(jnp.logical_not(fine))
    def _():
        stat[0] = jnp.float32(jnp.inf)
        for s in range(total):

            @pl.when(slots.live[s])
            def _():
                def lowest(i, low):
                    here = pl.ds(pl.multiple_of(i * chunk, chunk), chunk)
                    return jnp.minimum(low, jnp.min(cost_v[s, here, :].astype(F32)))

                low = lax.fori_loop(0, tile // chunk, lowest, jnp.float32(jnp.inf))
                stat[0] = jnp.minimum(stat[0], low * slots.scale[s])

        shifted = build(stat[0], False)

        @pl.when(jnp.logical_not(shifted))
        def _():
            zero[...] = jnp.zeros(zero.shape, F32)
            slow_lse(slots, cost_hbm, cost_v.at[0], sems.at[0, 0], other8, out8, zero, l_ref, True)

    send_copies(l_ref, copies_ref)


def row_kernel(total, first, ints, floats, log_b, cost_hbm, k_ref, parts, log_a, f, *rest):
    prev, lab = (None, rest[0]) if first else (rest[0], None)
    rest = rest[1:]
    copies_ref, g, l_ref, flat, sums, stat, cost_v, other8, out8, sem = rest
    slots = Slots(ints, floats, total)
    new_potential(g, log_b, parts, prev, flat)
    sums[...] = jnp.zeros(sums.shape, F32)
    stat[0] = jnp.float32(0.0)
    stat[1] = jnp.float32(jnp.inf)
    stat[2] = slots.high
    for s in range(slots.total):

        @pl.when(slots.live[s])
        def _():
            v = jnp.exp2(g[pl.ds(slots.col[s], 1), :] * TO2)
            part = jnp.sum(k_row(split_rows(v), k_ref[s]), axis=0, keepdims=True)
            at = pl.ds(slots.row[s], 1)
            sums[at, :] = sums[at, :] + part
            stat[0] = jnp.maximum(stat[0], jnp.max(part))
            stat[1] = jnp.minimum(stat[1], jnp.min(part))
            stat[2] = jnp.maximum(stat[2], jnp.max(v))

    l_ref[...] = to_log(sums[...], slots.shift)

    @pl.when(jnp.logical_not(sums_fine(stat[1], stat[0], stat[2])))
    def _():
        slow_lse(slots, cost_hbm, cost_v, sem, other8, out8, g, l_ref, True)

    send_relative(l_ref, f, log_a, flat, copies_ref)
    if first:
        half = lab.shape[0] // 2
        for k in range(copies_ref.shape[0]):
            copies_ref[k, flat.shape[0] :] = jnp.concatenate([lab[:half], lab[half:]], axis=1)


def relay_kernel(parts, out):
    rows, count = FLAT[0], parts.shape[0]
    total = tree_sum([parts[k, :rows].astype(F32) for k in range(count)]).astype(BF16)
    high = parts.shape[1] - rows
    for k in range(out.shape[0]):
        out[k, :rows] = total
        for p in range(count):
            out[k, rows + p * high : rows + (p + 1) * high] = parts[p, rows:]


def col_kernel(total, first, ints, floats, log_a, cost_hbm, k_ref, parts, *rest):
    (prev, log_b, g), rest = ((None, None, None), rest) if first else (rest[:3], rest[3:])
    copies_ref, f, l_ref, flat, sums, stat, cost_v, other8, out8, sem = rest
    slots = Slots(ints, floats, total)
    new_potential(f, log_a, parts, prev, flat)
    sums[...] = jnp.zeros(sums.shape, F32)
    stat[0] = jnp.float32(0.0)
    stat[1] = jnp.float32(jnp.inf)
    stat[2] = slots.high
    for s in range(slots.total):

        @pl.when(slots.live[s])
        def _():
            u = jnp.exp2(f[pl.ds(slots.row[s], 1), :] * TO2)
            part = jnp.sum(k_col(split_rows(u), k_ref[s]), axis=0, keepdims=True)
            at = pl.ds(slots.col[s], 1)
            sums[at, :] = sums[at, :] + part
            stat[0] = jnp.maximum(stat[0], jnp.max(part))
            stat[1] = jnp.minimum(stat[1], jnp.min(part))
            stat[2] = jnp.maximum(stat[2], jnp.max(u))

    l_ref[...] = to_log(sums[...], slots.shift)

    @pl.when(jnp.logical_not(sums_fine(stat[1], stat[0], stat[2])))
    def _():
        slow_lse(slots, cost_hbm, cost_v, sem, other8, out8, f, l_ref, False)

    if first:
        send_copies(l_ref, copies_ref)
    else:
        send_relative(l_ref, g, log_b, flat, copies_ref)


def label_kernel(total, own, ints, floats, log_a, cost_hbm, k_ref, prev, parts, box, *rest):
    (f_out,), rest = (rest[:1], rest[1:]) if own else ((None,), rest)
    out, f, row, acc, l_ref, flat, lab_v, sums, stat, cost_v, other8, out8, sem = rest
    slots = Slots(ints, floats, total)
    classes, width = acc.shape[1], acc.shape[2]
    new_potential(f, log_a, parts, prev, flat)
    sums[...] = jnp.zeros(sums.shape, F32)
    acc[...] = jnp.zeros(acc.shape, F32)
    stat[0] = jnp.float32(0.0)
    stat[1] = jnp.float32(jnp.inf)
    stat[2] = slots.high
    high = classes // 2
    core = slots.src % 2
    half = core if own else 1 - core
    lanes = pl.ds(pl.multiple_of(half * width, width), width)

    def label_piece(block, p):
        at = FLAT[0] + p * high
        both = box[block, at : at + high]
        return jnp.concatenate([both[:, :128], both[:, 128:]], axis=0)

    for s in range(slots.total):

        @pl.when(slots.live[s])
        def _():
            u = jnp.exp2(f[pl.ds(slots.row[s], 1), :] * TO2)
            lab = jnp.concatenate([label_piece(slots.row[s], p) for p in range(INNER)], axis=1)
            weighted = lab.astype(F32) * u
            hi = weighted.astype(BF16)
            low = (weighted - hi.astype(F32)).astype(BF16)
            res = k_col(jnp.concatenate([hi, low, split_rows(u)], axis=0), k_ref[s, :, lanes])
            part = jnp.sum(res[2 * classes :], axis=0, keepdims=True)
            at = pl.ds(slots.col[s], 1)
            sums[at, :] = sums[at, :] + part
            acc[slots.col[s]] = acc[slots.col[s]] + (res[:classes] + res[classes : 2 * classes])
            stat[0] = jnp.maximum(stat[0], jnp.max(part))
            stat[1] = jnp.minimum(stat[1], jnp.min(part))
            stat[2] = jnp.maximum(stat[2], jnp.max(u))

    l_ref[...] = to_log(sums[...], slots.shift)

    @pl.when(jnp.logical_not(sums_fine(stat[1], stat[0], stat[2])))
    def _():
        chunks = width // 128
        slow_lse(slots, cost_hbm, cost_v, sem, other8, out8, f, l_ref, False, half * chunks)
        acc[...] = jnp.zeros(acc.shape, F32)
        sums[...] = jnp.ones(sums.shape, F32)
        for s in range(slots.total):

            @pl.when(slots.live[s])
            def _():
                copy = pltpu.make_async_copy(cost_hbm.at[0, s], cost_v, sem)
                copy.start()
                copy.wait()
                chunked(f[pl.ds(slots.row[s], 1), :], other8)
                chunked(l_ref[pl.ds(slots.col[s], 1), :], out8)
                for p in range(INNER):
                    lab_v[p] = label_piece(slots.row[s], p)

                @pl.loop(0, chunks * INNER)
                def _(ij):
                    i, j = ij // INNER, ij % INNER
                    here = pl.ds(pl.multiple_of(i * 128, 128), 128)
                    z = tile_z(cost_v, slots.scale[s], other8, half * chunks + i, j, False)
                    p = jnp.exp(z - out8[pl.ds(i, 1), :]).astype(BF16)
                    term = jnp.dot(lab_v[j], p, preferred_element_type=F32)
                    acc[slots.col[s], :, here] = acc[slots.col[s], :, here] + term

    for c in range(acc.shape[0]):
        mass = sums[c : c + 1, :]
        out[c, :classes] = acc[c] * jnp.where(mass > 0, 1.0 / jnp.maximum(mass, 1e-38), 0.0)
        out[c, classes:] = jnp.broadcast_to(l_ref[c : c + 1, :], (8, width))
    if own:
        for r in range(f.shape[0]):
            row[:, r * f.shape[1] : (r + 1) * f.shape[1]] = f[r : r + 1, :]
        f_out[...] = row[...].reshape(f_out.shape)


def merge_kernel(keep, got, *outs):
    src = lax.axis_index("src")
    classes = keep.shape[1] - 8
    for q, out in enumerate(outs):
        block = (src // 2) ^ q
        mine, other = keep[block], got[block]
        first, second = mine[classes : classes + 1], other[classes : classes + 1]
        both = lse([first, second])
        mean = mine[:classes] * jnp.exp(first - both) + other[:classes] * jnp.exp(second - both)
        out[:classes] = mean.astype(BF16)
        out[classes:] = split_rows(both)


def tail_row(piece):
    return jnp.sum(piece[piece.shape[0] - 16 :].astype(F32), axis=0, keepdims=True)


def combine_kernel(log_b, *rest):
    pieces, out = rest[:-1], rest[-1]
    src = lax.axis_index("src")
    classes, width = out.shape[0] - 16, out.shape[1]
    ls = [tail_row(p[...]) for p in pieces]
    total = lse(ls)
    mass = piece_of(log_b, src, width)
    top = total - mass
    out[:classes] = tree_sum([p[:classes].astype(F32) * jnp.exp(l - top) for p, l in zip(pieces, ls)]).astype(BF16)
    out[classes:] = split_rows(EPS * mass - EPS * total)


def assemble_kernel(order, *refs):
    pieces, (g_out, out, row) = refs[: len(order)], refs[len(order) :]
    src = lax.axis_index("src")
    classes, width = out.shape[0], pieces[0].shape[1]
    for k, piece in zip(order, pieces):
        here = pl.ds(pl.multiple_of((src ^ k) * width, width), width)
        out[:, here] = piece[:classes]
        row[:, here] = tail_row(piece[...])
    g_out[...] = row[...].reshape(g_out.shape)


VM = pl.BlockSpec(memory_space=pltpu.VMEM)
SM = pl.BlockSpec(memory_space=pltpu.SMEM)
HB = pl.BlockSpec(memory_space=pltpu.HBM)
PARAMS = pltpu.CompilerParams(vmem_limit_bytes=LIMIT)


def local(cost, cost_scale, slot_block_row, slot_block_column, device_block_count, log_a, log_b, labels):
    n_src, n_tgt = lax.axis_size("src"), lax.axis_size("tgt")
    slots, tile = cost.shape[1], cost.shape[2]
    rb, cb = log_a.shape[0] // tile, log_b.shape[0] // tile
    classes = labels.shape[1]
    dims = (rb, cb, slots)
    in_hbm = functools.partial(pltpu.with_memory_space_constraint, memory_space=pltpu.HBM)
    in_vmem = functools.partial(pltpu.with_memory_space_constraint, memory_space=pltpu.VMEM)
    in_smem = functools.partial(pltpu.with_memory_space_constraint, memory_space=pltpu.SMEM)

    def xor(x, axis, k):
        return lax.ppermute(x, axis, [(i, i ^ k) for i in range(lax.axis_size(axis))])

    def doubled(part, axis):
        k = 1
        while 2 * k < lax.axis_size(axis):
            part = lse([part, xor(part, axis, k)])
            k *= 2
        return [part, xor(part, axis, k)]

    outer = n_tgt // INNER
    along_z = [[x * INNER + z for z in range(INNER)] for x in range(outer)]
    along_x = [[x * INNER + z for x in range(outer)] for z in range(INNER)]

    def everyone(copies, axis, groups=None):
        return lax.all_to_all(copies, axis, 0, 0, axis_index_groups=groups, tiled=True)

    cost = in_hbm(cost)
    vec = functools.partial(jax.ShapeDtypeStruct, dtype=F32)
    chunks = pltpu.VMEM((tile // 128, 128), F32)
    work = [pltpu.SMEM((3,), F32), pltpu.VMEM((tile, tile), BF16), chunks, chunks, pltpu.SemaphoreType.DMA]
    rows, cols = pltpu.VMEM((rb, tile), F32), pltpu.VMEM((cb, tile), F32)

    k_all, row_l, ints, floats, log_a, log_b = pl.pallas_call(
        functools.partial(build_kernel, dims),
        out_shape=(
            pltpu.VMEM((slots, tile, tile), BF16),
            vec((INNER, rb, tile)),
            pltpu.SMEM((1, 2 * slots + 1), jnp.int32),
            pltpu.SMEM((1, slots + 2), F32),
            pltpu.VMEM((rb, tile), F32),
            pltpu.VMEM((cb, tile), F32),
        ),
        in_specs=[SM] + [HB] * 6,
        out_specs=(VM, VM, SM, SM, VM, VM),
        scratch_shapes=[
            rows,
            pltpu.VMEM((slots, tile, tile), BF16),
            rows,
            cols,
            chunks,
            chunks,
            pltpu.SMEM((3,), F32),
            pltpu.SemaphoreType.DMA((slots, tile // PART)),
            pltpu.SMEM((1, slots), F32),
            pltpu.SMEM((1, slots), jnp.int32),
            pltpu.SMEM((1, slots), jnp.int32),
            pltpu.VMEM((rb * tile,), F32),
            pltpu.VMEM((cb * tile,), F32),
            pltpu.SemaphoreType.DMA((5,)),
            pltpu.VMEM((tile, 128), F32),
        ],
        compiler_params=PARAMS,
    )(
        device_block_count,
        in_hbm(cost_scale),
        in_hbm(slot_block_row),
        in_hbm(slot_block_column),
        in_hbm(log_a),
        in_hbm(log_b),
        cost,
    )
    k_all, log_a, log_b = in_vmem(k_all), in_vmem(log_a), in_vmem(log_b)
    scalars = (in_smem(ints), in_smem(floats))
    common = [SM] * 2 + [VM, HB, VM]

    flat = pltpu.VMEM(FLAT, F32)
    sent = functools.partial(jax.ShapeDtypeStruct, dtype=BF16)
    lab_t = labels.T
    f_pot = g_pot = box = None
    for step in range(ITERS):
        if step < 2:
            along = everyone(row_l, "tgt", along_z)
            if step == 0:
                part = lse([along[z] for z in range(INNER)])
                copies = jnp.broadcast_to(part[None], (outer,) + part.shape)
            else:
                high = FLAT[0] + INNER * (along.shape[1] - FLAT[0])
                copies = pl.pallas_call(
                    relay_kernel,
                    out_shape=sent((outer, high, FLAT[1])),
                    in_specs=[VM],
                    out_specs=VM,
                    compiler_params=PARAMS,
                )(along)
            row_parts = everyone(copies, "tgt", along_x)
            box = row_parts if step else None
        else:
            row_parts = everyone(row_l, "tgt")
        if step == ITERS - 1:
            break
        first = step == 0
        col_l, f_pot = pl.pallas_call(
            functools.partial(col_kernel, slots, first),
            out_shape=(vec((n_src, cb, tile)) if first else sent((n_src,) + FLAT), vec((rb, tile))),
            in_specs=common + [VM] * (1 if first else 4),
            out_specs=(VM, VM),
            scratch_shapes=[cols, flat, cols] + work,
            compiler_params=PARAMS,
        )(*scalars, log_a, cost, k_all, row_parts, *(() if first else (f_pot, log_b, g_pot)))
        col_parts = everyone(col_l, "src")
        extra = FLAT[0] * lab_t.size // (FLAT[0] * FLAT[1]) if first else 0
        last = step == ITERS - 2
        row_l, *g_out = pl.pallas_call(
            functools.partial(row_kernel, slots, first),
            out_shape=(sent((INNER if first else n_tgt, FLAT[0] + extra, FLAT[1])), vec((cb, tile)))[: 1 if last else 2],
            in_specs=common + [VM] * 4,
            out_specs=(VM, VM)[: 1 if last else 2],
            scratch_shapes=[cols] * last + [rows, flat, rows] + work,
            compiler_params=PARAMS,
        )(*scalars, log_b, cost, k_all, col_parts, log_a, f_pot, lab_t if first else g_pot)
        g_pot = g_out[0] if g_out else None

    width = cb * tile // n_src
    piece = jax.ShapeDtypeStruct((classes + 16, width), BF16)
    half = vec((cb, classes + 8, width))
    half_cols = pltpu.VMEM((cb, width), F32)

    def label_call(own):
        return pl.pallas_call(
            functools.partial(label_kernel, slots, own),
            out_shape=((vec((rb * tile,)),) if own else ()) + (half,),
            in_specs=common + [VM] * 3,
            out_specs=(VM,) * (1 + own),
            scratch_shapes=[
                rows,
                pltpu.VMEM((1, rb * tile), F32),
                pltpu.VMEM((cb, classes, width), F32),
                half_cols,
                flat,
                pltpu.VMEM((INNER, classes, 128), BF16),
                half_cols,
            ]
            + work[:3]
            + [pltpu.VMEM((width // 128, 128), F32), work[4]],
            cost_estimate=pl.CostEstimate(
                flops=slots * tile * tile * 150, bytes_accessed=slots * tile * tile, transcendentals=slots * tile
            ),
            compiler_params=PARAMS,
        )(*scalars, log_a, cost, k_all, f_pot, row_parts, box)

    got = xor(label_call(False)[0], "src", 1)
    f_pot, keep = label_call(True)
    n_y = n_src // 2
    pieces = pl.pallas_call(
        merge_kernel,
        out_shape=(piece,) * n_y,
        in_specs=[VM] * 2,
        out_specs=(VM,) * n_y,
        compiler_params=PARAMS,
    )(keep, got)
    pieces = [pieces[0]] + [xor(pieces[q], "src", 2 * q) for q in range(1, n_y)]
    done = pl.pallas_call(
        combine_kernel,
        out_shape=piece,
        in_specs=[VM] * (1 + n_y),
        out_specs=VM,
        compiler_params=PARAMS,
    )(log_b, *pieces)
    pieces = [done] + [xor(done, "src", 2 * q) for q in range(1, n_y)]
    pieces = pieces + [xor(p, "src", 1) for p in pieces]
    order = tuple(2 * q for q in range(n_y)) + tuple(2 * q + 1 for q in range(n_y))
    g_pot, out = pl.pallas_call(
        functools.partial(assemble_kernel, order),
        out_shape=(vec((cb * tile,)), jax.ShapeDtypeStruct((classes, cb * tile), BF16)),
        in_specs=[VM] * n_src,
        out_specs=(VM, VM),
        scratch_shapes=[pltpu.VMEM((1, cb * tile), F32)],
        compiler_params=PARAMS,
    )(*pieces)
    return f_pot, g_pot, out.T


def solution(mesh):
    in_specs = (
        P("src", "tgt", None, None),
        P("src", "tgt"),
        P("src", "tgt"),
        P("src", "tgt"),
        P("src", "tgt"),
        P("src"),
        P("tgt"),
        P(("src", "tgt"), None),
    )
    out_specs = (P("src"), P("tgt"), P("tgt", None))
    return jax.shard_map(local, mesh=mesh, in_specs=in_specs, out_specs=out_specs, check_vma=False)
```

```python
import functools

import jax
import jax.numpy as jnp
from jax import lax
from jax.experimental import pallas as pl
from jax.experimental.pallas import tpu as pltpu
from jax.sharding import PartitionSpec as P

ITERS = 4
EPS = 0.5
NEG = -1e30
LOG2E = 1.4426950408889634
TO2 = LOG2E / EPS
PART = 256
INNER = 8
FLAT = (16, 256)
LIMIT = 40 * 1024 * 1024
F32, BF16 = jnp.float32, jnp.bfloat16


def tree_sum(parts):
    while len(parts) > 1:
        parts = [a + b for a, b in zip(parts[0::2], parts[1::2])]
    return parts[0]


def lse(parts):
    top = functools.reduce(jnp.maximum, parts)
    return top + jnp.log(tree_sum([jnp.exp(p - top) for p in parts]))


class Slots:
    def __init__(self, ints, floats, total):
        self.total = total
        self.row = [ints[0, s] for s in range(total)]
        self.col = [ints[0, total + s] for s in range(total)]
        self.count = ints[0, 2 * total]
        self.live = [s < self.count for s in range(total)]
        self.scale = [floats[0, s] for s in range(total)]
        self.shift, self.high = floats[0, total], floats[0, total + 1]
        self.src, self.tgt = lax.axis_index("src"), lax.axis_index("tgt")


def split_rows(x):
    x = jnp.broadcast_to(x, (16, x.shape[1]))
    hi = x.astype(BF16).astype(F32)
    rest = x - hi
    mid = rest.astype(BF16).astype(F32)
    low = (rest - mid).astype(BF16).astype(F32)
    at = lax.broadcasted_iota(jnp.int32, x.shape, 0)
    zero = jnp.zeros_like(x)
    return jnp.where(at == 0, hi, jnp.where(at == 1, mid, jnp.where(at == 2, low, zero))).astype(BF16)


def k_row(lhs, k_block):
    return lax.dot_general(lhs, k_block, (((1,), (1,)), ((), ())), preferred_element_type=F32)


def fold_lanes(x):
    return tree_sum([x[:, c * 128 : (c + 1) * 128] for c in range(x.shape[1] // 128)])


def fold_rows(tall):
    wide = tall[...]
    hi = wide.astype(BF16)
    low = (wide - hi.astype(F32)).astype(BF16)
    ones = jnp.ones((16, 128), BF16)
    return (k_row(ones, hi) + k_row(ones, low))[0:1]


def k_col(lhs, k_block):
    return lax.dot_general(lhs, k_block, (((1,), (0,)), ((), ())), preferred_element_type=F32)


def chunked(row, out_ref):
    for c in range(out_ref.shape[0]):
        out_ref[c : c + 1, :] = row[:, c * 128 : (c + 1) * 128]


def tile_z(cost_v, scale, other8, out_chunk, red_chunk, rows_mode):
    mine = pl.ds(pl.multiple_of(out_chunk * 128, 128), 128)
    summed = pl.ds(pl.multiple_of(red_chunk * 128, 128), 128)
    other = jnp.broadcast_to(other8[pl.ds(red_chunk, 1), :], (128, 128)).T
    if rows_mode:
        tile = cost_v[mine, summed].astype(F32).T
    else:
        tile = cost_v[summed, mine].astype(F32)
    return (other - scale * tile) / EPS


def slow_lse(slots, cost_hbm, cost_v, sem, other8, out8, other_ref, l_ref, rows_mode, start=0):
    l_ref[...] = jnp.full(l_ref.shape, NEG, F32)
    chunks, out_chunks = other8.shape[0], out8.shape[0]
    for s in range(slots.total):
        out_at, other_at = (slots.row[s], slots.col[s]) if rows_mode else (slots.col[s], slots.row[s])

        @pl.when(slots.live[s])
        def _():
            copy = pltpu.make_async_copy(cost_hbm.at[0, s], cost_v, sem)
            copy.start()
            copy.wait()
            chunked(other_ref[pl.ds(other_at, 1), :], other8)

            @pl.loop(0, out_chunks)
            def _(i):
                def step(j, carry):
                    m, total = carry
                    z = tile_z(cost_v, slots.scale[s], other8, start + i, j, rows_mode)
                    top = jnp.maximum(m, jnp.max(z, axis=0, keepdims=True))
                    total = total * jnp.exp(m - top) + jnp.sum(jnp.exp(z - top), axis=0, keepdims=True)
                    return top, total

                first = (jnp.full((1, 128), NEG, F32), jnp.zeros((1, 128), F32))
                m, total = lax.fori_loop(0, chunks, step, first)
                out8[pl.ds(i, 1), :] = m + jnp.log(total)

            new = jnp.concatenate([out8[c : c + 1, :] for c in range(out_chunks)], axis=1)
            old = l_ref[pl.ds(out_at, 1), :]
            top = jnp.maximum(old, new)
            l_ref[pl.ds(out_at, 1), :] = top + jnp.log(jnp.exp(old - top) + jnp.exp(new - top))


def piece_of(ref, piece, width):
    per = ref.shape[1] // width
    row = ref[pl.ds(piece // per, 1), :]
    out = row[:, :width]
    for c in range(1, per):
        out = jnp.where(piece % per == c, row[:, c * width : (c + 1) * width], out)
    return out


def to_log(total, shift):
    return jnp.where(total > 0, jnp.log(jnp.maximum(total, 1e-38)) - shift / EPS, NEG)


def send_copies(l_ref, copies_ref):
    for k in range(copies_ref.shape[0]):
        copies_ref[k] = l_ref[...]


def send_relative(l_ref, pot, log_mass, flat, copies_ref):
    rel = jnp.exp(l_ref[...] + pot[...] / EPS - log_mass[...])
    count, width = rel.shape[0], flat.shape[1]
    for c in range(rel.shape[1] // width):
        flat[c * count : (c + 1) * count, :] = rel[:, c * width : (c + 1) * width]
    rel = flat[...].astype(BF16)
    for k in range(copies_ref.shape[0]):
        copies_ref[k, : flat.shape[0]] = rel


def new_potential(out, log_mass, parts, prev, flat):
    if prev is None:
        out[...] = EPS * log_mass[...] - EPS * lse([parts[k] for k in range(parts.shape[0])])
        return
    flat[...] = tree_sum([parts[k, : flat.shape[0]].astype(F32) for k in range(parts.shape[0])])
    count, width = out.shape[0], flat.shape[1]
    for c in range(out.shape[1] // width):
        here = slice(c * width, (c + 1) * width)
        out[:, here] = prev[:, here] - EPS * jnp.log(flat[c * count : (c + 1) * count, :])


def sums_fine(low, high, others):
    return (low >= 2.0**-80 * jnp.maximum(others, 1.0)) & (high <= 2.0**100)


def build_kernel(
    dims, count, scale_hbm, row_hbm, col_hbm, a_hbm, b_hbm, cost_hbm,
    k_ref, copies_ref, ints, floats, a_ref, b_ref,
    l_ref, cost_v, sums, zero, other8, out8, stat, sems,
    scale, row, col, log_a, log_b, small_sems, tall,
):
    rb, cb, total = dims
    small = [
        pltpu.make_async_copy(a, b, small_sems.at[i])
        for i, (a, b) in enumerate(
            ((scale_hbm, scale), (row_hbm, row), (col_hbm, col), (a_hbm, log_a), (b_hbm, log_b))
        )
    ]
    parts = cost_v.shape[1] // PART
    copies = [
        [
            pltpu.make_async_copy(
                cost_hbm.at[0, s, pl.ds(h * PART, PART)], cost_v.at[s, pl.ds(h * PART, PART)], sems.at[s, h]
            )
            for h in range(parts)
        ]
        for s in range(total)
    ]
    copies[0][0].start()
    for copy in small:
        copy.start()
    for s in range(total):

        @pl.when(s < count[0, 0])
        def _():
            for h in range(0 if s else 1, parts):
                copies[s][h].start()

    for copy in small[:3]:
        copy.wait()
    src, tgt = lax.axis_index("src"), lax.axis_index("tgt")
    for s in range(total):
        ints[0, s] = row[0, s] - src * rb
        ints[0, total + s] = col[0, s] - tgt * cb
        floats[0, s] = scale[0, s]
    ints[0, 2 * total] = count[0, 0]
    slots = Slots(ints, floats, total)
    chunk, tile = 32, cost_v.shape[2]

    def build(shift, wait):
        sums[...] = jnp.zeros(sums.shape, F32)
        floats[0, total] = jnp.float32(0.0) if shift is None else shift
        stat[1] = jnp.float32(0.0)
        stat[2] = jnp.float32(jnp.inf)
        for s in range(total):

            @pl.when(slots.live[s])
            def _():
                for h in range(parts):
                    if wait:
                        copies[s][h].wait()

                    @pl.loop(0, PART // chunk, unroll=2)
                    def _(i):
                        here = pl.ds(pl.multiple_of(h * PART + i * chunk, chunk), chunk)
                        x = cost_v[s, here, :].astype(F32) * (-TO2 * slots.scale[s])
                        if shift is not None:
                            x = x + shift * TO2
                        e = jnp.exp2(x)
                        k_ref[s, here, :] = e.astype(BF16)
                        tall[here, :] = fold_lanes(e)

                part = fold_rows(tall)
                at = pl.ds(slots.row[s], 1)
                sums[at, :] = sums[at, :] + part
                stat[1] = jnp.maximum(stat[1], jnp.max(part))
                stat[2] = jnp.minimum(stat[2], jnp.min(part))

        l_ref[...] = to_log(sums[...], floats[0, total])
        floats[0, total + 1] = stat[1]
        return sums_fine(stat[2], stat[1], stat[1])

    fine = build(None, True)
    for copy in small[3:]:
        copy.wait()
    for r in range(rb):
        a_ref[r : r + 1, :] = log_a[r * tile : (r + 1) * tile].reshape(1, tile)
    for c in range(cb):
        b_ref[c : c + 1, :] = log_b[c * tile : (c + 1) * tile].reshape(1, tile)

    @pl.when(jnp.logical_not(fine))
    def _():
        stat[0] = jnp.float32(jnp.inf)
        for s in range(total):

            @pl.when(slots.live[s])
            def _():
                def lowest(i, low):
                    here = pl.ds(pl.multiple_of(i * chunk, chunk), chunk)
                    return jnp.minimum(low, jnp.min(cost_v[s, here, :].astype(F32)))

                low = lax.fori_loop(0, tile // chunk, lowest, jnp.float32(jnp.inf))
                stat[0] = jnp.minimum(stat[0], low * slots.scale[s])

        shifted = build(stat[0], False)

        @pl.when(jnp.logical_not(shifted))
        def _():
            zero[...] = jnp.zeros(zero.shape, F32)
            slow_lse(slots, cost_hbm, cost_v.at[0], sems.at[0, 0], other8, out8, zero, l_ref, True)

    send_copies(l_ref, copies_ref)


def row_kernel(total, first, ints, floats, log_b, cost_hbm, k_ref, parts, log_a, f, *rest):
    prev, lab = (None, rest[0]) if first else (rest[0], None)
    rest = rest[1:]
    copies_ref, g, l_ref, flat, tall, sums, stat, cost_v, other8, out8, sem = rest
    slots = Slots(ints, floats, total)
    new_potential(g, log_b, parts, prev, flat)
    sums[...] = jnp.zeros(sums.shape, F32)
    stat[0] = jnp.float32(0.0)
    stat[1] = jnp.float32(jnp.inf)
    stat[2] = slots.high
    for s in range(slots.total):

        @pl.when(slots.live[s])
        def _():
            v = jnp.exp2(g[pl.ds(slots.col[s], 1), :] * TO2)

            @pl.loop(0, tall.shape[0] // 32, unroll=2)
            def _(i):
                here = pl.ds(pl.multiple_of(i * 32, 32), 32)
                tall[here, :] = fold_lanes(k_ref[s, here, :].astype(F32) * v)

            part = fold_rows(tall)
            at = pl.ds(slots.row[s], 1)
            sums[at, :] = sums[at, :] + part
            stat[0] = jnp.maximum(stat[0], jnp.max(part))
            stat[1] = jnp.minimum(stat[1], jnp.min(part))
            stat[2] = jnp.maximum(stat[2], jnp.max(v))

    l_ref[...] = to_log(sums[...], slots.shift)

    @pl.when(jnp.logical_not(sums_fine(stat[1], stat[0], stat[2])))
    def _():
        slow_lse(slots, cost_hbm, cost_v, sem, other8, out8, g, l_ref, True)

    send_relative(l_ref, f, log_a, flat, copies_ref)
    if first:
        half = lab.shape[0] // 2
        for k in range(copies_ref.shape[0]):
            copies_ref[k, flat.shape[0] :] = jnp.concatenate([lab[:half], lab[half:]], axis=1)


def relay_kernel(parts, out):
    rows, count = FLAT[0], parts.shape[0]
    total = tree_sum([parts[k, :rows].astype(F32) for k in range(count)]).astype(BF16)
    high = parts.shape[1] - rows
    for k in range(out.shape[0]):
        out[k, :rows] = total
        for p in range(count):
            out[k, rows + p * high : rows + (p + 1) * high] = parts[p, rows:]


def col_kernel(total, first, ints, floats, log_a, cost_hbm, k_ref, parts, *rest):
    (prev, log_b, g), rest = ((None, None, None), rest) if first else (rest[:3], rest[3:])
    copies_ref, f, l_ref, flat, sums, stat, cost_v, other8, out8, sem = rest
    slots = Slots(ints, floats, total)
    new_potential(f, log_a, parts, prev, flat)
    sums[...] = jnp.zeros(sums.shape, F32)
    stat[0] = jnp.float32(0.0)
    stat[1] = jnp.float32(jnp.inf)
    stat[2] = slots.high
    for s in range(slots.total):

        @pl.when(slots.live[s])
        def _():
            u = jnp.exp2(f[pl.ds(slots.row[s], 1), :] * TO2)
            part = jnp.sum(k_col(split_rows(u), k_ref[s]), axis=0, keepdims=True)
            at = pl.ds(slots.col[s], 1)
            sums[at, :] = sums[at, :] + part
            stat[0] = jnp.maximum(stat[0], jnp.max(part))
            stat[1] = jnp.minimum(stat[1], jnp.min(part))
            stat[2] = jnp.maximum(stat[2], jnp.max(u))

    l_ref[...] = to_log(sums[...], slots.shift)

    @pl.when(jnp.logical_not(sums_fine(stat[1], stat[0], stat[2])))
    def _():
        slow_lse(slots, cost_hbm, cost_v, sem, other8, out8, f, l_ref, False)

    if first:
        send_copies(l_ref, copies_ref)
    else:
        send_relative(l_ref, g, log_b, flat, copies_ref)


def label_kernel(total, own, ints, floats, log_a, cost_hbm, k_ref, prev, parts, box, *rest):
    (f, out), rest = (rest[:2] if own else rest[1::-1]), rest[2:]
    acc, l_ref, flat, lab_v, sums, stat, cost_v, other8, out8, sem = rest
    slots = Slots(ints, floats, total)
    classes, width = acc.shape[1], acc.shape[2]
    new_potential(f, log_a, parts, prev, flat)
    sums[...] = jnp.zeros(sums.shape, F32)
    acc[...] = jnp.zeros(acc.shape, F32)
    stat[0] = jnp.float32(0.0)
    stat[1] = jnp.float32(jnp.inf)
    stat[2] = slots.high
    high = classes // 2
    core = slots.src % 2
    half = core if own else 1 - core
    lanes = pl.ds(pl.multiple_of(half * width, width), width)

    def label_piece(block, p):
        at = FLAT[0] + p * high
        both = box[block, at : at + high]
        return jnp.concatenate([both[:, :128], both[:, 128:]], axis=0)

    for s in range(slots.total):

        @pl.when(slots.live[s])
        def _():
            u = jnp.exp2(f[pl.ds(slots.row[s], 1), :] * TO2)
            lab = jnp.concatenate([label_piece(slots.row[s], p) for p in range(INNER)], axis=1)
            weighted = lab.astype(F32) * u
            hi = weighted.astype(BF16)
            low = (weighted - hi.astype(F32)).astype(BF16)
            res = k_col(jnp.concatenate([hi, low, split_rows(u)], axis=0), k_ref[s, :, lanes])
            part = jnp.sum(res[2 * classes :], axis=0, keepdims=True)
            at = pl.ds(slots.col[s], 1)
            sums[at, :] = sums[at, :] + part
            acc[slots.col[s]] = acc[slots.col[s]] + (res[:classes] + res[classes : 2 * classes])
            stat[0] = jnp.maximum(stat[0], jnp.max(part))
            stat[1] = jnp.minimum(stat[1], jnp.min(part))
            stat[2] = jnp.maximum(stat[2], jnp.max(u))

    l_ref[...] = to_log(sums[...], slots.shift)

    @pl.when(jnp.logical_not(sums_fine(stat[1], stat[0], stat[2])))
    def _():
        chunks = width // 128
        slow_lse(slots, cost_hbm, cost_v, sem, other8, out8, f, l_ref, False, half * chunks)
        acc[...] = jnp.zeros(acc.shape, F32)
        sums[...] = jnp.ones(sums.shape, F32)
        for s in range(slots.total):

            @pl.when(slots.live[s])
            def _():
                copy = pltpu.make_async_copy(cost_hbm.at[0, s], cost_v, sem)
                copy.start()
                copy.wait()
                chunked(f[pl.ds(slots.row[s], 1), :], other8)
                chunked(l_ref[pl.ds(slots.col[s], 1), :], out8)
                for p in range(INNER):
                    lab_v[p] = label_piece(slots.row[s], p)

                @pl.loop(0, chunks * INNER)
                def _(ij):
                    i, j = ij // INNER, ij % INNER
                    here = pl.ds(pl.multiple_of(i * 128, 128), 128)
                    z = tile_z(cost_v, slots.scale[s], other8, half * chunks + i, j, False)
                    p = jnp.exp(z - out8[pl.ds(i, 1), :]).astype(BF16)
                    term = jnp.dot(lab_v[j], p, preferred_element_type=F32)
                    acc[slots.col[s], :, here] = acc[slots.col[s], :, here] + term

    for c in range(acc.shape[0]):
        mass = sums[c : c + 1, :]
        out[c, :classes] = acc[c] * jnp.where(mass > 0, 1.0 / jnp.maximum(mass, 1e-38), 0.0)
        out[c, classes:] = jnp.broadcast_to(l_ref[c : c + 1, :], (8, width))


def merge_kernel(keep, got, *outs):
    src = lax.axis_index("src")
    classes = keep.shape[1] - 8
    for q, out in enumerate(outs):
        block = (src // 2) ^ q
        mine, other = keep[block], got[block]
        first, second = mine[classes : classes + 1], other[classes : classes + 1]
        both = lse([first, second])
        mean = mine[:classes] * jnp.exp(first - both) + other[:classes] * jnp.exp(second - both)
        out[:classes] = mean.astype(BF16)
        out[classes:] = split_rows(both)


def tail_row(piece):
    return jnp.sum(piece[piece.shape[0] - 16 :].astype(F32), axis=0, keepdims=True)


def combine_kernel(log_b, *rest):
    pieces, out = rest[:-1], rest[-1]
    src = lax.axis_index("src")
    classes, width = out.shape[0] - 16, out.shape[1]
    ls = [tail_row(p[...]) for p in pieces]
    total = lse(ls)
    mass = piece_of(log_b, src, width)
    top = total - mass
    out[:classes] = tree_sum([p[:classes].astype(F32) * jnp.exp(l - top) for p, l in zip(pieces, ls)]).astype(BF16)
    out[classes:] = split_rows(EPS * mass - EPS * total)


def assemble_kernel(order, *refs):
    pieces, (g_out, out, row) = refs[: len(order)], refs[len(order) :]
    src = lax.axis_index("src")
    classes, width = out.shape[0], pieces[0].shape[1]
    for k, piece in zip(order, pieces):
        here = pl.ds(pl.multiple_of((src ^ k) * width, width), width)
        out[:, here] = piece[:classes]
        row[:, here] = tail_row(piece[...])
    g_out[...] = row[...].reshape(g_out.shape)


VM = pl.BlockSpec(memory_space=pltpu.VMEM)
SM = pl.BlockSpec(memory_space=pltpu.SMEM)
HB = pl.BlockSpec(memory_space=pltpu.HBM)
PARAMS = pltpu.CompilerParams(vmem_limit_bytes=LIMIT)


def local(cost, cost_scale, slot_block_row, slot_block_column, device_block_count, log_a, log_b, labels):
    n_src, n_tgt = lax.axis_size("src"), lax.axis_size("tgt")
    slots, tile = cost.shape[1], cost.shape[2]
    rb, cb = log_a.shape[0] // tile, log_b.shape[0] // tile
    classes = labels.shape[1]
    dims = (rb, cb, slots)
    in_hbm = functools.partial(pltpu.with_memory_space_constraint, memory_space=pltpu.HBM)
    in_vmem = functools.partial(pltpu.with_memory_space_constraint, memory_space=pltpu.VMEM)
    in_smem = functools.partial(pltpu.with_memory_space_constraint, memory_space=pltpu.SMEM)

    def xor(x, axis, k):
        return lax.ppermute(x, axis, [(i, i ^ k) for i in range(lax.axis_size(axis))])

    def doubled(part, axis):
        k = 1
        while 2 * k < lax.axis_size(axis):
            part = lse([part, xor(part, axis, k)])
            k *= 2
        return [part, xor(part, axis, k)]

    outer = n_tgt // INNER
    along_z = [[x * INNER + z for z in range(INNER)] for x in range(outer)]
    along_x = [[x * INNER + z for x in range(outer)] for z in range(INNER)]

    def everyone(copies, axis, groups=None):
        return lax.all_to_all(copies, axis, 0, 0, axis_index_groups=groups, tiled=True)

    cost = in_hbm(cost)
    vec = functools.partial(jax.ShapeDtypeStruct, dtype=F32)
    chunks = pltpu.VMEM((tile // 128, 128), F32)
    work = [pltpu.SMEM((3,), F32), pltpu.VMEM((tile, tile), BF16), chunks, chunks, pltpu.SemaphoreType.DMA]
    rows, cols = pltpu.VMEM((rb, tile), F32), pltpu.VMEM((cb, tile), F32)

    k_all, row_l, ints, floats, log_a, log_b = pl.pallas_call(
        functools.partial(build_kernel, dims),
        out_shape=(
            pltpu.VMEM((slots, tile, tile), BF16),
            vec((INNER, rb, tile)),
            pltpu.SMEM((1, 2 * slots + 1), jnp.int32),
            pltpu.SMEM((1, slots + 2), F32),
            pltpu.VMEM((rb, tile), F32),
            pltpu.VMEM((cb, tile), F32),
        ),
        in_specs=[SM] + [HB] * 6,
        out_specs=(VM, VM, SM, SM, VM, VM),
        scratch_shapes=[
            rows,
            pltpu.VMEM((slots, tile, tile), BF16),
            rows,
            cols,
            chunks,
            chunks,
            pltpu.SMEM((3,), F32),
            pltpu.SemaphoreType.DMA((slots, tile // PART)),
            pltpu.SMEM((1, slots), F32),
            pltpu.SMEM((1, slots), jnp.int32),
            pltpu.SMEM((1, slots), jnp.int32),
            pltpu.VMEM((rb * tile,), F32),
            pltpu.VMEM((cb * tile,), F32),
            pltpu.SemaphoreType.DMA((5,)),
            pltpu.VMEM((tile, 128), F32),
        ],
        compiler_params=PARAMS,
    )(
        device_block_count,
        in_hbm(cost_scale),
        in_hbm(slot_block_row),
        in_hbm(slot_block_column),
        in_hbm(log_a),
        in_hbm(log_b),
        cost,
    )
    k_all, log_a, log_b = in_vmem(k_all), in_vmem(log_a), in_vmem(log_b)
    scalars = (in_smem(ints), in_smem(floats))
    common = [SM] * 2 + [VM, HB, VM]

    flat = pltpu.VMEM(FLAT, F32)
    sent = functools.partial(jax.ShapeDtypeStruct, dtype=BF16)
    lab_t = labels.T
    f_pot = g_pot = box = None
    for step in range(ITERS):
        if step < 2:
            along = everyone(row_l, "tgt", along_z)
            if step == 0:
                part = lse([along[z] for z in range(INNER)])
                copies = jnp.broadcast_to(part[None], (outer,) + part.shape)
            else:
                high = FLAT[0] + INNER * (along.shape[1] - FLAT[0])
                copies = pl.pallas_call(
                    relay_kernel,
                    out_shape=sent((outer, high, FLAT[1])),
                    in_specs=[VM],
                    out_specs=VM,
                    compiler_params=PARAMS,
                )(along)
            row_parts = everyone(copies, "tgt", along_x)
            box = row_parts if step else None
        else:
            row_parts = everyone(row_l, "tgt")
        if step == ITERS - 1:
            break
        first = step == 0
        col_l, f_pot = pl.pallas_call(
            functools.partial(col_kernel, slots, first),
            out_shape=(vec((n_src, cb, tile)) if first else sent((n_src,) + FLAT), vec((rb, tile))),
            in_specs=common + [VM] * (1 if first else 4),
            out_specs=(VM, VM),
            scratch_shapes=[cols, flat, cols] + work,
            compiler_params=PARAMS,
        )(*scalars, log_a, cost, k_all, row_parts, *(() if first else (f_pot, log_b, g_pot)))
        col_parts = everyone(col_l, "src")
        extra = FLAT[0] * lab_t.size // (FLAT[0] * FLAT[1]) if first else 0
        last = step == ITERS - 2
        row_l, *g_out = pl.pallas_call(
            functools.partial(row_kernel, slots, first),
            out_shape=(sent((INNER if first else n_tgt, FLAT[0] + extra, FLAT[1])), vec((cb, tile)))[: 1 if last else 2],
            in_specs=common + [VM] * 4,
            out_specs=(VM, VM)[: 1 if last else 2],
            scratch_shapes=[cols] * last + [rows, flat, pltpu.VMEM((tile, 128), F32), rows] + work,
            compiler_params=PARAMS,
        )(*scalars, log_b, cost, k_all, col_parts, log_a, f_pot, lab_t if first else g_pot)
        g_pot = g_out[0] if g_out else None

    width = cb * tile // n_src
    piece = jax.ShapeDtypeStruct((classes + 16, width), BF16)
    half = vec((cb, classes + 8, width))
    half_cols = pltpu.VMEM((cb, width), F32)

    def label_call(own):
        return pl.pallas_call(
            functools.partial(label_kernel, slots, own),
            out_shape=(vec((rb, tile)), half) if own else (half,),
            in_specs=common + [VM] * 3,
            out_specs=(VM,) * (1 + own),
            scratch_shapes=[rows] * (not own)
            + [
                pltpu.VMEM((cb, classes, width), F32),
                half_cols,
                flat,
                pltpu.VMEM((INNER, classes, 128), BF16),
                half_cols,
            ]
            + work[:3]
            + [pltpu.VMEM((width // 128, 128), F32), work[4]],
            cost_estimate=pl.CostEstimate(
                flops=slots * tile * tile * 150, bytes_accessed=slots * tile * tile, transcendentals=slots * tile
            ),
            compiler_params=PARAMS,
        )(*scalars, log_a, cost, k_all, f_pot, row_parts, box)

    got = xor(label_call(False)[0], "src", 1)
    f_pot, keep = label_call(True)
    n_y = n_src // 2
    pieces = pl.pallas_call(
        merge_kernel,
        out_shape=(piece,) * n_y,
        in_specs=[VM] * 2,
        out_specs=(VM,) * n_y,
        compiler_params=PARAMS,
    )(keep, got)
    pieces = [pieces[0]] + [xor(pieces[q], "src", 2 * q) for q in range(1, n_y)]
    done = pl.pallas_call(
        combine_kernel,
        out_shape=piece,
        in_specs=[VM] * (1 + n_y),
        out_specs=VM,
        compiler_params=PARAMS,
    )(log_b, *pieces)
    pieces = [done] + [xor(done, "src", 2 * q) for q in range(1, n_y)]
    pieces = pieces + [xor(p, "src", 1) for p in pieces]
    order = tuple(2 * q for q in range(n_y)) + tuple(2 * q + 1 for q in range(n_y))
    g_pot, out = pl.pallas_call(
        functools.partial(assemble_kernel, order),
        out_shape=(vec((cb * tile,)), jax.ShapeDtypeStruct((classes, cb * tile), BF16)),
        in_specs=[VM] * n_src,
        out_specs=(VM, VM),
        scratch_shapes=[pltpu.VMEM((1, cb * tile), F32)],
        compiler_params=PARAMS,
    )(*pieces)
    return f_pot.reshape(-1), g_pot, out.T


def solution(mesh):
    in_specs = (
        P("src", "tgt", None, None),
        P("src", "tgt"),
        P("src", "tgt"),
        P("src", "tgt"),
        P("src", "tgt"),
        P("src"),
        P("tgt"),
        P(("src", "tgt"), None),
    )
    out_specs = (P("src"), P("tgt"), P("tgt", None))
    return jax.shard_map(local, mesh=mesh, in_specs=in_specs, out_specs=out_specs, check_vma=False)
```

```python
import functools

import jax
import jax.numpy as jnp
from jax import lax
from jax.experimental import pallas as pl
from jax.experimental.pallas import tpu as pltpu
from jax.sharding import PartitionSpec as P

ITERS = 4
EPS = 0.5
NEG = -1e30
LOG2E = 1.4426950408889634
TO2 = LOG2E / EPS
PART = 256
INNER = 8
MIDDLE = 116.0
FLAT = (16, 256)
LIMIT = 40 * 1024 * 1024
F32, BF16 = jnp.float32, jnp.bfloat16


def tree_sum(parts):
    while len(parts) > 1:
        parts = [a + b for a, b in zip(parts[0::2], parts[1::2])]
    return parts[0]


def lse(parts):
    top = functools.reduce(jnp.maximum, parts)
    return top + jnp.log(tree_sum([jnp.exp(p - top) for p in parts]))


class Slots:
    def __init__(self, ints, floats, total):
        self.total = total
        self.row = [ints[0, s] for s in range(total)]
        self.col = [ints[0, total + s] for s in range(total)]
        self.count = ints[0, 2 * total]
        self.live = [s < self.count for s in range(total)]
        self.scale = [floats[0, s] for s in range(total)]
        self.shift, self.high = floats[0, total], floats[0, total + 1]
        self.src, self.tgt = lax.axis_index("src"), lax.axis_index("tgt")


def split_rows(x):
    x = jnp.broadcast_to(x, (16, x.shape[1]))
    hi = x.astype(BF16).astype(F32)
    rest = x - hi
    mid = rest.astype(BF16).astype(F32)
    low = (rest - mid).astype(BF16).astype(F32)
    at = lax.broadcasted_iota(jnp.int32, x.shape, 0)
    zero = jnp.zeros_like(x)
    return jnp.where(at == 0, hi, jnp.where(at == 1, mid, jnp.where(at == 2, low, zero))).astype(BF16)


def k_row(lhs, k_block):
    return lax.dot_general(lhs, k_block, (((1,), (1,)), ((), ())), preferred_element_type=F32)


def fold_lanes(x):
    return tree_sum([x[:, c * 128 : (c + 1) * 128] for c in range(x.shape[1] // 128)])


def fold_rows(tall):
    wide = tall[...]
    hi = wide.astype(BF16)
    low = (wide - hi.astype(F32)).astype(BF16)
    ones = jnp.ones((16, 128), BF16)
    return (k_row(ones, hi) + k_row(ones, low))[0:1]


def k_col(lhs, k_block):
    return lax.dot_general(lhs, k_block, (((1,), (0,)), ((), ())), preferred_element_type=F32)


def chunked(row, out_ref):
    for c in range(out_ref.shape[0]):
        out_ref[c : c + 1, :] = row[:, c * 128 : (c + 1) * 128]


def tile_z(cost_v, scale, other8, out_chunk, red_chunk, rows_mode):
    mine = pl.ds(pl.multiple_of(out_chunk * 128, 128), 128)
    summed = pl.ds(pl.multiple_of(red_chunk * 128, 128), 128)
    other = jnp.broadcast_to(other8[pl.ds(red_chunk, 1), :], (128, 128)).T
    if rows_mode:
        tile = cost_v[mine, summed].astype(F32).T
    else:
        tile = cost_v[summed, mine].astype(F32)
    return (other - scale * tile) / EPS


def slow_lse(slots, cost_hbm, cost_v, sem, other8, out8, other_ref, l_ref, rows_mode, start=0):
    l_ref[...] = jnp.full(l_ref.shape, NEG, F32)
    chunks, out_chunks = other8.shape[0], out8.shape[0]
    for s in range(slots.total):
        out_at, other_at = (slots.row[s], slots.col[s]) if rows_mode else (slots.col[s], slots.row[s])

        @pl.when(slots.live[s])
        def _():
            copy = pltpu.make_async_copy(cost_hbm.at[0, s], cost_v, sem)
            copy.start()
            copy.wait()
            chunked(other_ref[pl.ds(other_at, 1), :], other8)

            @pl.loop(0, out_chunks)
            def _(i):
                def step(j, carry):
                    m, total = carry
                    z = tile_z(cost_v, slots.scale[s], other8, start + i, j, rows_mode)
                    top = jnp.maximum(m, jnp.max(z, axis=0, keepdims=True))
                    total = total * jnp.exp(m - top) + jnp.sum(jnp.exp(z - top), axis=0, keepdims=True)
                    return top, total

                first = (jnp.full((1, 128), NEG, F32), jnp.zeros((1, 128), F32))
                m, total = lax.fori_loop(0, chunks, step, first)
                out8[pl.ds(i, 1), :] = m + jnp.log(total)

            new = jnp.concatenate([out8[c : c + 1, :] for c in range(out_chunks)], axis=1)
            old = l_ref[pl.ds(out_at, 1), :]
            top = jnp.maximum(old, new)
            l_ref[pl.ds(out_at, 1), :] = top + jnp.log(jnp.exp(old - top) + jnp.exp(new - top))


def piece_of(ref, piece, width):
    per = ref.shape[1] // width
    row = ref[pl.ds(piece // per, 1), :]
    out = row[:, :width]
    for c in range(1, per):
        out = jnp.where(piece % per == c, row[:, c * width : (c + 1) * width], out)
    return out


def to_log(total, shift):
    return jnp.where(total > 0, jnp.log(jnp.maximum(total, 1e-38)) - shift / EPS, NEG)


def send_copies(l_ref, copies_ref):
    for k in range(copies_ref.shape[0]):
        copies_ref[k] = l_ref[...]


def send_flat(x, flat, copies_ref):
    count, width = x.shape[0], flat.shape[1]
    for c in range(x.shape[1] // width):
        flat[c * count : (c + 1) * count, :] = x[:, c * width : (c + 1) * width]
    x = flat[...].astype(BF16)
    for k in range(copies_ref.shape[0]):
        copies_ref[k, : flat.shape[0]] = x


def send_relative(l_ref, pot, log_mass, flat, copies_ref):
    send_flat(jnp.exp(l_ref[...] + pot[...] / EPS - log_mass[...]), flat, copies_ref)


def new_potential(out, log_mass, parts, prev, flat):
    if parts.dtype == F32:
        out[...] = EPS * log_mass[...] - EPS * lse([parts[k] for k in range(parts.shape[0])])
        return
    parts = [parts[k, : flat.shape[0]].astype(F32) for k in range(parts.shape[0])]
    if prev is None:
        top = functools.reduce(jnp.maximum, parts)
        inv = 1.0 / top
        flat[...] = MIDDLE + 2.0 * jnp.log(top) + jnp.log(tree_sum([(p * inv) * (p * inv) for p in parts]))
    else:
        flat[...] = jnp.log(tree_sum(parts))
    count, width = out.shape[0], flat.shape[1]
    for c in range(out.shape[1] // width):
        here = slice(c * width, (c + 1) * width)
        base = EPS * log_mass[:, here] if prev is None else prev[:, here]
        out[:, here] = base - EPS * flat[c * count : (c + 1) * count, :]


def sums_fine(low, high, others):
    return (low >= 2.0**-80 * jnp.maximum(others, 1.0)) & (high <= 2.0**100)


def build_kernel(
    dims, count, scale_hbm, row_hbm, col_hbm, a_hbm, b_hbm, cost_hbm,
    k_ref, copies_ref, ints, floats, a_ref, b_ref,
    l_ref, cost_v, sums, zero, other8, out8, stat, sems,
    scale, row, col, log_a, log_b, small_sems, tall, flat,
):
    rb, cb, total = dims
    small = [
        pltpu.make_async_copy(a, b, small_sems.at[i])
        for i, (a, b) in enumerate(
            ((scale_hbm, scale), (row_hbm, row), (col_hbm, col), (a_hbm, log_a), (b_hbm, log_b))
        )
    ]
    parts = cost_v.shape[1] // PART
    copies = [
        [
            pltpu.make_async_copy(
                cost_hbm.at[0, s, pl.ds(h * PART, PART)], cost_v.at[s, pl.ds(h * PART, PART)], sems.at[s, h]
            )
            for h in range(parts)
        ]
        for s in range(total)
    ]
    copies[0][0].start()
    for copy in small:
        copy.start()
    for s in range(total):

        @pl.when(s < count[0, 0])
        def _():
            for h in range(0 if s else 1, parts):
                copies[s][h].start()

    for copy in small[:3]:
        copy.wait()
    src, tgt = lax.axis_index("src"), lax.axis_index("tgt")
    for s in range(total):
        ints[0, s] = row[0, s] - src * rb
        ints[0, total + s] = col[0, s] - tgt * cb
        floats[0, s] = scale[0, s]
    ints[0, 2 * total] = count[0, 0]
    slots = Slots(ints, floats, total)
    chunk, tile = 32, cost_v.shape[2]

    def build(shift, wait):
        sums[...] = jnp.zeros(sums.shape, F32)
        floats[0, total] = jnp.float32(0.0) if shift is None else shift
        stat[1] = jnp.float32(0.0)
        stat[2] = jnp.float32(jnp.inf)
        for s in range(total):

            @pl.when(slots.live[s])
            def _():
                for h in range(parts):
                    if wait:
                        copies[s][h].wait()

                    @pl.loop(0, PART // chunk, unroll=2)
                    def _(i):
                        here = pl.ds(pl.multiple_of(h * PART + i * chunk, chunk), chunk)
                        x = cost_v[s, here, :].astype(F32) * (-TO2 * slots.scale[s])
                        if shift is not None:
                            x = x + shift * TO2
                        e = jnp.exp2(x)
                        k_ref[s, here, :] = e.astype(BF16)
                        tall[here, :] = fold_lanes(e)

                part = fold_rows(tall)
                at = pl.ds(slots.row[s], 1)
                sums[at, :] = sums[at, :] + part
                stat[1] = jnp.maximum(stat[1], jnp.max(part))
                stat[2] = jnp.minimum(stat[2], jnp.min(part))

        l_ref[...] = to_log(sums[...], floats[0, total])
        floats[0, total + 1] = stat[1]
        return sums_fine(stat[2], stat[1], stat[1])

    fine = build(None, True)
    for copy in small[3:]:
        copy.wait()
    for r in range(rb):
        a_ref[r : r + 1, :] = log_a[r * tile : (r + 1) * tile].reshape(1, tile)
    for c in range(cb):
        b_ref[c : c + 1, :] = log_b[c * tile : (c + 1) * tile].reshape(1, tile)

    @pl.when(jnp.logical_not(fine))
    def _():
        stat[0] = jnp.float32(jnp.inf)
        for s in range(total):

            @pl.when(slots.live[s])
            def _():
                def lowest(i, low):
                    here = pl.ds(pl.multiple_of(i * chunk, chunk), chunk)
                    return jnp.minimum(low, jnp.min(cost_v[s, here, :].astype(F32)))

                low = lax.fori_loop(0, tile // chunk, lowest, jnp.float32(jnp.inf))
                stat[0] = jnp.minimum(stat[0], low * slots.scale[s])

        shifted = build(stat[0], False)

        @pl.when(jnp.logical_not(shifted))
        def _():
            zero[...] = jnp.zeros(zero.shape, F32)
            slow_lse(slots, cost_hbm, cost_v.at[0], sems.at[0, 0], other8, out8, zero, l_ref, True)

    send_flat(jnp.exp((l_ref[...] - MIDDLE) / 2), flat, copies_ref)


def row_kernel(total, first, ints, floats, log_b, cost_hbm, k_ref, parts, log_a, f, *rest):
    prev, lab = (None, rest[0]) if first else (rest[0], None)
    rest = rest[1:]
    copies_ref, g, l_ref, flat, sums, stat, cost_v, other8, out8, sem = rest
    slots = Slots(ints, floats, total)
    new_potential(g, log_b, parts, prev, flat)
    sums[...] = jnp.zeros(sums.shape, F32)
    stat[0] = jnp.float32(0.0)
    stat[1] = jnp.float32(jnp.inf)
    stat[2] = slots.high
    for s in range(slots.total):

        @pl.when(slots.live[s])
        def _():
            v = jnp.exp2(g[pl.ds(slots.col[s], 1), :] * TO2)
            part = jnp.sum(k_row(split_rows(v), k_ref[s]), axis=0, keepdims=True)
            at = pl.ds(slots.row[s], 1)
            sums[at, :] = sums[at, :] + part
            stat[0] = jnp.maximum(stat[0], jnp.max(part))
            stat[1] = jnp.minimum(stat[1], jnp.min(part))
            stat[2] = jnp.maximum(stat[2], jnp.max(v))

    l_ref[...] = to_log(sums[...], slots.shift)

    @pl.when(jnp.logical_not(sums_fine(stat[1], stat[0], stat[2])))
    def _():
        slow_lse(slots, cost_hbm, cost_v, sem, other8, out8, g, l_ref, True)

    send_relative(l_ref, f, log_a, flat, copies_ref)
    if first:
        half = lab.shape[0] // 2
        for k in range(copies_ref.shape[0]):
            copies_ref[k, flat.shape[0] :] = jnp.concatenate([lab[:half], lab[half:]], axis=1)


def relay_kernel(parts, out):
    rows, count = FLAT[0], parts.shape[0]
    total = tree_sum([parts[k, :rows].astype(F32) for k in range(count)]).astype(BF16)
    high = parts.shape[1] - rows
    for k in range(out.shape[0]):
        out[k, :rows] = total
        for p in range(count):
            out[k, rows + p * high : rows + (p + 1) * high] = parts[p, rows:]


def col_kernel(total, first, ints, floats, log_a, cost_hbm, k_ref, parts, *rest):
    (prev, log_b, g), rest = ((None, None, None), rest) if first else (rest[:3], rest[3:])
    copies_ref, f, l_ref, flat, sums, stat, cost_v, other8, out8, sem = rest
    slots = Slots(ints, floats, total)
    new_potential(f, log_a, parts, prev, flat)
    sums[...] = jnp.zeros(sums.shape, F32)
    stat[0] = jnp.float32(0.0)
    stat[1] = jnp.float32(jnp.inf)
    stat[2] = slots.high
    for s in range(slots.total):

        @pl.when(slots.live[s])
        def _():
            u = jnp.exp2(f[pl.ds(slots.row[s], 1), :] * TO2)
            part = jnp.sum(k_col(split_rows(u), k_ref[s]), axis=0, keepdims=True)
            at = pl.ds(slots.col[s], 1)
            sums[at, :] = sums[at, :] + part
            stat[0] = jnp.maximum(stat[0], jnp.max(part))
            stat[1] = jnp.minimum(stat[1], jnp.min(part))
            stat[2] = jnp.maximum(stat[2], jnp.max(u))

    l_ref[...] = to_log(sums[...], slots.shift)

    @pl.when(jnp.logical_not(sums_fine(stat[1], stat[0], stat[2])))
    def _():
        slow_lse(slots, cost_hbm, cost_v, sem, other8, out8, f, l_ref, False)

    if first:
        send_copies(l_ref, copies_ref)
    else:
        send_relative(l_ref, g, log_b, flat, copies_ref)


def label_kernel(total, own, ints, floats, log_a, cost_hbm, k_ref, prev, parts, box, *rest):
    (f, out), rest = (rest[:2] if own else rest[1::-1]), rest[2:]
    acc, l_ref, flat, lab_v, sums, stat, cost_v, other8, out8, sem = rest
    slots = Slots(ints, floats, total)
    classes, width = acc.shape[1], acc.shape[2]
    new_potential(f, log_a, parts, prev, flat)
    sums[...] = jnp.zeros(sums.shape, F32)
    acc[...] = jnp.zeros(acc.shape, F32)
    stat[0] = jnp.float32(0.0)
    stat[1] = jnp.float32(jnp.inf)
    stat[2] = slots.high
    high = classes // 2
    core = slots.src % 2
    half = core if own else 1 - core
    lanes = pl.ds(pl.multiple_of(half * width, width), width)

    def label_piece(block, p):
        at = FLAT[0] + p * high
        both = box[block, at : at + high]
        return jnp.concatenate([both[:, :128], both[:, 128:]], axis=0)

    for s in range(slots.total):

        @pl.when(slots.live[s])
        def _():
            u = jnp.exp2(f[pl.ds(slots.row[s], 1), :] * TO2)
            lab = jnp.concatenate([label_piece(slots.row[s], p) for p in range(INNER)], axis=1)
            weighted = lab.astype(F32) * u
            hi = weighted.astype(BF16)
            low = (weighted - hi.astype(F32)).astype(BF16)
            res = k_col(jnp.concatenate([hi, low, split_rows(u)], axis=0), k_ref[s, :, lanes])
            part = jnp.sum(res[2 * classes :], axis=0, keepdims=True)
            at = pl.ds(slots.col[s], 1)
            sums[at, :] = sums[at, :] + part
            acc[slots.col[s]] = acc[slots.col[s]] + (res[:classes] + res[classes : 2 * classes])
            stat[0] = jnp.maximum(stat[0], jnp.max(part))
            stat[1] = jnp.minimum(stat[1], jnp.min(part))
            stat[2] = jnp.maximum(stat[2], jnp.max(u))

    l_ref[...] = to_log(sums[...], slots.shift)

    @pl.when(jnp.logical_not(sums_fine(stat[1], stat[0], stat[2])))
    def _():
        chunks = width // 128
        slow_lse(slots, cost_hbm, cost_v, sem, other8, out8, f, l_ref, False, half * chunks)
        acc[...] = jnp.zeros(acc.shape, F32)
        sums[...] = jnp.ones(sums.shape, F32)
        for s in range(slots.total):

            @pl.when(slots.live[s])
            def _():
                copy = pltpu.make_async_copy(cost_hbm.at[0, s], cost_v, sem)
                copy.start()
                copy.wait()
                chunked(f[pl.ds(slots.row[s], 1), :], other8)
                chunked(l_ref[pl.ds(slots.col[s], 1), :], out8)
                for p in range(INNER):
                    lab_v[p] = label_piece(slots.row[s], p)

                @pl.loop(0, chunks * INNER)
                def _(ij):
                    i, j = ij // INNER, ij % INNER
                    here = pl.ds(pl.multiple_of(i * 128, 128), 128)
                    z = tile_z(cost_v, slots.scale[s], other8, half * chunks + i, j, False)
                    p = jnp.exp(z - out8[pl.ds(i, 1), :]).astype(BF16)
                    term = jnp.dot(lab_v[j], p, preferred_element_type=F32)
                    acc[slots.col[s], :, here] = acc[slots.col[s], :, here] + term

    for c in range(acc.shape[0]):
        mass = sums[c : c + 1, :]
        out[c, :classes] = acc[c] * jnp.where(mass > 0, 1.0 / jnp.maximum(mass, 1e-38), 0.0)
        out[c, classes:] = jnp.broadcast_to(l_ref[c : c + 1, :], (8, width))


def merge_kernel(keep, got, *outs):
    src = lax.axis_index("src")
    classes = keep.shape[1] - 8
    for q, out in enumerate(outs):
        block = (src // 2) ^ q
        mine, other = keep[block], got[block]
        first, second = mine[classes : classes + 1], other[classes : classes + 1]
        both = lse([first, second])
        mean = mine[:classes] * jnp.exp(first - both) + other[:classes] * jnp.exp(second - both)
        out[:classes] = mean.astype(BF16)
        out[classes:] = split_rows(both)


def tail_row(piece):
    return jnp.sum(piece[piece.shape[0] - 16 :].astype(F32), axis=0, keepdims=True)


def combine_kernel(log_b, *rest):
    pieces, out = rest[:-1], rest[-1]
    src = lax.axis_index("src")
    classes, width = out.shape[0] - 16, out.shape[1]
    ls = [tail_row(p[...]) for p in pieces]
    total = lse(ls)
    mass = piece_of(log_b, src, width)
    top = total - mass
    out[:classes] = tree_sum([p[:classes].astype(F32) * jnp.exp(l - top) for p, l in zip(pieces, ls)]).astype(BF16)
    out[classes:] = split_rows(EPS * mass - EPS * total)


def assemble_kernel(order, *refs):
    pieces, (g_out, out, row) = refs[: len(order)], refs[len(order) :]
    src = lax.axis_index("src")
    classes, width = out.shape[0], pieces[0].shape[1]
    for k, piece in zip(order, pieces):
        here = pl.ds(pl.multiple_of((src ^ k) * width, width), width)
        out[:, here] = piece[:classes]
        row[:, here] = tail_row(piece[...])
    g_out[...] = row[...].reshape(g_out.shape)


VM = pl.BlockSpec(memory_space=pltpu.VMEM)
SM = pl.BlockSpec(memory_space=pltpu.SMEM)
HB = pl.BlockSpec(memory_space=pltpu.HBM)
PARAMS = pltpu.CompilerParams(vmem_limit_bytes=LIMIT)


def local(cost, cost_scale, slot_block_row, slot_block_column, device_block_count, log_a, log_b, labels):
    n_src, n_tgt = lax.axis_size("src"), lax.axis_size("tgt")
    slots, tile = cost.shape[1], cost.shape[2]
    rb, cb = log_a.shape[0] // tile, log_b.shape[0] // tile
    classes = labels.shape[1]
    dims = (rb, cb, slots)
    in_hbm = functools.partial(pltpu.with_memory_space_constraint, memory_space=pltpu.HBM)
    in_vmem = functools.partial(pltpu.with_memory_space_constraint, memory_space=pltpu.VMEM)
    in_smem = functools.partial(pltpu.with_memory_space_constraint, memory_space=pltpu.SMEM)

    def xor(x, axis, k):
        return lax.ppermute(x, axis, [(i, i ^ k) for i in range(lax.axis_size(axis))])

    def doubled(part, axis):
        k = 1
        while 2 * k < lax.axis_size(axis):
            part = lse([part, xor(part, axis, k)])
            k *= 2
        return [part, xor(part, axis, k)]

    outer = n_tgt // INNER
    along_z = [[x * INNER + z for z in range(INNER)] for x in range(outer)]
    along_x = [[x * INNER + z for x in range(outer)] for z in range(INNER)]

    def everyone(copies, axis, groups=None):
        return lax.all_to_all(copies, axis, 0, 0, axis_index_groups=groups, tiled=True)

    cost = in_hbm(cost)
    vec = functools.partial(jax.ShapeDtypeStruct, dtype=F32)
    sent = functools.partial(jax.ShapeDtypeStruct, dtype=BF16)
    chunks = pltpu.VMEM((tile // 128, 128), F32)
    work = [pltpu.SMEM((3,), F32), pltpu.VMEM((tile, tile), BF16), chunks, chunks, pltpu.SemaphoreType.DMA]
    rows, cols = pltpu.VMEM((rb, tile), F32), pltpu.VMEM((cb, tile), F32)

    k_all, row_l, ints, floats, log_a, log_b = pl.pallas_call(
        functools.partial(build_kernel, dims),
        out_shape=(
            pltpu.VMEM((slots, tile, tile), BF16),
            sent((n_tgt,) + FLAT),
            pltpu.SMEM((1, 2 * slots + 1), jnp.int32),
            pltpu.SMEM((1, slots + 2), F32),
            pltpu.VMEM((rb, tile), F32),
            pltpu.VMEM((cb, tile), F32),
        ),
        in_specs=[SM] + [HB] * 6,
        out_specs=(VM, VM, SM, SM, VM, VM),
        scratch_shapes=[
            rows,
            pltpu.VMEM((slots, tile, tile), BF16),
            rows,
            cols,
            chunks,
            chunks,
            pltpu.SMEM((3,), F32),
            pltpu.SemaphoreType.DMA((slots, tile // PART)),
            pltpu.SMEM((1, slots), F32),
            pltpu.SMEM((1, slots), jnp.int32),
            pltpu.SMEM((1, slots), jnp.int32),
            pltpu.VMEM((rb * tile,), F32),
            pltpu.VMEM((cb * tile,), F32),
            pltpu.SemaphoreType.DMA((5,)),
            pltpu.VMEM((tile, 128), F32),
            pltpu.VMEM(FLAT, F32),
        ],
        compiler_params=PARAMS,
    )(
        device_block_count,
        in_hbm(cost_scale),
        in_hbm(slot_block_row),
        in_hbm(slot_block_column),
        in_hbm(log_a),
        in_hbm(log_b),
        cost,
    )
    k_all, log_a, log_b = in_vmem(k_all), in_vmem(log_a), in_vmem(log_b)
    scalars = (in_smem(ints), in_smem(floats))
    common = [SM] * 2 + [VM, HB, VM]

    flat = pltpu.VMEM(FLAT, F32)
    lab_t = labels.T
    f_pot = g_pot = box = None
    for step in range(ITERS):
        if step == 1:
            along = everyone(row_l, "tgt", along_z)
            high = FLAT[0] + INNER * (along.shape[1] - FLAT[0])
            copies = pl.pallas_call(
                relay_kernel,
                out_shape=sent((outer, high, FLAT[1])),
                in_specs=[VM],
                out_specs=VM,
                compiler_params=PARAMS,
            )(along)
            row_parts = box = everyone(copies, "tgt", along_x)
        else:
            row_parts = everyone(row_l, "tgt")
        if step == ITERS - 1:
            break
        first = step == 0
        col_l, f_pot = pl.pallas_call(
            functools.partial(col_kernel, slots, first),
            out_shape=(vec((n_src, cb, tile)) if first else sent((n_src,) + FLAT), vec((rb, tile))),
            in_specs=common + [VM] * (1 if first else 4),
            out_specs=(VM, VM),
            scratch_shapes=[cols, flat, cols] + work,
            compiler_params=PARAMS,
        )(*scalars, log_a, cost, k_all, row_parts, *(() if first else (f_pot, log_b, g_pot)))
        col_parts = everyone(col_l, "src")
        extra = FLAT[0] * lab_t.size // (FLAT[0] * FLAT[1]) if first else 0
        last = step == ITERS - 2
        row_l, *g_out = pl.pallas_call(
            functools.partial(row_kernel, slots, first),
            out_shape=(sent((INNER if first else n_tgt, FLAT[0] + extra, FLAT[1])), vec((cb, tile)))[: 1 if last else 2],
            in_specs=common + [VM] * 4,
            out_specs=(VM, VM)[: 1 if last else 2],
            scratch_shapes=[cols] * last + [rows, flat, rows] + work,
            compiler_params=PARAMS,
        )(*scalars, log_b, cost, k_all, col_parts, log_a, f_pot, lab_t if first else g_pot)
        g_pot = g_out[0] if g_out else None

    width = cb * tile // n_src
    piece = jax.ShapeDtypeStruct((classes + 16, width), BF16)
    half = vec((cb, classes + 8, width))
    half_cols = pltpu.VMEM((cb, width), F32)

    def label_call(own):
        return pl.pallas_call(
            functools.partial(label_kernel, slots, own),
            out_shape=(vec((rb, tile)), half) if own else (half,),
            in_specs=common + [VM] * 3,
            out_specs=(VM,) * (1 + own),
            scratch_shapes=[rows] * (not own)
            + [
                pltpu.VMEM((cb, classes, width), F32),
                half_cols,
                flat,
                pltpu.VMEM((INNER, classes, 128), BF16),
                half_cols,
            ]
            + work[:3]
            + [pltpu.VMEM((width // 128, 128), F32), work[4]],
            cost_estimate=pl.CostEstimate(
                flops=slots * tile * tile * 150, bytes_accessed=slots * tile * tile, transcendentals=slots * tile
            ),
            compiler_params=PARAMS,
        )(*scalars, log_a, cost, k_all, f_pot, row_parts, box)

    got = xor(label_call(False)[0], "src", 1)
    f_pot, keep = label_call(True)
    n_y = n_src // 2
    pieces = pl.pallas_call(
        merge_kernel,
        out_shape=(piece,) * n_y,
        in_specs=[VM] * 2,
        out_specs=(VM,) * n_y,
        compiler_params=PARAMS,
    )(keep, got)
    pieces = [pieces[0]] + [xor(pieces[q], "src", 2 * q) for q in range(1, n_y)]
    done = pl.pallas_call(
        combine_kernel,
        out_shape=piece,
        in_specs=[VM] * (1 + n_y),
        out_specs=VM,
        compiler_params=PARAMS,
    )(log_b, *pieces)
    pieces = [done] + [xor(done, "src", 2 * q) for q in range(1, n_y)]
    pieces = pieces + [xor(p, "src", 1) for p in pieces]
    order = tuple(2 * q for q in range(n_y)) + tuple(2 * q + 1 for q in range(n_y))
    g_pot, out = pl.pallas_call(
        functools.partial(assemble_kernel, order),
        out_shape=(vec((cb * tile,)), jax.ShapeDtypeStruct((classes, cb * tile), BF16)),
        in_specs=[VM] * n_src,
        out_specs=(VM, VM),
        scratch_shapes=[pltpu.VMEM((1, cb * tile), F32)],
        compiler_params=PARAMS,
    )(*pieces)
    return f_pot.reshape(-1), g_pot, out.T


def solution(mesh):
    in_specs = (
        P("src", "tgt", None, None),
        P("src", "tgt"),
        P("src", "tgt"),
        P("src", "tgt"),
        P("src", "tgt"),
        P("src"),
        P("tgt"),
        P(("src", "tgt"), None),
    )
    out_specs = (P("src"), P("tgt"), P("tgt", None))
    return jax.shard_map(local, mesh=mesh, in_specs=in_specs, out_specs=out_specs, check_vma=False)
```

```python
import functools

import jax
import jax.numpy as jnp
from jax import lax
from jax.experimental import pallas as pl
from jax.experimental.pallas import tpu as pltpu
from jax.sharding import PartitionSpec as P

ITERS = 4
EPS = 0.5
NEG = -1e30
LOG2E = 1.4426950408889634
TO2 = LOG2E / EPS
PART = 256
INNER = 8
MIDDLE = 116.0
FLAT = (16, 256)
LIMIT = 40 * 1024 * 1024
F32, BF16 = jnp.float32, jnp.bfloat16


def tree_sum(parts):
    while len(parts) > 1:
        parts = [a + b for a, b in zip(parts[0::2], parts[1::2])]
    return parts[0]


def lse(parts):
    top = functools.reduce(jnp.maximum, parts)
    return top + jnp.log(tree_sum([jnp.exp(p - top) for p in parts]))


class Slots:
    def __init__(self, ints, floats, total):
        self.total = total
        self.row = [ints[0, s] for s in range(total)]
        self.col = [ints[0, total + s] for s in range(total)]
        self.count = ints[0, 2 * total]
        self.live = [s < self.count for s in range(total)]
        self.scale = [floats[0, s] for s in range(total)]
        self.shift, self.high = floats[0, total], floats[0, total + 1]
        self.src, self.tgt = lax.axis_index("src"), lax.axis_index("tgt")


def split_rows(x):
    x = jnp.broadcast_to(x, (16, x.shape[1]))
    hi = x.astype(BF16).astype(F32)
    rest = x - hi
    mid = rest.astype(BF16).astype(F32)
    low = (rest - mid).astype(BF16).astype(F32)
    at = lax.broadcasted_iota(jnp.int32, x.shape, 0)
    zero = jnp.zeros_like(x)
    return jnp.where(at == 0, hi, jnp.where(at == 1, mid, jnp.where(at == 2, low, zero))).astype(BF16)


def k_row(lhs, k_block):
    return lax.dot_general(lhs, k_block, (((1,), (1,)), ((), ())), preferred_element_type=F32)


def fold_lanes(x):
    return tree_sum([x[:, c * 128 : (c + 1) * 128] for c in range(x.shape[1] // 128)])


def fold_rows(tall):
    wide = tall[...]
    hi = wide.astype(BF16)
    low = (wide - hi.astype(F32)).astype(BF16)
    ones = jnp.ones((16, 128), BF16)
    return (k_row(ones, hi) + k_row(ones, low))[0:1]


def k_col(lhs, k_block):
    return lax.dot_general(lhs, k_block, (((1,), (0,)), ((), ())), preferred_element_type=F32)


def chunked(row, out_ref):
    for c in range(out_ref.shape[0]):
        out_ref[c : c + 1, :] = row[:, c * 128 : (c + 1) * 128]


def tile_z(cost_v, scale, other8, out_chunk, red_chunk, rows_mode):
    mine = pl.ds(pl.multiple_of(out_chunk * 128, 128), 128)
    summed = pl.ds(pl.multiple_of(red_chunk * 128, 128), 128)
    other = jnp.broadcast_to(other8[pl.ds(red_chunk, 1), :], (128, 128)).T
    if rows_mode:
        tile = cost_v[mine, summed].astype(F32).T
    else:
        tile = cost_v[summed, mine].astype(F32)
    return (other - scale * tile) / EPS


def slow_lse(slots, cost_hbm, cost_v, sem, other8, out8, other_ref, l_ref, rows_mode, start=0):
    l_ref[...] = jnp.full(l_ref.shape, NEG, F32)
    chunks, out_chunks = other8.shape[0], out8.shape[0]
    for s in range(slots.total):
        out_at, other_at = (slots.row[s], slots.col[s]) if rows_mode else (slots.col[s], slots.row[s])

        @pl.when(slots.live[s])
        def _():
            copy = pltpu.make_async_copy(cost_hbm.at[0, s], cost_v, sem)
            copy.start()
            copy.wait()
            chunked(other_ref[pl.ds(other_at, 1), :], other8)

            @pl.loop(0, out_chunks)
            def _(i):
                def step(j, carry):
                    m, total = carry
                    z = tile_z(cost_v, slots.scale[s], other8, start + i, j, rows_mode)
                    top = jnp.maximum(m, jnp.max(z, axis=0, keepdims=True))
                    total = total * jnp.exp(m - top) + jnp.sum(jnp.exp(z - top), axis=0, keepdims=True)
                    return top, total

                first = (jnp.full((1, 128), NEG, F32), jnp.zeros((1, 128), F32))
                m, total = lax.fori_loop(0, chunks, step, first)
                out8[pl.ds(i, 1), :] = m + jnp.log(total)

            new = jnp.concatenate([out8[c : c + 1, :] for c in range(out_chunks)], axis=1)
            old = l_ref[pl.ds(out_at, 1), :]
            top = jnp.maximum(old, new)
            l_ref[pl.ds(out_at, 1), :] = top + jnp.log(jnp.exp(old - top) + jnp.exp(new - top))


def piece_of(ref, piece, width):
    per = ref.shape[1] // width
    row = ref[pl.ds(piece // per, 1), :]
    out = row[:, :width]
    for c in range(1, per):
        out = jnp.where(piece % per == c, row[:, c * width : (c + 1) * width], out)
    return out


def to_log(total, shift):
    return jnp.where(total > 0, jnp.log(jnp.maximum(total, 1e-38)) - shift / EPS, NEG)


def send_copies(l_ref, copies_ref):
    for k in range(copies_ref.shape[0]):
        copies_ref[k] = l_ref[...]


def send_flat(x, flat, copies_ref):
    count, width = x.shape[0], flat.shape[1]
    for c in range(x.shape[1] // width):
        flat[c * count : (c + 1) * count, :] = x[:, c * width : (c + 1) * width]
    x = flat[...].astype(BF16)
    for k in range(copies_ref.shape[0]):
        copies_ref[k, : flat.shape[0]] = x


def send_relative(l_ref, pot, log_mass, flat, copies_ref):
    send_flat(jnp.exp(l_ref[...] + pot[...] / EPS - log_mass[...]), flat, copies_ref)


def new_potential(out, log_mass, parts, prev, flat):
    if parts.dtype == F32:
        out[...] = EPS * log_mass[...] - EPS * lse([parts[k] for k in range(parts.shape[0])])
        return
    parts = [parts[k, : flat.shape[0]].astype(F32) for k in range(parts.shape[0])]
    if prev is None:
        top = functools.reduce(jnp.maximum, parts)
        inv = 1.0 / top
        flat[...] = MIDDLE + 2.0 * jnp.log(top) + jnp.log(tree_sum([(p * inv) * (p * inv) for p in parts]))
    else:
        flat[...] = jnp.log(tree_sum(parts))
    count, width = out.shape[0], flat.shape[1]
    for c in range(out.shape[1] // width):
        here = slice(c * width, (c + 1) * width)
        base = EPS * log_mass[:, here] if prev is None else prev[:, here]
        out[:, here] = base - EPS * flat[c * count : (c + 1) * count, :]


def sums_fine(low, high, others):
    return (low >= 2.0**-80 * jnp.maximum(others, 1.0)) & (high <= 2.0**100)


def build_kernel(
    dims, count, scale_hbm, row_hbm, col_hbm, a_hbm, b_hbm, cost_hbm,
    k_ref, copies_ref, ints, floats, a_ref, b_ref,
    l_ref, cost_v, sums, zero, other8, out8, stat, sems,
    scale, row, col, log_a, log_b, small_sems, tall, flat,
):
    rb, cb, total = dims
    small = [
        pltpu.make_async_copy(a, b, small_sems.at[i])
        for i, (a, b) in enumerate(
            ((scale_hbm, scale), (row_hbm, row), (col_hbm, col), (a_hbm, log_a), (b_hbm, log_b))
        )
    ]
    parts = cost_v.shape[1] // PART
    copies = [
        [
            pltpu.make_async_copy(
                cost_hbm.at[0, s, pl.ds(h * PART, PART)], cost_v.at[s, pl.ds(h * PART, PART)], sems.at[s, h]
            )
            for h in range(parts)
        ]
        for s in range(total)
    ]
    copies[0][0].start()
    for copy in small:
        copy.start()
    for s in range(total):

        @pl.when(s < count[0, 0])
        def _():
            for h in range(0 if s else 1, parts):
                copies[s][h].start()

    for copy in small[:3]:
        copy.wait()
    src, tgt = lax.axis_index("src"), lax.axis_index("tgt")
    for s in range(total):
        ints[0, s] = row[0, s] - src * rb
        ints[0, total + s] = col[0, s] - tgt * cb
        floats[0, s] = scale[0, s]
    ints[0, 2 * total] = count[0, 0]
    slots = Slots(ints, floats, total)
    chunk, tile = 16, cost_v.shape[2]

    def build(shift, wait):
        sums[...] = jnp.zeros(sums.shape, F32)
        floats[0, total] = jnp.float32(0.0) if shift is None else shift
        stat[1] = jnp.float32(0.0)
        stat[2] = jnp.float32(jnp.inf)
        for s in range(total):

            @pl.when(slots.live[s])
            def _():
                for h in range(parts):
                    if wait:
                        copies[s][h].wait()

                    @pl.loop(0, PART // chunk, unroll=4)
                    def _(i):
                        here = pl.ds(pl.multiple_of(h * PART + i * chunk, chunk), chunk)
                        x = cost_v[s, here, :].astype(F32) * (-TO2 * slots.scale[s])
                        if shift is not None:
                            x = x + shift * TO2
                        e = jnp.exp2(x)
                        k_ref[s, here, :] = e.astype(BF16)
                        tall[here, :] = fold_lanes(e)

                part = fold_rows(tall)
                at = pl.ds(slots.row[s], 1)
                sums[at, :] = sums[at, :] + part
                stat[1] = jnp.maximum(stat[1], jnp.max(part))
                stat[2] = jnp.minimum(stat[2], jnp.min(part))

        l_ref[...] = to_log(sums[...], floats[0, total])
        floats[0, total + 1] = stat[1]
        return sums_fine(stat[2], stat[1], stat[1])

    fine = build(None, True)
    for copy in small[3:]:
        copy.wait()
    for r in range(rb):
        a_ref[r : r + 1, :] = log_a[r * tile : (r + 1) * tile].reshape(1, tile)
    for c in range(cb):
        b_ref[c : c + 1, :] = log_b[c * tile : (c + 1) * tile].reshape(1, tile)

    @pl.when(jnp.logical_not(fine))
    def _():
        stat[0] = jnp.float32(jnp.inf)
        for s in range(total):

            @pl.when(slots.live[s])
            def _():
                def lowest(i, low):
                    here = pl.ds(pl.multiple_of(i * chunk, chunk), chunk)
                    return jnp.minimum(low, jnp.min(cost_v[s, here, :].astype(F32)))

                low = lax.fori_loop(0, tile // chunk, lowest, jnp.float32(jnp.inf))
                stat[0] = jnp.minimum(stat[0], low * slots.scale[s])

        shifted = build(stat[0], False)

        @pl.when(jnp.logical_not(shifted))
        def _():
            zero[...] = jnp.zeros(zero.shape, F32)
            slow_lse(slots, cost_hbm, cost_v.at[0], sems.at[0, 0], other8, out8, zero, l_ref, True)

    send_flat(jnp.exp((l_ref[...] - MIDDLE) / 2), flat, copies_ref)


def row_kernel(total, first, ints, floats, log_b, cost_hbm, k_ref, parts, log_a, f, *rest):
    prev, lab = (None, rest[0]) if first else (rest[0], None)
    rest = rest[1:]
    copies_ref, g, l_ref, flat, sums, stat, cost_v, other8, out8, sem = rest
    slots = Slots(ints, floats, total)
    new_potential(g, log_b, parts, prev, flat)
    sums[...] = jnp.zeros(sums.shape, F32)
    stat[0] = jnp.float32(0.0)
    stat[1] = jnp.float32(jnp.inf)
    stat[2] = slots.high
    for s in range(slots.total):

        @pl.when(slots.live[s])
        def _():
            v = jnp.exp2(g[pl.ds(slots.col[s], 1), :] * TO2)
            part = jnp.sum(k_row(split_rows(v), k_ref[s]), axis=0, keepdims=True)
            at = pl.ds(slots.row[s], 1)
            sums[at, :] = sums[at, :] + part
            stat[0] = jnp.maximum(stat[0], jnp.max(part))
            stat[1] = jnp.minimum(stat[1], jnp.min(part))
            stat[2] = jnp.maximum(stat[2], jnp.max(v))

    l_ref[...] = to_log(sums[...], slots.shift)

    @pl.when(jnp.logical_not(sums_fine(stat[1], stat[0], stat[2])))
    def _():
        slow_lse(slots, cost_hbm, cost_v, sem, other8, out8, g, l_ref, True)

    send_relative(l_ref, f, log_a, flat, copies_ref)
    if first:
        half = lab.shape[0] // 2
        for k in range(copies_ref.shape[0]):
            copies_ref[k, flat.shape[0] :] = jnp.concatenate([lab[:half], lab[half:]], axis=1)


def relay_kernel(parts, out):
    rows, count = FLAT[0], parts.shape[0]
    total = tree_sum([parts[k, :rows].astype(F32) for k in range(count)]).astype(BF16)
    high = parts.shape[1] - rows
    for k in range(out.shape[0]):
        out[k, :rows] = total
        for p in range(count):
            out[k, rows + p * high : rows + (p + 1) * high] = parts[p, rows:]


def col_kernel(total, first, ints, floats, log_a, cost_hbm, k_ref, parts, *rest):
    (prev, log_b, g), rest = ((None, None, None), rest) if first else (rest[:3], rest[3:])
    copies_ref, f, l_ref, flat, sums, stat, cost_v, other8, out8, sem = rest
    slots = Slots(ints, floats, total)
    new_potential(f, log_a, parts, prev, flat)
    sums[...] = jnp.zeros(sums.shape, F32)
    stat[0] = jnp.float32(0.0)
    stat[1] = jnp.float32(jnp.inf)
    stat[2] = slots.high
    for s in range(slots.total):

        @pl.when(slots.live[s])
        def _():
            u = jnp.exp2(f[pl.ds(slots.row[s], 1), :] * TO2)
            part = jnp.sum(k_col(split_rows(u), k_ref[s]), axis=0, keepdims=True)
            at = pl.ds(slots.col[s], 1)
            sums[at, :] = sums[at, :] + part
            stat[0] = jnp.maximum(stat[0], jnp.max(part))
            stat[1] = jnp.minimum(stat[1], jnp.min(part))
            stat[2] = jnp.maximum(stat[2], jnp.max(u))

    l_ref[...] = to_log(sums[...], slots.shift)

    @pl.when(jnp.logical_not(sums_fine(stat[1], stat[0], stat[2])))
    def _():
        slow_lse(slots, cost_hbm, cost_v, sem, other8, out8, f, l_ref, False)

    if first:
        send_copies(l_ref, copies_ref)
    else:
        send_relative(l_ref, g, log_b, flat, copies_ref)


def label_kernel(total, own, ints, floats, log_a, cost_hbm, k_ref, prev, parts, box, *rest):
    (f, out), rest = (rest[:2] if own else rest[1::-1]), rest[2:]
    acc, l_ref, flat, lab_v, sums, stat, cost_v, other8, out8, sem = rest
    slots = Slots(ints, floats, total)
    classes, width = acc.shape[1], acc.shape[2]
    new_potential(f, log_a, parts, prev, flat)
    sums[...] = jnp.zeros(sums.shape, F32)
    acc[...] = jnp.zeros(acc.shape, F32)
    stat[0] = jnp.float32(0.0)
    stat[1] = jnp.float32(jnp.inf)
    stat[2] = slots.high
    high = classes // 2
    core = slots.src % 2
    half = core if own else 1 - core
    lanes = pl.ds(pl.multiple_of(half * width, width), width)

    def label_piece(block, p):
        at = FLAT[0] + p * high
        both = box[block, at : at + high]
        return jnp.concatenate([both[:, :128], both[:, 128:]], axis=0)

    for s in range(slots.total):

        @pl.when(slots.live[s])
        def _():
            u = jnp.exp2(f[pl.ds(slots.row[s], 1), :] * TO2)
            lab = jnp.concatenate([label_piece(slots.row[s], p) for p in range(INNER)], axis=1)
            weighted = lab.astype(F32) * u
            hi = weighted.astype(BF16)
            low = (weighted - hi.astype(F32)).astype(BF16)
            res = k_col(jnp.concatenate([hi, low, split_rows(u)], axis=0), k_ref[s, :, lanes])
            part = jnp.sum(res[2 * classes :], axis=0, keepdims=True)
            at = pl.ds(slots.col[s], 1)
            sums[at, :] = sums[at, :] + part
            acc[slots.col[s]] = acc[slots.col[s]] + (res[:classes] + res[classes : 2 * classes])
            stat[0] = jnp.maximum(stat[0], jnp.max(part))
            stat[1] = jnp.minimum(stat[1], jnp.min(part))
            stat[2] = jnp.maximum(stat[2], jnp.max(u))

    l_ref[...] = to_log(sums[...], slots.shift)

    @pl.when(jnp.logical_not(sums_fine(stat[1], stat[0], stat[2])))
    def _():
        chunks = width // 128
        slow_lse(slots, cost_hbm, cost_v, sem, other8, out8, f, l_ref, False, half * chunks)
        acc[...] = jnp.zeros(acc.shape, F32)
        sums[...] = jnp.ones(sums.shape, F32)
        for s in range(slots.total):

            @pl.when(slots.live[s])
            def _():
                copy = pltpu.make_async_copy(cost_hbm.at[0, s], cost_v, sem)
                copy.start()
                copy.wait()
                chunked(f[pl.ds(slots.row[s], 1), :], other8)
                chunked(l_ref[pl.ds(slots.col[s], 1), :], out8)
                for p in range(INNER):
                    lab_v[p] = label_piece(slots.row[s], p)

                @pl.loop(0, chunks * INNER)
                def _(ij):
                    i, j = ij // INNER, ij % INNER
                    here = pl.ds(pl.multiple_of(i * 128, 128), 128)
                    z = tile_z(cost_v, slots.scale[s], other8, half * chunks + i, j, False)
                    p = jnp.exp(z - out8[pl.ds(i, 1), :]).astype(BF16)
                    term = jnp.dot(lab_v[j], p, preferred_element_type=F32)
                    acc[slots.col[s], :, here] = acc[slots.col[s], :, here] + term

    for c in range(acc.shape[0]):
        mass = sums[c : c + 1, :]
        out[c, :classes] = acc[c] * jnp.where(mass > 0, 1.0 / jnp.maximum(mass, 1e-38), 0.0)
        out[c, classes:] = jnp.broadcast_to(l_ref[c : c + 1, :], (8, width))


def merge_kernel(keep, got, *outs):
    src = lax.axis_index("src")
    classes = keep.shape[1] - 8
    for q, out in enumerate(outs):
        block = (src // 2) ^ q
        mine, other = keep[block], got[block]
        first, second = mine[classes : classes + 1], other[classes : classes + 1]
        both = lse([first, second])
        mean = mine[:classes] * jnp.exp(first - both) + other[:classes] * jnp.exp(second - both)
        out[:classes] = mean.astype(BF16)
        out[classes:] = split_rows(both)


def tail_row(piece):
    return jnp.sum(piece[piece.shape[0] - 16 :].astype(F32), axis=0, keepdims=True)


def combine_kernel(log_b, *rest):
    pieces, out = rest[:-1], rest[-1]
    src = lax.axis_index("src")
    classes, width = out.shape[0] - 16, out.shape[1]
    ls = [tail_row(p[...]) for p in pieces]
    total = lse(ls)
    mass = piece_of(log_b, src, width)
    top = total - mass
    out[:classes] = tree_sum([p[:classes].astype(F32) * jnp.exp(l - top) for p, l in zip(pieces, ls)]).astype(BF16)
    out[classes:] = split_rows(EPS * mass - EPS * total)


def assemble_kernel(order, f, *refs):
    pieces, (f_out, g_out, out, row, f_row) = refs[: len(order)], refs[len(order) :]
    src = lax.axis_index("src")
    classes, width = out.shape[0], pieces[0].shape[1]
    for k, piece in zip(order, pieces):
        here = pl.ds(pl.multiple_of((src ^ k) * width, width), width)
        out[:, here] = piece[:classes]
        row[:, here] = tail_row(piece[...])
    g_out[...] = row[...].reshape(g_out.shape)
    tile = f.shape[1]
    for r in range(f.shape[0]):
        f_row[:, r * tile : (r + 1) * tile] = f[r : r + 1, :]
    f_out[...] = f_row[...].reshape(f_out.shape)


VM = pl.BlockSpec(memory_space=pltpu.VMEM)
SM = pl.BlockSpec(memory_space=pltpu.SMEM)
HB = pl.BlockSpec(memory_space=pltpu.HBM)
PARAMS = pltpu.CompilerParams(vmem_limit_bytes=LIMIT)


def local(cost, cost_scale, slot_block_row, slot_block_column, device_block_count, log_a, log_b, labels):
    n_src, n_tgt = lax.axis_size("src"), lax.axis_size("tgt")
    slots, tile = cost.shape[1], cost.shape[2]
    rb, cb = log_a.shape[0] // tile, log_b.shape[0] // tile
    classes = labels.shape[1]
    dims = (rb, cb, slots)
    in_hbm = functools.partial(pltpu.with_memory_space_constraint, memory_space=pltpu.HBM)
    in_vmem = functools.partial(pltpu.with_memory_space_constraint, memory_space=pltpu.VMEM)
    in_smem = functools.partial(pltpu.with_memory_space_constraint, memory_space=pltpu.SMEM)

    def xor(x, axis, k):
        return lax.ppermute(x, axis, [(i, i ^ k) for i in range(lax.axis_size(axis))])

    def doubled(part, axis):
        k = 1
        while 2 * k < lax.axis_size(axis):
            part = lse([part, xor(part, axis, k)])
            k *= 2
        return [part, xor(part, axis, k)]

    outer = n_tgt // INNER
    along_z = [[x * INNER + z for z in range(INNER)] for x in range(outer)]
    along_x = [[x * INNER + z for x in range(outer)] for z in range(INNER)]

    def everyone(copies, axis, groups=None):
        return lax.all_to_all(copies, axis, 0, 0, axis_index_groups=groups, tiled=True)

    cost = in_hbm(cost)
    vec = functools.partial(jax.ShapeDtypeStruct, dtype=F32)
    sent = functools.partial(jax.ShapeDtypeStruct, dtype=BF16)
    chunks = pltpu.VMEM((tile // 128, 128), F32)
    work = [pltpu.SMEM((3,), F32), pltpu.VMEM((tile, tile), BF16), chunks, chunks, pltpu.SemaphoreType.DMA]
    rows, cols = pltpu.VMEM((rb, tile), F32), pltpu.VMEM((cb, tile), F32)

    k_all, row_l, ints, floats, log_a, log_b = pl.pallas_call(
        functools.partial(build_kernel, dims),
        out_shape=(
            pltpu.VMEM((slots, tile, tile), BF16),
            sent((n_tgt,) + FLAT),
            pltpu.SMEM((1, 2 * slots + 1), jnp.int32),
            pltpu.SMEM((1, slots + 2), F32),
            pltpu.VMEM((rb, tile), F32),
            pltpu.VMEM((cb, tile), F32),
        ),
        in_specs=[SM] + [HB] * 6,
        out_specs=(VM, VM, SM, SM, VM, VM),
        scratch_shapes=[
            rows,
            pltpu.VMEM((slots, tile, tile), BF16),
            rows,
            cols,
            chunks,
            chunks,
            pltpu.SMEM((3,), F32),
            pltpu.SemaphoreType.DMA((slots, tile // PART)),
            pltpu.SMEM((1, slots), F32),
            pltpu.SMEM((1, slots), jnp.int32),
            pltpu.SMEM((1, slots), jnp.int32),
            pltpu.VMEM((rb * tile,), F32),
            pltpu.VMEM((cb * tile,), F32),
            pltpu.SemaphoreType.DMA((5,)),
            pltpu.VMEM((tile, 128), F32),
            pltpu.VMEM(FLAT, F32),
        ],
        compiler_params=PARAMS,
    )(
        device_block_count,
        in_hbm(cost_scale),
        in_hbm(slot_block_row),
        in_hbm(slot_block_column),
        in_hbm(log_a),
        in_hbm(log_b),
        cost,
    )
    k_all, log_a, log_b = in_vmem(k_all), in_vmem(log_a), in_vmem(log_b)
    scalars = (in_smem(ints), in_smem(floats))
    common = [SM] * 2 + [VM, HB, VM]

    flat = pltpu.VMEM(FLAT, F32)
    lab_t = labels.T
    f_pot = g_pot = box = None
    for step in range(ITERS):
        if step == 1:
            along = everyone(row_l, "tgt", along_z)
            high = FLAT[0] + INNER * (along.shape[1] - FLAT[0])
            copies = pl.pallas_call(
                relay_kernel,
                out_shape=sent((outer, high, FLAT[1])),
                in_specs=[VM],
                out_specs=VM,
                compiler_params=PARAMS,
            )(along)
            row_parts = box = everyone(copies, "tgt", along_x)
        else:
            row_parts = everyone(row_l, "tgt")
        if step == ITERS - 1:
            break
        first = step == 0
        col_l, f_pot = pl.pallas_call(
            functools.partial(col_kernel, slots, first),
            out_shape=(vec((n_src, cb, tile)) if first else sent((n_src,) + FLAT), vec((rb, tile))),
            in_specs=common + [VM] * (1 if first else 4),
            out_specs=(VM, VM),
            scratch_shapes=[cols, flat, cols] + work,
            compiler_params=PARAMS,
        )(*scalars, log_a, cost, k_all, row_parts, *(() if first else (f_pot, log_b, g_pot)))
        col_parts = everyone(col_l, "src")
        extra = FLAT[0] * lab_t.size // (FLAT[0] * FLAT[1]) if first else 0
        last = step == ITERS - 2
        row_l, *g_out = pl.pallas_call(
            functools.partial(row_kernel, slots, first),
            out_shape=(sent((INNER if first else n_tgt, FLAT[0] + extra, FLAT[1])), vec((cb, tile)))[: 1 if last else 2],
            in_specs=common + [VM] * 4,
            out_specs=(VM, VM)[: 1 if last else 2],
            scratch_shapes=[cols] * last + [rows, flat, rows] + work,
            compiler_params=PARAMS,
        )(*scalars, log_b, cost, k_all, col_parts, log_a, f_pot, lab_t if first else g_pot)
        g_pot = g_out[0] if g_out else None

    width = cb * tile // n_src
    piece = jax.ShapeDtypeStruct((classes + 16, width), BF16)
    half = vec((cb, classes + 8, width))
    half_cols = pltpu.VMEM((cb, width), F32)

    def label_call(own):
        return pl.pallas_call(
            functools.partial(label_kernel, slots, own),
            out_shape=(vec((rb, tile)), half) if own else (half,),
            in_specs=common + [VM] * 3,
            out_specs=(VM,) * (1 + own),
            scratch_shapes=[rows] * (not own)
            + [
                pltpu.VMEM((cb, classes, width), F32),
                half_cols,
                flat,
                pltpu.VMEM((INNER, classes, 128), BF16),
                half_cols,
            ]
            + work[:3]
            + [pltpu.VMEM((width // 128, 128), F32), work[4]],
            cost_estimate=pl.CostEstimate(
                flops=slots * tile * tile * 150, bytes_accessed=slots * tile * tile, transcendentals=slots * tile
            ),
            compiler_params=PARAMS,
        )(*scalars, log_a, cost, k_all, f_pot, row_parts, box)

    got = xor(label_call(False)[0], "src", 1)
    f_pot, keep = label_call(True)
    n_y = n_src // 2
    pieces = pl.pallas_call(
        merge_kernel,
        out_shape=(piece,) * n_y,
        in_specs=[VM] * 2,
        out_specs=(VM,) * n_y,
        compiler_params=PARAMS,
    )(keep, got)
    far_first = (2, 1, 3)
    pieces = [pieces[0]] + [xor(pieces[q], "src", 2 * q) for q in far_first]
    done = pl.pallas_call(
        combine_kernel,
        out_shape=piece,
        in_specs=[VM] * (1 + n_y),
        out_specs=VM,
        compiler_params=PARAMS,
    )(log_b, *pieces)
    pieces = [done] + [xor(done, "src", 2 * q) for q in far_first]
    pieces = pieces + [xor(p, "src", 1) for p in pieces]
    order = (0,) + tuple(2 * q for q in far_first)
    order = order + tuple(k + 1 for k in order)
    f_pot, g_pot, out = pl.pallas_call(
        functools.partial(assemble_kernel, order),
        out_shape=(vec((rb * tile,)), vec((cb * tile,)), jax.ShapeDtypeStruct((classes, cb * tile), BF16)),
        in_specs=[VM] * (1 + n_src),
        out_specs=(VM,) * 3,
        scratch_shapes=[pltpu.VMEM((1, cb * tile), F32), pltpu.VMEM((1, rb * tile), F32)],
        compiler_params=PARAMS,
    )(f_pot, *pieces)
    return f_pot, g_pot, out.T


def solution(mesh):
    in_specs = (
        P("src", "tgt", None, None),
        P("src", "tgt"),
        P("src", "tgt"),
        P("src", "tgt"),
        P("src", "tgt"),
        P("src"),
        P("tgt"),
        P(("src", "tgt"), None),
    )
    out_specs = (P("src"), P("tgt"), P("tgt", None))
    return jax.shard_map(local, mesh=mesh, in_specs=in_specs, out_specs=out_specs, check_vma=False)
```

```python
import functools

import jax
import jax.numpy as jnp
from jax import lax
from jax.experimental import pallas as pl
from jax.experimental.pallas import tpu as pltpu
from jax.sharding import PartitionSpec as P

ITERS = 4
EPS = 0.5
NEG = -1e30
LOG2E = 1.4426950408889634
TO2 = LOG2E / EPS
PART = 256
INNER = 8
MIDDLE = 116.0
FLAT = (16, 256)
LIMIT = 40 * 1024 * 1024
F32, BF16 = jnp.float32, jnp.bfloat16


def tree_sum(parts):
    while len(parts) > 1:
        parts = [a + b for a, b in zip(parts[0::2], parts[1::2])]
    return parts[0]


def lse(parts):
    top = functools.reduce(jnp.maximum, parts)
    return top + jnp.log(tree_sum([jnp.exp(p - top) for p in parts]))


class Slots:
    def __init__(self, ints, floats, total):
        self.total = total
        self.row = [ints[0, s] for s in range(total)]
        self.col = [ints[0, total + s] for s in range(total)]
        self.count = ints[0, 2 * total]
        self.live = [s < self.count for s in range(total)]
        self.scale = [floats[0, s] for s in range(total)]
        self.shift, self.high = floats[0, total], floats[0, total + 1]
        self.src, self.tgt = lax.axis_index("src"), lax.axis_index("tgt")


def split_rows(x):
    x = jnp.broadcast_to(x, (16, x.shape[1]))
    hi = x.astype(BF16).astype(F32)
    rest = x - hi
    mid = rest.astype(BF16).astype(F32)
    low = (rest - mid).astype(BF16).astype(F32)
    at = lax.broadcasted_iota(jnp.int32, x.shape, 0)
    zero = jnp.zeros_like(x)
    return jnp.where(at == 0, hi, jnp.where(at == 1, mid, jnp.where(at == 2, low, zero))).astype(BF16)


def k_row(lhs, k_block):
    return lax.dot_general(lhs, k_block, (((1,), (1,)), ((), ())), preferred_element_type=F32)


def fold_lanes(x):
    return tree_sum([x[:, c * 128 : (c + 1) * 128] for c in range(x.shape[1] // 128)])


def fold_rows(tall):
    wide = tall[...]
    hi = wide.astype(BF16)
    low = (wide - hi.astype(F32)).astype(BF16)
    ones = jnp.ones((16, 128), BF16)
    return (k_row(ones, hi) + k_row(ones, low))[0:1]


def k_col(lhs, k_block):
    return lax.dot_general(lhs, k_block, (((1,), (0,)), ((), ())), preferred_element_type=F32)


def chunked(row, out_ref):
    for c in range(out_ref.shape[0]):
        out_ref[c : c + 1, :] = row[:, c * 128 : (c + 1) * 128]


def tile_z(cost_v, scale, other8, out_chunk, red_chunk, rows_mode):
    mine = pl.ds(pl.multiple_of(out_chunk * 128, 128), 128)
    summed = pl.ds(pl.multiple_of(red_chunk * 128, 128), 128)
    other = jnp.broadcast_to(other8[pl.ds(red_chunk, 1), :], (128, 128)).T
    if rows_mode:
        tile = cost_v[mine, summed].astype(F32).T
    else:
        tile = cost_v[summed, mine].astype(F32)
    return (other - scale * tile) / EPS


def slow_lse(slots, cost_hbm, cost_v, sem, other8, out8, other_ref, l_ref, rows_mode, start=0):
    l_ref[...] = jnp.full(l_ref.shape, NEG, F32)
    chunks, out_chunks = other8.shape[0], out8.shape[0]
    for s in range(slots.total):
        out_at, other_at = (slots.row[s], slots.col[s]) if rows_mode else (slots.col[s], slots.row[s])

        @pl.when(slots.live[s])
        def _():
            copy = pltpu.make_async_copy(cost_hbm.at[0, s], cost_v, sem)
            copy.start()
            copy.wait()
            chunked(other_ref[pl.ds(other_at, 1), :], other8)

            @pl.loop(0, out_chunks)
            def _(i):
                def step(j, carry):
                    m, total = carry
                    z = tile_z(cost_v, slots.scale[s], other8, start + i, j, rows_mode)
                    top = jnp.maximum(m, jnp.max(z, axis=0, keepdims=True))
                    total = total * jnp.exp(m - top) + jnp.sum(jnp.exp(z - top), axis=0, keepdims=True)
                    return top, total

                first = (jnp.full((1, 128), NEG, F32), jnp.zeros((1, 128), F32))
                m, total = lax.fori_loop(0, chunks, step, first)
                out8[pl.ds(i, 1), :] = m + jnp.log(total)

            new = jnp.concatenate([out8[c : c + 1, :] for c in range(out_chunks)], axis=1)
            old = l_ref[pl.ds(out_at, 1), :]
            top = jnp.maximum(old, new)
            l_ref[pl.ds(out_at, 1), :] = top + jnp.log(jnp.exp(old - top) + jnp.exp(new - top))


def piece_of(ref, piece, width):
    per = ref.shape[1] // width
    row = ref[pl.ds(piece // per, 1), :]
    out = row[:, :width]
    for c in range(1, per):
        out = jnp.where(piece % per == c, row[:, c * width : (c + 1) * width], out)
    return out


def to_log(total, shift):
    return jnp.where(total > 0, jnp.log(jnp.maximum(total, 1e-38)) - shift / EPS, NEG)


def send_copies(l_ref, copies_ref):
    for k in range(copies_ref.shape[0]):
        copies_ref[k] = l_ref[...]


def send_flat(x, flat, copies_ref):
    count, width = x.shape[0], flat.shape[1]
    for c in range(x.shape[1] // width):
        flat[c * count : (c + 1) * count, :] = x[:, c * width : (c + 1) * width]
    x = flat[...].astype(BF16)
    for k in range(copies_ref.shape[0]):
        copies_ref[k, : flat.shape[0]] = x


def send_relative(l_ref, pot, log_mass, flat, copies_ref):
    send_flat(jnp.exp(l_ref[...] + pot[...] / EPS - log_mass[...]), flat, copies_ref)


def new_potential(out, log_mass, parts, prev, flat):
    if parts.dtype == F32:
        out[...] = EPS * log_mass[...] - EPS * lse([parts[k] for k in range(parts.shape[0])])
        return
    parts = [parts[k, : flat.shape[0]].astype(F32) for k in range(parts.shape[0])]
    if prev is None:
        top = functools.reduce(jnp.maximum, parts)
        inv = 1.0 / top
        flat[...] = MIDDLE + 2.0 * jnp.log(top) + jnp.log(tree_sum([(p * inv) * (p * inv) for p in parts]))
    else:
        flat[...] = jnp.log(tree_sum(parts))
    count, width = out.shape[0], flat.shape[1]
    for c in range(out.shape[1] // width):
        here = slice(c * width, (c + 1) * width)
        base = EPS * log_mass[:, here] if prev is None else prev[:, here]
        out[:, here] = base - EPS * flat[c * count : (c + 1) * count, :]


def clear_stat(stat):
    stat[0:1, :] = jnp.zeros((1, stat.shape[1]), F32)
    stat[1:2, :] = jnp.full((1, stat.shape[1]), jnp.inf, F32)
    stat[2:3, :] = jnp.zeros((1, stat.shape[1]), F32)


def note_stat(stat, part, other=None):
    here = slice(0, part.shape[1])
    stat[0:1, here] = jnp.maximum(stat[0:1, here], jnp.where(part <= 2.0**100, part, jnp.inf))
    stat[1:2, here] = jnp.minimum(stat[1:2, here], part)
    if other is not None:
        stat[2:3, :] = jnp.maximum(stat[2:3, :], other)


def sums_fine(stat, high=None):
    top = jnp.max(stat[0:1, :], axis=1, keepdims=True)
    low = jnp.min(stat[1:2, :], axis=1, keepdims=True)
    others = top if high is None else jnp.maximum(jnp.max(stat[2:3, :], axis=1, keepdims=True), high)
    fine = (low >= 2.0**-80 * jnp.maximum(others, 1.0)) & (top <= 2.0**100)
    return jnp.max(jnp.where(fine, 0.0, 1.0)) < 0.5


def build_kernel(
    dims, count, scale_hbm, row_hbm, col_hbm, a_hbm, b_hbm, cost_hbm,
    k_ref, copies_ref, ints, floats, a_ref, b_ref,
    l_ref, cost_v, sums, zero, other8, out8, stat, sems,
    scale, row, col, log_a, log_b, small_sems, tall, flat,
):
    rb, cb, total = dims
    small = [
        pltpu.make_async_copy(a, b, small_sems.at[i])
        for i, (a, b) in enumerate(
            ((scale_hbm, scale), (row_hbm, row), (col_hbm, col), (a_hbm, log_a), (b_hbm, log_b))
        )
    ]
    parts = cost_v.shape[1] // PART
    copies = [
        [
            pltpu.make_async_copy(
                cost_hbm.at[0, s, pl.ds(h * PART, PART)], cost_v.at[s, pl.ds(h * PART, PART)], sems.at[s, h]
            )
            for h in range(parts)
        ]
        for s in range(total)
    ]
    copies[0][0].start()
    for copy in small:
        copy.start()
    for s in range(total):

        @pl.when(s < count[0, 0])
        def _():
            for h in range(0 if s else 1, parts):
                copies[s][h].start()

    for copy in small[:3]:
        copy.wait()
    src, tgt = lax.axis_index("src"), lax.axis_index("tgt")
    for s in range(total):
        ints[0, s] = row[0, s] - src * rb
        ints[0, total + s] = col[0, s] - tgt * cb
        floats[0, s] = scale[0, s]
    ints[0, 2 * total] = count[0, 0]
    slots = Slots(ints, floats, total)
    chunk, tile = 16, cost_v.shape[2]

    def build(shift, wait):
        sums[...] = jnp.zeros(sums.shape, F32)
        floats[0, total] = jnp.float32(0.0) if shift is None else shift
        clear_stat(stat)
        for s in range(total):

            @pl.when(slots.live[s])
            def _():
                for h in range(parts):
                    if wait:
                        copies[s][h].wait()

                    @pl.loop(0, PART // chunk, unroll=4)
                    def _(i):
                        here = pl.ds(pl.multiple_of(h * PART + i * chunk, chunk), chunk)
                        x = cost_v[s, here, :].astype(F32) * (-TO2 * slots.scale[s])
                        if shift is not None:
                            x = x + shift * TO2
                        e = jnp.exp2(x)
                        k_ref[s, here, :] = e.astype(BF16)
                        tall[here, :] = fold_lanes(e)

                part = fold_rows(tall)
                at = pl.ds(slots.row[s], 1)
                sums[at, :] = sums[at, :] + part
                note_stat(stat, part)

        l_ref[...] = to_log(sums[...], floats[0, total])
        floats[0, total + 1] = jnp.max(stat[0:1, :])
        return sums_fine(stat)

    fine = build(None, True)
    for copy in small[3:]:
        copy.wait()
    for r in range(rb):
        a_ref[r : r + 1, :] = log_a[r * tile : (r + 1) * tile].reshape(1, tile)
    for c in range(cb):
        b_ref[c : c + 1, :] = log_b[c * tile : (c + 1) * tile].reshape(1, tile)

    @pl.when(jnp.logical_not(fine))
    def _():
        floats[0, total] = jnp.float32(jnp.inf)
        for s in range(total):

            @pl.when(slots.live[s])
            def _():
                def lowest(i, low):
                    here = pl.ds(pl.multiple_of(i * chunk, chunk), chunk)
                    return jnp.minimum(low, jnp.min(cost_v[s, here, :].astype(F32)))

                low = lax.fori_loop(0, tile // chunk, lowest, jnp.float32(jnp.inf))
                floats[0, total] = jnp.minimum(floats[0, total], low * slots.scale[s])

        shifted = build(floats[0, total], False)

        @pl.when(jnp.logical_not(shifted))
        def _():
            zero[...] = jnp.zeros(zero.shape, F32)
            slow_lse(slots, cost_hbm, cost_v.at[0], sems.at[0, 0], other8, out8, zero, l_ref, True)

    send_flat(jnp.exp((l_ref[...] - MIDDLE) / 2), flat, copies_ref)


def row_kernel(total, first, ints, floats, log_b, cost_hbm, k_ref, parts, log_a, f, *rest):
    prev, lab = (None, rest[0]) if first else (rest[0], None)
    rest = rest[1:]
    copies_ref, g, l_ref, flat, sums, stat, cost_v, other8, out8, sem = rest
    slots = Slots(ints, floats, total)
    new_potential(g, log_b, parts, prev, flat)
    sums[...] = jnp.zeros(sums.shape, F32)
    clear_stat(stat)
    for s in range(slots.total):

        @pl.when(slots.live[s])
        def _():
            v = jnp.exp2(g[pl.ds(slots.col[s], 1), :] * TO2)
            part = jnp.sum(k_row(split_rows(v), k_ref[s]), axis=0, keepdims=True)
            at = pl.ds(slots.row[s], 1)
            sums[at, :] = sums[at, :] + part
            note_stat(stat, part, v)

    l_ref[...] = to_log(sums[...], slots.shift)

    @pl.when(jnp.logical_not(sums_fine(stat, slots.high)))
    def _():
        slow_lse(slots, cost_hbm, cost_v, sem, other8, out8, g, l_ref, True)

    send_relative(l_ref, f, log_a, flat, copies_ref)
    if first:
        half = lab.shape[0] // 2
        for k in range(copies_ref.shape[0]):
            copies_ref[k, flat.shape[0] :] = jnp.concatenate([lab[:half], lab[half:]], axis=1)


def relay_kernel(parts, out):
    rows, count = FLAT[0], parts.shape[0]
    total = tree_sum([parts[k, :rows].astype(F32) for k in range(count)]).astype(BF16)
    high = parts.shape[1] - rows
    for k in range(out.shape[0]):
        out[k, :rows] = total
        for p in range(count):
            out[k, rows + p * high : rows + (p + 1) * high] = parts[p, rows:]


def col_kernel(total, first, ints, floats, log_a, cost_hbm, k_ref, parts, *rest):
    (prev, log_b, g), rest = ((None, None, None), rest) if first else (rest[:3], rest[3:])
    copies_ref, f, l_ref, flat, sums, stat, cost_v, other8, out8, sem = rest
    slots = Slots(ints, floats, total)
    new_potential(f, log_a, parts, prev, flat)
    sums[...] = jnp.zeros(sums.shape, F32)
    clear_stat(stat)
    for s in range(slots.total):

        @pl.when(slots.live[s])
        def _():
            u = jnp.exp2(f[pl.ds(slots.row[s], 1), :] * TO2)
            part = jnp.sum(k_col(split_rows(u), k_ref[s]), axis=0, keepdims=True)
            at = pl.ds(slots.col[s], 1)
            sums[at, :] = sums[at, :] + part
            note_stat(stat, part, u)

    l_ref[...] = to_log(sums[...], slots.shift)

    @pl.when(jnp.logical_not(sums_fine(stat, slots.high)))
    def _():
        slow_lse(slots, cost_hbm, cost_v, sem, other8, out8, f, l_ref, False)

    if first:
        send_copies(l_ref, copies_ref)
    else:
        send_relative(l_ref, g, log_b, flat, copies_ref)


def label_kernel(total, own, ints, floats, log_a, cost_hbm, k_ref, prev, parts, box, *rest):
    (f, out), rest = (rest[:2] if own else rest[1::-1]), rest[2:]
    acc, l_ref, flat, lab_v, sums, stat, cost_v, other8, out8, sem = rest
    slots = Slots(ints, floats, total)
    classes, width = acc.shape[1], acc.shape[2]
    new_potential(f, log_a, parts, prev, flat)
    sums[...] = jnp.zeros(sums.shape, F32)
    acc[...] = jnp.zeros(acc.shape, F32)
    clear_stat(stat)
    high = classes // 2
    core = slots.src % 2
    half = core if own else 1 - core
    lanes = pl.ds(pl.multiple_of(half * width, width), width)

    def label_piece(block, p):
        at = FLAT[0] + p * high
        both = box[block, at : at + high]
        return jnp.concatenate([both[:, :128], both[:, 128:]], axis=0)

    for s in range(slots.total):

        @pl.when(slots.live[s])
        def _():
            u = jnp.exp2(f[pl.ds(slots.row[s], 1), :] * TO2)
            lab = jnp.concatenate([label_piece(slots.row[s], p) for p in range(INNER)], axis=1)
            weighted = lab.astype(F32) * u
            hi = weighted.astype(BF16)
            low = (weighted - hi.astype(F32)).astype(BF16)
            res = k_col(jnp.concatenate([hi, low, split_rows(u)], axis=0), k_ref[s, :, lanes])
            part = jnp.sum(res[2 * classes :], axis=0, keepdims=True)
            at = pl.ds(slots.col[s], 1)
            sums[at, :] = sums[at, :] + part
            acc[slots.col[s]] = acc[slots.col[s]] + (res[:classes] + res[classes : 2 * classes])
            note_stat(stat, part, u)

    l_ref[...] = to_log(sums[...], slots.shift)

    @pl.when(jnp.logical_not(sums_fine(stat, slots.high)))
    def _():
        chunks = width // 128
        slow_lse(slots, cost_hbm, cost_v, sem, other8, out8, f, l_ref, False, half * chunks)
        acc[...] = jnp.zeros(acc.shape, F32)
        sums[...] = jnp.ones(sums.shape, F32)
        for s in range(slots.total):

            @pl.when(slots.live[s])
            def _():
                copy = pltpu.make_async_copy(cost_hbm.at[0, s], cost_v, sem)
                copy.start()
                copy.wait()
                chunked(f[pl.ds(slots.row[s], 1), :], other8)
                chunked(l_ref[pl.ds(slots.col[s], 1), :], out8)
                for p in range(INNER):
                    lab_v[p] = label_piece(slots.row[s], p)

                @pl.loop(0, chunks * INNER)
                def _(ij):
                    i, j = ij // INNER, ij % INNER
                    here = pl.ds(pl.multiple_of(i * 128, 128), 128)
                    z = tile_z(cost_v, slots.scale[s], other8, half * chunks + i, j, False)
                    p = jnp.exp(z - out8[pl.ds(i, 1), :]).astype(BF16)
                    term = jnp.dot(lab_v[j], p, preferred_element_type=F32)
                    acc[slots.col[s], :, here] = acc[slots.col[s], :, here] + term

    for c in range(acc.shape[0]):
        mass = sums[c : c + 1, :]
        out[c, :classes] = acc[c] * jnp.where(mass > 0, 1.0 / jnp.maximum(mass, 1e-38), 0.0)
        out[c, classes:] = jnp.broadcast_to(l_ref[c : c + 1, :], (8, width))


def merge_kernel(keep, got, *outs):
    src = lax.axis_index("src")
    classes = keep.shape[1] - 8
    for q, out in enumerate(outs):
        block = (src // 2) ^ q
        mine, other = keep[block], got[block]
        first, second = mine[classes : classes + 1], other[classes : classes + 1]
        both = lse([first, second])
        mean = mine[:classes] * jnp.exp(first - both) + other[:classes] * jnp.exp(second - both)
        out[:classes] = mean.astype(BF16)
        out[classes:] = split_rows(both)


def tail_row(piece):
    return jnp.sum(piece[piece.shape[0] - 16 :].astype(F32), axis=0, keepdims=True)


def combine_kernel(log_b, *rest):
    pieces, out = rest[:-1], rest[-1]
    src = lax.axis_index("src")
    classes, width = out.shape[0] - 16, out.shape[1]
    ls = [tail_row(p[...]) for p in pieces]
    total = lse(ls)
    mass = piece_of(log_b, src, width)
    top = total - mass
    out[:classes] = tree_sum([p[:classes].astype(F32) * jnp.exp(l - top) for p, l in zip(pieces, ls)]).astype(BF16)
    out[classes:] = split_rows(EPS * mass - EPS * total)


def assemble_kernel(order, f, *refs):
    pieces, (f_out, g_out, out, row, f_row) = refs[: len(order)], refs[len(order) :]
    src = lax.axis_index("src")
    classes, width = out.shape[0], pieces[0].shape[1]
    for k, piece in zip(order, pieces):
        here = pl.ds(pl.multiple_of((src ^ k) * width, width), width)
        out[:, here] = piece[:classes]
        row[:, here] = tail_row(piece[...])
    g_out[...] = row[...].reshape(g_out.shape)
    tile = f.shape[1]
    for r in range(f.shape[0]):
        f_row[:, r * tile : (r + 1) * tile] = f[r : r + 1, :]
    f_out[...] = f_row[...].reshape(f_out.shape)


VM = pl.BlockSpec(memory_space=pltpu.VMEM)
SM = pl.BlockSpec(memory_space=pltpu.SMEM)
HB = pl.BlockSpec(memory_space=pltpu.HBM)
PARAMS = pltpu.CompilerParams(vmem_limit_bytes=LIMIT)


def local(cost, cost_scale, slot_block_row, slot_block_column, device_block_count, log_a, log_b, labels):
    n_src, n_tgt = lax.axis_size("src"), lax.axis_size("tgt")
    slots, tile = cost.shape[1], cost.shape[2]
    rb, cb = log_a.shape[0] // tile, log_b.shape[0] // tile
    classes = labels.shape[1]
    dims = (rb, cb, slots)
    in_hbm = functools.partial(pltpu.with_memory_space_constraint, memory_space=pltpu.HBM)
    in_vmem = functools.partial(pltpu.with_memory_space_constraint, memory_space=pltpu.VMEM)
    in_smem = functools.partial(pltpu.with_memory_space_constraint, memory_space=pltpu.SMEM)

    def xor(x, axis, k):
        return lax.ppermute(x, axis, [(i, i ^ k) for i in range(lax.axis_size(axis))])

    def doubled(part, axis):
        k = 1
        while 2 * k < lax.axis_size(axis):
            part = lse([part, xor(part, axis, k)])
            k *= 2
        return [part, xor(part, axis, k)]

    outer = n_tgt // INNER
    along_z = [[x * INNER + z for z in range(INNER)] for x in range(outer)]
    along_x = [[x * INNER + z for x in range(outer)] for z in range(INNER)]

    def everyone(copies, axis, groups=None):
        return lax.all_to_all(copies, axis, 0, 0, axis_index_groups=groups, tiled=True)

    cost = in_hbm(cost)
    vec = functools.partial(jax.ShapeDtypeStruct, dtype=F32)
    sent = functools.partial(jax.ShapeDtypeStruct, dtype=BF16)
    chunks = pltpu.VMEM((tile // 128, 128), F32)
    work = [pltpu.VMEM((3, tile), F32), pltpu.VMEM((tile, tile), BF16), chunks, chunks, pltpu.SemaphoreType.DMA]
    rows, cols = pltpu.VMEM((rb, tile), F32), pltpu.VMEM((cb, tile), F32)

    k_all, row_l, ints, floats, log_a, log_b = pl.pallas_call(
        functools.partial(build_kernel, dims),
        out_shape=(
            pltpu.VMEM((slots, tile, tile), BF16),
            sent((n_tgt,) + FLAT),
            pltpu.SMEM((1, 2 * slots + 1), jnp.int32),
            pltpu.SMEM((1, slots + 2), F32),
            pltpu.VMEM((rb, tile), F32),
            pltpu.VMEM((cb, tile), F32),
        ),
        in_specs=[SM] + [HB] * 6,
        out_specs=(VM, VM, SM, SM, VM, VM),
        scratch_shapes=[
            rows,
            pltpu.VMEM((slots, tile, tile), BF16),
            rows,
            cols,
            chunks,
            chunks,
            pltpu.VMEM((3, tile), F32),
            pltpu.SemaphoreType.DMA((slots, tile // PART)),
            pltpu.SMEM((1, slots), F32),
            pltpu.SMEM((1, slots), jnp.int32),
            pltpu.SMEM((1, slots), jnp.int32),
            pltpu.VMEM((rb * tile,), F32),
            pltpu.VMEM((cb * tile,), F32),
            pltpu.SemaphoreType.DMA((5,)),
            pltpu.VMEM((tile, 128), F32),
            pltpu.VMEM(FLAT, F32),
        ],
        compiler_params=PARAMS,
    )(
        device_block_count,
        in_hbm(cost_scale),
        in_hbm(slot_block_row),
        in_hbm(slot_block_column),
        in_hbm(log_a),
        in_hbm(log_b),
        cost,
    )
    k_all, log_a, log_b = in_vmem(k_all), in_vmem(log_a), in_vmem(log_b)
    scalars = (in_smem(ints), in_smem(floats))
    common = [SM] * 2 + [VM, HB, VM]

    flat = pltpu.VMEM(FLAT, F32)
    lab_t = labels.T
    f_pot = g_pot = box = None
    for step in range(ITERS):
        if step == 1:
            along = everyone(row_l, "tgt", along_z)
            high = FLAT[0] + INNER * (along.shape[1] - FLAT[0])
            copies = pl.pallas_call(
                relay_kernel,
                out_shape=sent((outer, high, FLAT[1])),
                in_specs=[VM],
                out_specs=VM,
                compiler_params=PARAMS,
            )(along)
            row_parts = box = everyone(copies, "tgt", along_x)
        else:
            row_parts = everyone(row_l, "tgt")
        if step == ITERS - 1:
            break
        first = step == 0
        col_l, f_pot = pl.pallas_call(
            functools.partial(col_kernel, slots, first),
            out_shape=(vec((n_src, cb, tile)) if first else sent((n_src,) + FLAT), vec((rb, tile))),
            in_specs=common + [VM] * (1 if first else 4),
            out_specs=(VM, VM),
            scratch_shapes=[cols, flat, cols] + work,
            compiler_params=PARAMS,
        )(*scalars, log_a, cost, k_all, row_parts, *(() if first else (f_pot, log_b, g_pot)))
        col_parts = everyone(col_l, "src")
        extra = FLAT[0] * lab_t.size // (FLAT[0] * FLAT[1]) if first else 0
        last = step == ITERS - 2
        row_l, *g_out = pl.pallas_call(
            functools.partial(row_kernel, slots, first),
            out_shape=(sent((INNER if first else n_tgt, FLAT[0] + extra, FLAT[1])), vec((cb, tile)))[: 1 if last else 2],
            in_specs=common + [VM] * 4,
            out_specs=(VM, VM)[: 1 if last else 2],
            scratch_shapes=[cols] * last + [rows, flat, rows] + work,
            compiler_params=PARAMS,
        )(*scalars, log_b, cost, k_all, col_parts, log_a, f_pot, lab_t if first else g_pot)
        g_pot = g_out[0] if g_out else None

    width = cb * tile // n_src
    piece = jax.ShapeDtypeStruct((classes + 16, width), BF16)
    half = vec((cb, classes + 8, width))
    half_cols = pltpu.VMEM((cb, width), F32)

    def label_call(own):
        return pl.pallas_call(
            functools.partial(label_kernel, slots, own),
            out_shape=(vec((rb, tile)), half) if own else (half,),
            in_specs=common + [VM] * 3,
            out_specs=(VM,) * (1 + own),
            scratch_shapes=[rows] * (not own)
            + [
                pltpu.VMEM((cb, classes, width), F32),
                half_cols,
                flat,
                pltpu.VMEM((INNER, classes, 128), BF16),
                half_cols,
            ]
            + work[:3]
            + [pltpu.VMEM((width // 128, 128), F32), work[4]],
            cost_estimate=pl.CostEstimate(
                flops=slots * tile * tile * 150, bytes_accessed=slots * tile * tile, transcendentals=slots * tile
            ),
            compiler_params=PARAMS,
        )(*scalars, log_a, cost, k_all, f_pot, row_parts, box)

    got = xor(label_call(False)[0], "src", 1)
    f_pot, keep = label_call(True)
    n_y = n_src // 2
    pieces = pl.pallas_call(
        merge_kernel,
        out_shape=(piece,) * n_y,
        in_specs=[VM] * 2,
        out_specs=(VM,) * n_y,
        compiler_params=PARAMS,
    )(keep, got)
    far_first = (2, 1, 3)
    pieces = [pieces[0]] + [xor(pieces[q], "src", 2 * q) for q in far_first]
    done = pl.pallas_call(
        combine_kernel,
        out_shape=piece,
        in_specs=[VM] * (1 + n_y),
        out_specs=VM,
        compiler_params=PARAMS,
    )(log_b, *pieces)
    pieces = [done] + [xor(done, "src", 2 * q) for q in far_first]
    pieces = pieces + [xor(p, "src", 1) for p in pieces]
    order = (0,) + tuple(2 * q for q in far_first)
    order = order + tuple(k + 1 for k in order)
    f_pot, g_pot, out = pl.pallas_call(
        functools.partial(assemble_kernel, order),
        out_shape=(vec((rb * tile,)), vec((cb * tile,)), jax.ShapeDtypeStruct((classes, cb * tile), BF16)),
        in_specs=[VM] * (1 + n_src),
        out_specs=(VM,) * 3,
        scratch_shapes=[pltpu.VMEM((1, cb * tile), F32), pltpu.VMEM((1, rb * tile), F32)],
        compiler_params=PARAMS,
    )(f_pot, *pieces)
    return f_pot, g_pot, out.T


def solution(mesh):
    in_specs = (
        P("src", "tgt", None, None),
        P("src", "tgt"),
        P("src", "tgt"),
        P("src", "tgt"),
        P("src", "tgt"),
        P("src"),
        P("tgt"),
        P(("src", "tgt"), None),
    )
    out_specs = (P("src"), P("tgt"), P("tgt", None))
    return jax.shard_map(local, mesh=mesh, in_specs=in_specs, out_specs=out_specs, check_vma=False)
```

```python
import functools

import jax
import jax.numpy as jnp
from jax import lax
from jax.experimental import pallas as pl
from jax.experimental.pallas import tpu as pltpu
from jax.sharding import PartitionSpec as P

ITERS = 4
EPS = 0.5
NEG = -1e30
LOG2E = 1.4426950408889634
TO2 = LOG2E / EPS
PART = 256
INNER = 8
MIDDLE = 116.0
FLAT = (16, 256)
LIMIT = 40 * 1024 * 1024
F32, BF16 = jnp.float32, jnp.bfloat16


def tree_sum(parts):
    while len(parts) > 1:
        parts = [a + b for a, b in zip(parts[0::2], parts[1::2])]
    return parts[0]


def lse(parts):
    top = functools.reduce(jnp.maximum, parts)
    return top + jnp.log(tree_sum([jnp.exp(p - top) for p in parts]))


class Slots:
    def __init__(self, ints, floats, total):
        self.total = total
        self.row = [ints[0, s] for s in range(total)]
        self.col = [ints[0, total + s] for s in range(total)]
        self.count = ints[0, 2 * total]
        self.live = [s < self.count for s in range(total)]
        self.scale = [floats[0, s] for s in range(total)]
        self.shift, self.high = floats[0, total], floats[0, total + 1]
        self.src, self.tgt = lax.axis_index("src"), lax.axis_index("tgt")


def split_rows(x):
    x = jnp.broadcast_to(x, (16, x.shape[1]))
    hi = x.astype(BF16).astype(F32)
    rest = x - hi
    mid = rest.astype(BF16).astype(F32)
    low = (rest - mid).astype(BF16).astype(F32)
    at = lax.broadcasted_iota(jnp.int32, x.shape, 0)
    zero = jnp.zeros_like(x)
    return jnp.where(at == 0, hi, jnp.where(at == 1, mid, jnp.where(at == 2, low, zero))).astype(BF16)


def k_row(lhs, k_block):
    return lax.dot_general(lhs, k_block, (((1,), (1,)), ((), ())), preferred_element_type=F32)


def fold_lanes(x):
    return tree_sum([x[:, c * 128 : (c + 1) * 128] for c in range(x.shape[1] // 128)])


def fold_rows(tall):
    wide = tall[...]
    hi = wide.astype(BF16)
    low = (wide - hi.astype(F32)).astype(BF16)
    ones = jnp.ones((16, 128), BF16)
    return (k_row(ones, hi) + k_row(ones, low))[0:1]


def k_col(lhs, k_block):
    return lax.dot_general(lhs, k_block, (((1,), (0,)), ((), ())), preferred_element_type=F32)


def chunked(row, out_ref):
    for c in range(out_ref.shape[0]):
        out_ref[c : c + 1, :] = row[:, c * 128 : (c + 1) * 128]


def tile_z(cost_v, scale, other8, out_chunk, red_chunk, rows_mode):
    mine = pl.ds(pl.multiple_of(out_chunk * 128, 128), 128)
    summed = pl.ds(pl.multiple_of(red_chunk * 128, 128), 128)
    other = jnp.broadcast_to(other8[pl.ds(red_chunk, 1), :], (128, 128)).T
    if rows_mode:
        tile = cost_v[mine, summed].astype(F32).T
    else:
        tile = cost_v[summed, mine].astype(F32)
    return (other - scale * tile) / EPS


def slow_lse(slots, cost_hbm, cost_v, sem, other8, out8, other_ref, l_ref, rows_mode, start=0):
    l_ref[...] = jnp.full(l_ref.shape, NEG, F32)
    chunks, out_chunks = other8.shape[0], out8.shape[0]
    for s in range(slots.total):
        out_at, other_at = (slots.row[s], slots.col[s]) if rows_mode else (slots.col[s], slots.row[s])

        @pl.when(slots.live[s])
        def _():
            copy = pltpu.make_async_copy(cost_hbm.at[0, s], cost_v, sem)
            copy.start()
            copy.wait()
            chunked(other_ref[pl.ds(other_at, 1), :], other8)

            @pl.loop(0, out_chunks)
            def _(i):
                def step(j, carry):
                    m, total = carry
                    z = tile_z(cost_v, slots.scale[s], other8, start + i, j, rows_mode)
                    top = jnp.maximum(m, jnp.max(z, axis=0, keepdims=True))
                    total = total * jnp.exp(m - top) + jnp.sum(jnp.exp(z - top), axis=0, keepdims=True)
                    return top, total

                first = (jnp.full((1, 128), NEG, F32), jnp.zeros((1, 128), F32))
                m, total = lax.fori_loop(0, chunks, step, first)
                out8[pl.ds(i, 1), :] = m + jnp.log(total)

            new = jnp.concatenate([out8[c : c + 1, :] for c in range(out_chunks)], axis=1)
            old = l_ref[pl.ds(out_at, 1), :]
            top = jnp.maximum(old, new)
            l_ref[pl.ds(out_at, 1), :] = top + jnp.log(jnp.exp(old - top) + jnp.exp(new - top))


def piece_of(ref, piece, width):
    per = ref.shape[1] // width
    row = ref[pl.ds(piece // per, 1), :]
    out = row[:, :width]
    for c in range(1, per):
        out = jnp.where(piece % per == c, row[:, c * width : (c + 1) * width], out)
    return out


def to_log(total, shift):
    return jnp.where(total > 0, jnp.log(jnp.maximum(total, 1e-38)) - shift / EPS, NEG)


def send_copies(l_ref, copies_ref):
    for k in range(copies_ref.shape[0]):
        copies_ref[k] = l_ref[...]


def send_flat(x, flat, copies_ref):
    count, width = x.shape[0], flat.shape[1]
    for c in range(x.shape[1] // width):
        flat[c * count : (c + 1) * count, :] = x[:, c * width : (c + 1) * width]
    x = flat[...].astype(BF16)
    for k in range(copies_ref.shape[0]):
        copies_ref[k, : flat.shape[0]] = x


def send_relative(l_ref, pot, log_mass, flat, copies_ref):
    send_flat(jnp.exp(l_ref[...] + pot[...] / EPS - log_mass[...]), flat, copies_ref)


def new_potential(out, log_mass, parts, prev, flat):
    if parts.dtype == F32:
        out[...] = EPS * log_mass[...] - EPS * lse([parts[k] for k in range(parts.shape[0])])
        return
    parts = [parts[k, : flat.shape[0]].astype(F32) for k in range(parts.shape[0])]
    if prev is None:
        top = functools.reduce(jnp.maximum, parts)
        inv = 1.0 / top
        flat[...] = MIDDLE + 2.0 * jnp.log(top) + jnp.log(tree_sum([(p * inv) * (p * inv) for p in parts]))
    else:
        flat[...] = jnp.log(tree_sum(parts))
    count, width = out.shape[0], flat.shape[1]
    for c in range(out.shape[1] // width):
        here = slice(c * width, (c + 1) * width)
        base = EPS * log_mass[:, here] if prev is None else prev[:, here]
        out[:, here] = base - EPS * flat[c * count : (c + 1) * count, :]


def clear_stat(stat):
    stat[0:1, :] = jnp.zeros((1, stat.shape[1]), F32)
    stat[1:2, :] = jnp.full((1, stat.shape[1]), jnp.inf, F32)
    stat[2:3, :] = jnp.zeros((1, stat.shape[1]), F32)


def note_stat(stat, part, other=None):
    here = slice(0, part.shape[1])
    stat[0:1, here] = jnp.maximum(stat[0:1, here], jnp.where(part <= 2.0**100, part, jnp.inf))
    stat[1:2, here] = jnp.minimum(stat[1:2, here], part)
    if other is not None:
        stat[2:3, :] = jnp.maximum(stat[2:3, :], other)


def sums_fine(stat, high=None):
    top = jnp.max(stat[0:1, :], axis=1, keepdims=True)
    low = jnp.min(stat[1:2, :], axis=1, keepdims=True)
    others = top if high is None else jnp.maximum(jnp.max(stat[2:3, :], axis=1, keepdims=True), high)
    fine = (low >= 2.0**-80 * jnp.maximum(others, 1.0)) & (top <= 2.0**100)
    return jnp.max(jnp.where(fine, 0.0, 1.0)) < 0.5


def build_kernel(
    dims, count, scale_hbm, row_hbm, col_hbm, a_hbm, b_hbm, cost_hbm,
    k_ref, copies_ref, ints, floats, a_ref, b_ref,
    l_ref, cost_v, sums, zero, other8, out8, stat, sems,
    scale, row, col, log_a, log_b, small_sems, tall, flat,
):
    rb, cb, total = dims
    small = [
        pltpu.make_async_copy(a, b, small_sems.at[i])
        for i, (a, b) in enumerate(
            ((scale_hbm, scale), (row_hbm, row), (col_hbm, col), (a_hbm, log_a), (b_hbm, log_b))
        )
    ]
    parts = cost_v.shape[1] // PART
    copies = [
        [
            pltpu.make_async_copy(
                cost_hbm.at[0, s, pl.ds(h * PART, PART)], cost_v.at[s, pl.ds(h * PART, PART)], sems.at[s, h]
            )
            for h in range(parts)
        ]
        for s in range(total)
    ]
    copies[0][0].start()
    for copy in small:
        copy.start()
    for s in range(total):

        @pl.when(s < count[0, 0])
        def _():
            for h in range(0 if s else 1, parts):
                copies[s][h].start()

    for copy in small[:3]:
        copy.wait()
    src, tgt = lax.axis_index("src"), lax.axis_index("tgt")
    for s in range(total):
        ints[0, s] = row[0, s] - src * rb
        ints[0, total + s] = col[0, s] - tgt * cb
        floats[0, s] = scale[0, s]
    ints[0, 2 * total] = count[0, 0]
    slots = Slots(ints, floats, total)
    chunk, tile = 16, cost_v.shape[2]

    def build(shift, wait):
        sums[...] = jnp.zeros(sums.shape, F32)
        floats[0, total] = jnp.float32(0.0) if shift is None else shift
        clear_stat(stat)
        for s in range(total):

            @pl.when(slots.live[s])
            def _():
                for h in range(parts):
                    if wait:
                        copies[s][h].wait()

                    @pl.loop(0, PART // chunk, unroll=4)
                    def _(i):
                        here = pl.ds(pl.multiple_of(h * PART + i * chunk, chunk), chunk)
                        x = cost_v[s, here, :].astype(F32) * (-TO2 * slots.scale[s])
                        if shift is not None:
                            x = x + shift * TO2
                        e = jnp.exp2(x)
                        k_ref[s, here, :] = e.astype(BF16)
                        tall[here, :] = fold_lanes(e)

                part = fold_rows(tall)
                at = pl.ds(slots.row[s], 1)
                sums[at, :] = sums[at, :] + part
                note_stat(stat, part)

        l_ref[...] = to_log(sums[...], floats[0, total])
        floats[0, total + 1] = jnp.max(stat[0:1, :])
        return sums_fine(stat)

    fine = build(None, True)
    for copy in small[3:]:
        copy.wait()
    for r in range(rb):
        a_ref[r : r + 1, :] = log_a[r * tile : (r + 1) * tile].reshape(1, tile)
    for c in range(cb):
        b_ref[c : c + 1, :] = log_b[c * tile : (c + 1) * tile].reshape(1, tile)

    @pl.when(jnp.logical_not(fine))
    def _():
        floats[0, total] = jnp.float32(jnp.inf)
        for s in range(total):

            @pl.when(slots.live[s])
            def _():
                def lowest(i, low):
                    here = pl.ds(pl.multiple_of(i * chunk, chunk), chunk)
                    return jnp.minimum(low, jnp.min(cost_v[s, here, :].astype(F32)))

                low = lax.fori_loop(0, tile // chunk, lowest, jnp.float32(jnp.inf))
                floats[0, total] = jnp.minimum(floats[0, total], low * slots.scale[s])

        shifted = build(floats[0, total], False)

        @pl.when(jnp.logical_not(shifted))
        def _():
            zero[...] = jnp.zeros(zero.shape, F32)
            slow_lse(slots, cost_hbm, cost_v.at[0], sems.at[0, 0], other8, out8, zero, l_ref, True)

    send_flat(jnp.exp((l_ref[...] - MIDDLE) / 2), flat, copies_ref)


def row_kernel(total, first, ints, floats, log_b, cost_hbm, k_ref, parts, log_a, f, *rest):
    prev, lab = (None, rest[0]) if first else (rest[0], None)
    rest = rest[1:]
    copies_ref, g, l_ref, flat, sums, stat, cost_v, other8, out8, sem = rest
    slots = Slots(ints, floats, total)
    new_potential(g, log_b, parts, prev, flat)
    sums[...] = jnp.zeros(sums.shape, F32)
    clear_stat(stat)
    for s in range(slots.total):

        @pl.when(slots.live[s])
        def _():
            v = jnp.exp2(g[pl.ds(slots.col[s], 1), :] * TO2)
            part = jnp.sum(k_row(split_rows(v), k_ref[s]), axis=0, keepdims=True)
            at = pl.ds(slots.row[s], 1)
            sums[at, :] = sums[at, :] + part
            note_stat(stat, part, v)

    l_ref[...] = to_log(sums[...], slots.shift)

    @pl.when(jnp.logical_not(sums_fine(stat, slots.high)))
    def _():
        slow_lse(slots, cost_hbm, cost_v, sem, other8, out8, g, l_ref, True)

    send_relative(l_ref, f, log_a, flat, copies_ref)
    if first:
        half = lab.shape[0] // 2
        for k in range(copies_ref.shape[0]):
            copies_ref[k, flat.shape[0] :] = jnp.concatenate([lab[:half], lab[half:]], axis=1)


def relay_kernel(parts, out):
    rows, count = FLAT[0], parts.shape[0]
    total = tree_sum([parts[k, :rows].astype(F32) for k in range(count)]).astype(BF16)
    high = parts.shape[1] - rows
    for k in range(out.shape[0]):
        out[k, :rows] = total
        for p in range(count):
            out[k, rows + p * high : rows + (p + 1) * high] = parts[p, rows:]


def col_kernel(total, first, ints, floats, log_a, cost_hbm, k_ref, parts, *rest):
    (prev, log_b, g), rest = ((None, None, None), rest) if first else (rest[:3], rest[3:])
    copies_ref, f, l_ref, flat, sums, stat, cost_v, other8, out8, sem = rest
    slots = Slots(ints, floats, total)
    new_potential(f, log_a, parts, prev, flat)
    sums[...] = jnp.zeros(sums.shape, F32)
    clear_stat(stat)
    for s in range(slots.total):

        @pl.when(slots.live[s])
        def _():
            u = jnp.exp2(f[pl.ds(slots.row[s], 1), :] * TO2)
            part = jnp.sum(k_col(split_rows(u), k_ref[s]), axis=0, keepdims=True)
            at = pl.ds(slots.col[s], 1)
            sums[at, :] = sums[at, :] + part
            note_stat(stat, part, u)

    l_ref[...] = to_log(sums[...], slots.shift)

    @pl.when(jnp.logical_not(sums_fine(stat, slots.high)))
    def _():
        slow_lse(slots, cost_hbm, cost_v, sem, other8, out8, f, l_ref, False)

    if first:
        send_copies(l_ref, copies_ref)
    else:
        send_relative(l_ref, g, log_b, flat, copies_ref)


def label_kernel(total, own, ints, floats, log_a, cost_hbm, k_ref, prev, parts, box, *rest):
    (f, out), rest = (rest[:2] if own else rest[1::-1]), rest[2:]
    acc, l_ref, flat, lab_v, sums, stat, cost_v, other8, out8, sem = rest
    slots = Slots(ints, floats, total)
    classes, width = acc.shape[1], acc.shape[2]
    new_potential(f, log_a, parts, prev, flat)
    sums[...] = jnp.zeros(sums.shape, F32)
    acc[...] = jnp.zeros(acc.shape, F32)
    clear_stat(stat)
    high = classes // 2
    core = slots.src % 2
    half = core if own else 1 - core
    lanes = pl.ds(pl.multiple_of(half * width, width), width)

    def label_piece(block, p):
        at = FLAT[0] + p * high
        both = box[block, at : at + high]
        return jnp.concatenate([both[:, :128], both[:, 128:]], axis=0)

    for s in range(slots.total):

        @pl.when(slots.live[s])
        def _():
            u = jnp.exp2(f[pl.ds(slots.row[s], 1), :] * TO2)
            lab = jnp.concatenate([label_piece(slots.row[s], p) for p in range(INNER)], axis=1)
            weighted = lab.astype(F32) * u
            hi = weighted.astype(BF16)
            low = (weighted - hi.astype(F32)).astype(BF16)
            res = k_col(jnp.concatenate([hi, low, split_rows(u)], axis=0), k_ref[s, :, lanes])
            part = jnp.sum(res[2 * classes :], axis=0, keepdims=True)
            at = pl.ds(slots.col[s], 1)
            sums[at, :] = sums[at, :] + part
            acc[slots.col[s]] = acc[slots.col[s]] + (res[:classes] + res[classes : 2 * classes])
            note_stat(stat, part, u)

    l_ref[...] = to_log(sums[...], slots.shift)

    @pl.when(jnp.logical_not(sums_fine(stat, slots.high)))
    def _():
        chunks = width // 128
        slow_lse(slots, cost_hbm, cost_v, sem, other8, out8, f, l_ref, False, half * chunks)
        acc[...] = jnp.zeros(acc.shape, F32)
        sums[...] = jnp.ones(sums.shape, F32)
        for s in range(slots.total):

            @pl.when(slots.live[s])
            def _():
                copy = pltpu.make_async_copy(cost_hbm.at[0, s], cost_v, sem)
                copy.start()
                copy.wait()
                chunked(f[pl.ds(slots.row[s], 1), :], other8)
                chunked(l_ref[pl.ds(slots.col[s], 1), :], out8)
                for p in range(INNER):
                    lab_v[p] = label_piece(slots.row[s], p)

                @pl.loop(0, chunks * INNER)
                def _(ij):
                    i, j = ij // INNER, ij % INNER
                    here = pl.ds(pl.multiple_of(i * 128, 128), 128)
                    z = tile_z(cost_v, slots.scale[s], other8, half * chunks + i, j, False)
                    p = jnp.exp(z - out8[pl.ds(i, 1), :]).astype(BF16)
                    term = jnp.dot(lab_v[j], p, preferred_element_type=F32)
                    acc[slots.col[s], :, here] = acc[slots.col[s], :, here] + term

    for c in range(acc.shape[0]):
        mass = sums[c : c + 1, :]
        out[c, :classes] = acc[c] * jnp.where(mass > 0, 1.0 / jnp.maximum(mass, 1e-38), 0.0)
        out[c, classes:] = jnp.broadcast_to(l_ref[c : c + 1, :], (8, width))


def merge_kernel(keep, got, *outs):
    src = lax.axis_index("src")
    classes = keep.shape[1] - 8
    for q, out in enumerate(outs):
        block = (src // 2) ^ q
        mine, other = keep[block], got[block]
        first, second = mine[classes : classes + 1], other[classes : classes + 1]
        both = lse([first, second])
        mean = mine[:classes] * jnp.exp(first - both) + other[:classes] * jnp.exp(second - both)
        out[:classes] = mean.astype(BF16)
        out[classes:] = split_rows(both)


def tail_row(piece):
    return jnp.sum(piece[piece.shape[0] - 16 :].astype(F32), axis=0, keepdims=True)


def combine_kernel(log_b, *rest):
    pieces, out = rest[:-1], rest[-1]
    src = lax.axis_index("src")
    classes, width = out.shape[0] - 16, out.shape[1]
    ls = [tail_row(p[...]) for p in pieces]
    total = lse(ls)
    mass = piece_of(log_b, src, width)
    top = total - mass
    out[:classes] = tree_sum([p[:classes].astype(F32) * jnp.exp(l - top) for p, l in zip(pieces, ls)]).astype(BF16)
    out[classes:] = split_rows(EPS * mass - EPS * total)


def assemble_kernel(order, f, *refs):
    pieces, (f_out, g_out, out, row, f_row) = refs[: len(order)], refs[len(order) :]
    src = lax.axis_index("src")
    classes, width = out.shape[0], pieces[0].shape[1]
    for k, piece in zip(order, pieces):
        here = pl.ds(pl.multiple_of((src ^ k) * width, width), width)
        out[:, here] = piece[:classes]
        row[:, here] = tail_row(piece[...])
    g_out[...] = row[...].reshape(g_out.shape)
    tile = f.shape[1]
    for r in range(f.shape[0]):
        f_row[:, r * tile : (r + 1) * tile] = f[r : r + 1, :]
    f_out[...] = f_row[...].reshape(f_out.shape)


VM = pl.BlockSpec(memory_space=pltpu.VMEM)
SM = pl.BlockSpec(memory_space=pltpu.SMEM)
HB = pl.BlockSpec(memory_space=pltpu.HBM)
PARAMS = pltpu.CompilerParams(vmem_limit_bytes=LIMIT)


def local(cost, cost_scale, slot_block_row, slot_block_column, device_block_count, log_a, log_b, labels):
    n_src, n_tgt = lax.axis_size("src"), lax.axis_size("tgt")
    slots, tile = cost.shape[1], cost.shape[2]
    rb, cb = log_a.shape[0] // tile, log_b.shape[0] // tile
    classes = labels.shape[1]
    dims = (rb, cb, slots)
    in_hbm = functools.partial(pltpu.with_memory_space_constraint, memory_space=pltpu.HBM)
    in_vmem = functools.partial(pltpu.with_memory_space_constraint, memory_space=pltpu.VMEM)
    in_smem = functools.partial(pltpu.with_memory_space_constraint, memory_space=pltpu.SMEM)

    def xor(x, axis, k):
        return lax.ppermute(x, axis, [(i, i ^ k) for i in range(lax.axis_size(axis))])

    def doubled(part, axis):
        k = 1
        while 2 * k < lax.axis_size(axis):
            part = lse([part, xor(part, axis, k)])
            k *= 2
        return [part, xor(part, axis, k)]

    outer = n_tgt // INNER
    along_z = [[x * INNER + z for z in range(INNER)] for x in range(outer)]
    along_x = [[x * INNER + z for x in range(outer)] for z in range(INNER)]

    def everyone(copies, axis, groups=None):
        return lax.all_to_all(copies, axis, 0, 0, axis_index_groups=groups, tiled=True)

    cost = in_hbm(cost)
    vec = functools.partial(jax.ShapeDtypeStruct, dtype=F32)
    sent = functools.partial(jax.ShapeDtypeStruct, dtype=BF16)
    chunks = pltpu.VMEM((tile // 128, 128), F32)
    work = [pltpu.VMEM((3, tile), F32), pltpu.VMEM((tile, tile), BF16), chunks, chunks, pltpu.SemaphoreType.DMA]
    rows, cols = pltpu.VMEM((rb, tile), F32), pltpu.VMEM((cb, tile), F32)

    k_all, row_l, ints, floats, log_a, log_b = pl.pallas_call(
        functools.partial(build_kernel, dims),
        out_shape=(
            pltpu.VMEM((slots, tile, tile), BF16),
            sent((n_tgt,) + FLAT),
            pltpu.SMEM((1, 2 * slots + 1), jnp.int32),
            pltpu.SMEM((1, slots + 2), F32),
            pltpu.VMEM((rb, tile), F32),
            pltpu.VMEM((cb, tile), F32),
        ),
        in_specs=[SM] + [HB] * 6,
        out_specs=(VM, VM, SM, SM, VM, VM),
        scratch_shapes=[
            rows,
            pltpu.VMEM((slots, tile, tile), BF16),
            rows,
            cols,
            chunks,
            chunks,
            pltpu.VMEM((3, tile), F32),
            pltpu.SemaphoreType.DMA((slots, tile // PART)),
            pltpu.SMEM((1, slots), F32),
            pltpu.SMEM((1, slots), jnp.int32),
            pltpu.SMEM((1, slots), jnp.int32),
            pltpu.VMEM((rb * tile,), F32),
            pltpu.VMEM((cb * tile,), F32),
            pltpu.SemaphoreType.DMA((5,)),
            pltpu.VMEM((tile, 128), F32),
            pltpu.VMEM(FLAT, F32),
        ],
        compiler_params=PARAMS,
    )(
        device_block_count,
        in_hbm(cost_scale),
        in_hbm(slot_block_row),
        in_hbm(slot_block_column),
        in_hbm(log_a),
        in_hbm(log_b),
        cost,
    )
    k_all, log_a, log_b = in_vmem(k_all), in_vmem(log_a), in_vmem(log_b)
    scalars = (in_smem(ints), in_smem(floats))
    common = [SM] * 2 + [VM, HB, VM]

    flat = pltpu.VMEM(FLAT, F32)
    lab_t = labels.T
    f_pot = g_pot = box = None
    for step in range(ITERS):
        if step == 1:
            along = everyone(row_l, "tgt", along_z)
            high = FLAT[0] + INNER * (along.shape[1] - FLAT[0])
            copies = pl.pallas_call(
                relay_kernel,
                out_shape=sent((outer, high, FLAT[1])),
                in_specs=[VM],
                out_specs=VM,
                compiler_params=PARAMS,
            )(along)
            row_parts = box = everyone(copies, "tgt", along_x)
        else:
            row_parts = everyone(row_l, "tgt")
        if step == ITERS - 1:
            break
        first = step == 0
        col_l, f_pot = pl.pallas_call(
            functools.partial(col_kernel, slots, first),
            out_shape=(vec((n_src, cb, tile)) if first else sent((n_src,) + FLAT), vec((rb, tile))),
            in_specs=common + [VM] * (1 if first else 4),
            out_specs=(VM, VM),
            scratch_shapes=[cols, flat, cols] + work,
            compiler_params=PARAMS,
        )(*scalars, log_a, cost, k_all, row_parts, *(() if first else (f_pot, log_b, g_pot)))
        col_parts = everyone(col_l, "src")
        extra = FLAT[0] * lab_t.size // (FLAT[0] * FLAT[1]) if first else 0
        last = step == ITERS - 2
        row_l, *g_out = pl.pallas_call(
            functools.partial(row_kernel, slots, first),
            out_shape=(sent((INNER if first else n_tgt, FLAT[0] + extra, FLAT[1])), vec((cb, tile)))[: 1 if last else 2],
            in_specs=common + [VM] * 4,
            out_specs=(VM, VM)[: 1 if last else 2],
            scratch_shapes=[cols] * last + [rows, flat, rows] + work,
            compiler_params=PARAMS,
        )(*scalars, log_b, cost, k_all, col_parts, log_a, f_pot, lab_t if first else g_pot)
        g_pot = g_out[0] if g_out else None

    width = cb * tile // n_src
    piece = jax.ShapeDtypeStruct((classes + 16, width), BF16)
    half = vec((cb, classes + 8, width))
    half_cols = pltpu.VMEM((cb, width), F32)

    def label_call(own):
        return pl.pallas_call(
            functools.partial(label_kernel, slots, own),
            out_shape=(vec((rb, tile)), half) if own else (half,),
            in_specs=common + [VM] * 3,
            out_specs=(VM,) * (1 + own),
            scratch_shapes=[rows] * (not own)
            + [
                pltpu.VMEM((cb, classes, width), F32),
                half_cols,
                flat,
                pltpu.VMEM((INNER, classes, 128), BF16),
                half_cols,
            ]
            + work[:3]
            + [pltpu.VMEM((width // 128, 128), F32), work[4]],
            cost_estimate=pl.CostEstimate(
                flops=slots * tile * tile * 150, bytes_accessed=slots * tile * tile, transcendentals=slots * tile
            ),
            compiler_params=PARAMS,
        )(*scalars, log_a, cost, k_all, f_pot, row_parts, box)

    got = xor(label_call(False)[0], "src", 1)
    f_pot, keep = label_call(True)
    n_y = n_src // 2
    pieces = pl.pallas_call(
        merge_kernel,
        out_shape=(piece,) * n_y,
        in_specs=[VM] * 2,
        out_specs=(VM,) * n_y,
        compiler_params=PARAMS,
    )(keep, got)
    far_first = (2, 1, 3)
    pieces = [pieces[0]] + [xor(pieces[q], "src", 2 * q) for q in far_first]
    done = pl.pallas_call(
        combine_kernel,
        out_shape=piece,
        in_specs=[VM] * (1 + n_y),
        out_specs=VM,
        compiler_params=PARAMS,
    )(log_b, *pieces)
    pieces = [done] + [xor(done, "src", 2 * q) for q in far_first]
    straight = xor(done, "src", 2 * far_first[-1] + 1)
    pieces = pieces + [xor(p, "src", 1) for p in pieces[:-1]] + [straight]
    order = (0,) + tuple(2 * q for q in far_first)
    order = order + tuple(k + 1 for k in order)
    f_pot, g_pot, out = pl.pallas_call(
        functools.partial(assemble_kernel, order),
        out_shape=(vec((rb * tile,)), vec((cb * tile,)), jax.ShapeDtypeStruct((classes, cb * tile), BF16)),
        in_specs=[VM] * (1 + n_src),
        out_specs=(VM,) * 3,
        scratch_shapes=[pltpu.VMEM((1, cb * tile), F32), pltpu.VMEM((1, rb * tile), F32)],
        compiler_params=PARAMS,
    )(f_pot, *pieces)
    return f_pot, g_pot, out.T


def solution(mesh):
    in_specs = (
        P("src", "tgt", None, None),
        P("src", "tgt"),
        P("src", "tgt"),
        P("src", "tgt"),
        P("src", "tgt"),
        P("src"),
        P("tgt"),
        P(("src", "tgt"), None),
    )
    out_specs = (P("src"), P("tgt"), P("tgt", None))
    return jax.shard_map(local, mesh=mesh, in_specs=in_specs, out_specs=out_specs, check_vma=False)
```

```python
import functools

import jax
import jax.numpy as jnp
from jax import lax
from jax.experimental import pallas as pl
from jax.experimental.pallas import tpu as pltpu
from jax.sharding import PartitionSpec as P

ITERS = 4
EPS = 0.5
NEG = -1e30
LOG2E = 1.4426950408889634
TO2 = LOG2E / EPS
PART = 256
INNER = 8
MIDDLE = 116.0
MIDDLE_COL = -130.0
FLAT = (16, 256)
LIMIT = 40 * 1024 * 1024
F32, BF16 = jnp.float32, jnp.bfloat16


def tree_sum(parts):
    while len(parts) > 1:
        parts = [a + b for a, b in zip(parts[0::2], parts[1::2])]
    return parts[0]


def lse(parts):
    top = functools.reduce(jnp.maximum, parts)
    return top + jnp.log(tree_sum([jnp.exp(p - top) for p in parts]))


class Slots:
    def __init__(self, ints, floats, total):
        self.total = total
        self.row = [ints[0, s] for s in range(total)]
        self.col = [ints[0, total + s] for s in range(total)]
        self.count = ints[0, 2 * total]
        self.live = [s < self.count for s in range(total)]
        self.scale = [floats[0, s] for s in range(total)]
        self.shift, self.high = floats[0, total], floats[0, total + 1]
        self.src, self.tgt = lax.axis_index("src"), lax.axis_index("tgt")


def split_rows(x):
    x = jnp.broadcast_to(x, (16, x.shape[1]))
    hi = x.astype(BF16).astype(F32)
    rest = x - hi
    mid = rest.astype(BF16).astype(F32)
    low = (rest - mid).astype(BF16).astype(F32)
    at = lax.broadcasted_iota(jnp.int32, x.shape, 0)
    zero = jnp.zeros_like(x)
    return jnp.where(at == 0, hi, jnp.where(at == 1, mid, jnp.where(at == 2, low, zero))).astype(BF16)


def k_row(lhs, k_block):
    return lax.dot_general(lhs, k_block, (((1,), (1,)), ((), ())), preferred_element_type=F32)


def fold_lanes(x):
    return tree_sum([x[:, c * 128 : (c + 1) * 128] for c in range(x.shape[1] // 128)])


def fold_rows(tall):
    wide = tall[...]
    hi = wide.astype(BF16)
    low = (wide - hi.astype(F32)).astype(BF16)
    ones = jnp.ones((16, 128), BF16)
    return (k_row(ones, hi) + k_row(ones, low))[0:1]


def k_col(lhs, k_block):
    return lax.dot_general(lhs, k_block, (((1,), (0,)), ((), ())), preferred_element_type=F32)


def chunked(row, out_ref):
    for c in range(out_ref.shape[0]):
        out_ref[c : c + 1, :] = row[:, c * 128 : (c + 1) * 128]


def tile_z(cost_v, scale, other8, out_chunk, red_chunk, rows_mode):
    mine = pl.ds(pl.multiple_of(out_chunk * 128, 128), 128)
    summed = pl.ds(pl.multiple_of(red_chunk * 128, 128), 128)
    other = jnp.broadcast_to(other8[pl.ds(red_chunk, 1), :], (128, 128)).T
    if rows_mode:
        tile = cost_v[mine, summed].astype(F32).T
    else:
        tile = cost_v[summed, mine].astype(F32)
    return (other - scale * tile) / EPS


def slow_lse(slots, cost_hbm, cost_v, sem, other8, out8, other_ref, l_ref, rows_mode, start=0):
    l_ref[...] = jnp.full(l_ref.shape, NEG, F32)
    chunks, out_chunks = other8.shape[0], out8.shape[0]
    for s in range(slots.total):
        out_at, other_at = (slots.row[s], slots.col[s]) if rows_mode else (slots.col[s], slots.row[s])

        @pl.when(slots.live[s])
        def _():
            copy = pltpu.make_async_copy(cost_hbm.at[0, s], cost_v, sem)
            copy.start()
            copy.wait()
            chunked(other_ref[pl.ds(other_at, 1), :], other8)

            @pl.loop(0, out_chunks)
            def _(i):
                def step(j, carry):
                    m, total = carry
                    z = tile_z(cost_v, slots.scale[s], other8, start + i, j, rows_mode)
                    top = jnp.maximum(m, jnp.max(z, axis=0, keepdims=True))
                    total = total * jnp.exp(m - top) + jnp.sum(jnp.exp(z - top), axis=0, keepdims=True)
                    return top, total

                first = (jnp.full((1, 128), NEG, F32), jnp.zeros((1, 128), F32))
                m, total = lax.fori_loop(0, chunks, step, first)
                out8[pl.ds(i, 1), :] = m + jnp.log(total)

            new = jnp.concatenate([out8[c : c + 1, :] for c in range(out_chunks)], axis=1)
            old = l_ref[pl.ds(out_at, 1), :]
            top = jnp.maximum(old, new)
            l_ref[pl.ds(out_at, 1), :] = top + jnp.log(jnp.exp(old - top) + jnp.exp(new - top))


def piece_of(ref, piece, width):
    per = ref.shape[1] // width
    row = ref[pl.ds(piece // per, 1), :]
    out = row[:, :width]
    for c in range(1, per):
        out = jnp.where(piece % per == c, row[:, c * width : (c + 1) * width], out)
    return out


def to_log(total, shift):
    return jnp.where(total > 0, jnp.log(jnp.maximum(total, 1e-38)) - shift / EPS, NEG)


def send_flat(x, flat, copies_ref):
    count, width = x.shape[0], flat.shape[1]
    for c in range(x.shape[1] // width):
        flat[c * count : (c + 1) * count, :] = x[:, c * width : (c + 1) * width]
    x = flat[...].astype(BF16)
    for k in range(copies_ref.shape[0]):
        copies_ref[k, : flat.shape[0]] = x


def send_relative(l_ref, pot, log_mass, flat, copies_ref):
    send_flat(jnp.exp(l_ref[...] + pot[...] / EPS - log_mass[...]), flat, copies_ref)


def new_potential(out, log_mass, parts, prev, flat, middle=MIDDLE):
    parts = [parts[k, : flat.shape[0]].astype(F32) for k in range(parts.shape[0])]
    if prev is None:
        top = functools.reduce(jnp.maximum, parts)
        inv = 1.0 / top
        flat[...] = middle + 2.0 * jnp.log(top) + jnp.log(tree_sum([(p * inv) * (p * inv) for p in parts]))
    else:
        flat[...] = jnp.log(tree_sum(parts))
    count, width = out.shape[0], flat.shape[1]
    for c in range(out.shape[1] // width):
        here = slice(c * width, (c + 1) * width)
        base = EPS * log_mass[:, here] if prev is None else prev[:, here]
        out[:, here] = base - EPS * flat[c * count : (c + 1) * count, :]


def clear_stat(stat):
    stat[0:1, :] = jnp.zeros((1, stat.shape[1]), F32)
    stat[1:2, :] = jnp.full((1, stat.shape[1]), jnp.inf, F32)
    stat[2:3, :] = jnp.zeros((1, stat.shape[1]), F32)


def note_stat(stat, part, other=None):
    here = slice(0, part.shape[1])
    stat[0:1, here] = jnp.maximum(stat[0:1, here], jnp.where(part <= 2.0**100, part, jnp.inf))
    stat[1:2, here] = jnp.minimum(stat[1:2, here], part)
    if other is not None:
        stat[2:3, :] = jnp.maximum(stat[2:3, :], other)


def sums_fine(stat, high=None):
    top = jnp.max(stat[0:1, :], axis=1, keepdims=True)
    low = jnp.min(stat[1:2, :], axis=1, keepdims=True)
    others = top if high is None else jnp.maximum(jnp.max(stat[2:3, :], axis=1, keepdims=True), high)
    fine = (low >= 2.0**-80 * jnp.maximum(others, 1.0)) & (top <= 2.0**100)
    return jnp.max(jnp.where(fine, 0.0, 1.0)) < 0.5


def build_kernel(
    dims, count, scale_hbm, row_hbm, col_hbm, a_hbm, b_hbm, cost_hbm,
    k_ref, copies_ref, ints, floats, a_ref, b_ref,
    l_ref, cost_v, sums, zero, other8, out8, stat, sems,
    scale, row, col, log_a, log_b, small_sems, tall, flat,
):
    rb, cb, total = dims
    small = [
        pltpu.make_async_copy(a, b, small_sems.at[i])
        for i, (a, b) in enumerate(
            ((scale_hbm, scale), (row_hbm, row), (col_hbm, col), (a_hbm, log_a), (b_hbm, log_b))
        )
    ]
    parts = cost_v.shape[1] // PART
    copies = [
        [
            pltpu.make_async_copy(
                cost_hbm.at[0, s, pl.ds(h * PART, PART)], cost_v.at[s, pl.ds(h * PART, PART)], sems.at[s, h]
            )
            for h in range(parts)
        ]
        for s in range(total)
    ]
    copies[0][0].start()
    for copy in small:
        copy.start()
    for s in range(total):

        @pl.when(s < count[0, 0])
        def _():
            for h in range(0 if s else 1, parts):
                copies[s][h].start()

    for copy in small[:3]:
        copy.wait()
    src, tgt = lax.axis_index("src"), lax.axis_index("tgt")
    for s in range(total):
        ints[0, s] = row[0, s] - src * rb
        ints[0, total + s] = col[0, s] - tgt * cb
        floats[0, s] = scale[0, s]
    ints[0, 2 * total] = count[0, 0]
    slots = Slots(ints, floats, total)
    chunk, tile = 16, cost_v.shape[2]

    def build(shift, wait):
        sums[...] = jnp.zeros(sums.shape, F32)
        floats[0, total] = jnp.float32(0.0) if shift is None else shift
        clear_stat(stat)
        for s in range(total):

            @pl.when(slots.live[s])
            def _():
                for h in range(parts):
                    if wait:
                        copies[s][h].wait()

                    @pl.loop(0, PART // chunk, unroll=4)
                    def _(i):
                        here = pl.ds(pl.multiple_of(h * PART + i * chunk, chunk), chunk)
                        x = cost_v[s, here, :].astype(F32) * (-TO2 * slots.scale[s])
                        if shift is not None:
                            x = x + shift * TO2
                        e = jnp.exp2(x)
                        k_ref[s, here, :] = e.astype(BF16)
                        tall[here, :] = fold_lanes(e)

                part = fold_rows(tall)
                at = pl.ds(slots.row[s], 1)
                sums[at, :] = sums[at, :] + part
                note_stat(stat, part)

        l_ref[...] = to_log(sums[...], floats[0, total])
        floats[0, total + 1] = jnp.max(stat[0:1, :])
        return sums_fine(stat)

    fine = build(None, True)
    for copy in small[3:]:
        copy.wait()
    for r in range(rb):
        a_ref[r : r + 1, :] = log_a[r * tile : (r + 1) * tile].reshape(1, tile)
    for c in range(cb):
        b_ref[c : c + 1, :] = log_b[c * tile : (c + 1) * tile].reshape(1, tile)

    @pl.when(jnp.logical_not(fine))
    def _():
        floats[0, total] = jnp.float32(jnp.inf)
        for s in range(total):

            @pl.when(slots.live[s])
            def _():
                def lowest(i, low):
                    here = pl.ds(pl.multiple_of(i * chunk, chunk), chunk)
                    return jnp.minimum(low, jnp.min(cost_v[s, here, :].astype(F32)))

                low = lax.fori_loop(0, tile // chunk, lowest, jnp.float32(jnp.inf))
                floats[0, total] = jnp.minimum(floats[0, total], low * slots.scale[s])

        shifted = build(floats[0, total], False)

        @pl.when(jnp.logical_not(shifted))
        def _():
            zero[...] = jnp.zeros(zero.shape, F32)
            slow_lse(slots, cost_hbm, cost_v.at[0], sems.at[0, 0], other8, out8, zero, l_ref, True)

    send_flat(jnp.exp((l_ref[...] - MIDDLE) / 2), flat, copies_ref)


def row_kernel(total, first, ints, floats, log_b, cost_hbm, k_ref, parts, log_a, f, *rest):
    prev, lab = (None, rest[0]) if first else (rest[0], None)
    rest = rest[1:]
    copies_ref, g, l_ref, flat, sums, stat, cost_v, other8, out8, sem = rest
    slots = Slots(ints, floats, total)
    new_potential(g, log_b, parts, prev, flat, MIDDLE_COL)
    sums[...] = jnp.zeros(sums.shape, F32)
    clear_stat(stat)
    for s in range(slots.total):

        @pl.when(slots.live[s])
        def _():
            v = jnp.exp2(g[pl.ds(slots.col[s], 1), :] * TO2)
            part = jnp.sum(k_row(split_rows(v), k_ref[s]), axis=0, keepdims=True)
            at = pl.ds(slots.row[s], 1)
            sums[at, :] = sums[at, :] + part
            note_stat(stat, part, v)

    l_ref[...] = to_log(sums[...], slots.shift)

    @pl.when(jnp.logical_not(sums_fine(stat, slots.high)))
    def _():
        slow_lse(slots, cost_hbm, cost_v, sem, other8, out8, g, l_ref, True)

    send_relative(l_ref, f, log_a, flat, copies_ref)
    if first:
        half = lab.shape[0] // 2
        for k in range(copies_ref.shape[0]):
            copies_ref[k, flat.shape[0] :] = jnp.concatenate([lab[:half], lab[half:]], axis=1)


def relay_kernel(parts, out):
    rows, count = FLAT[0], parts.shape[0]
    total = tree_sum([parts[k, :rows].astype(F32) for k in range(count)]).astype(BF16)
    high = parts.shape[1] - rows
    for k in range(out.shape[0]):
        out[k, :rows] = total
        for p in range(count):
            out[k, rows + p * high : rows + (p + 1) * high] = parts[p, rows:]


def col_kernel(total, first, ints, floats, log_a, cost_hbm, k_ref, parts, *rest):
    (prev, log_b, g), rest = ((None, None, None), rest) if first else (rest[:3], rest[3:])
    copies_ref, f, l_ref, flat, sums, stat, cost_v, other8, out8, sem = rest
    slots = Slots(ints, floats, total)
    new_potential(f, log_a, parts, prev, flat)
    sums[...] = jnp.zeros(sums.shape, F32)
    clear_stat(stat)
    for s in range(slots.total):

        @pl.when(slots.live[s])
        def _():
            u = jnp.exp2(f[pl.ds(slots.row[s], 1), :] * TO2)
            part = jnp.sum(k_col(split_rows(u), k_ref[s]), axis=0, keepdims=True)
            at = pl.ds(slots.col[s], 1)
            sums[at, :] = sums[at, :] + part
            note_stat(stat, part, u)

    l_ref[...] = to_log(sums[...], slots.shift)

    @pl.when(jnp.logical_not(sums_fine(stat, slots.high)))
    def _():
        slow_lse(slots, cost_hbm, cost_v, sem, other8, out8, f, l_ref, False)

    if first:
        send_flat(jnp.exp((l_ref[...] - MIDDLE_COL) / 2), flat, copies_ref)
    else:
        send_relative(l_ref, g, log_b, flat, copies_ref)


def label_kernel(total, own, ints, floats, log_a, cost_hbm, k_ref, prev, parts, box, *rest):
    (f, out), rest = (rest[:2] if own else rest[1::-1]), rest[2:]
    acc, l_ref, flat, lab_v, sums, stat, cost_v, other8, out8, sem = rest
    slots = Slots(ints, floats, total)
    classes, width = acc.shape[1], acc.shape[2]
    new_potential(f, log_a, parts, prev, flat)
    sums[...] = jnp.zeros(sums.shape, F32)
    acc[...] = jnp.zeros(acc.shape, F32)
    clear_stat(stat)
    high = classes // 2
    core = slots.src % 2
    half = core if own else 1 - core
    lanes = pl.ds(pl.multiple_of(half * width, width), width)

    def label_piece(block, p):
        at = FLAT[0] + p * high
        both = box[block, at : at + high]
        return jnp.concatenate([both[:, :128], both[:, 128:]], axis=0)

    for s in range(slots.total):

        @pl.when(slots.live[s])
        def _():
            u = jnp.exp2(f[pl.ds(slots.row[s], 1), :] * TO2)
            lab = jnp.concatenate([label_piece(slots.row[s], p) for p in range(INNER)], axis=1)
            weighted = lab.astype(F32) * u
            hi = weighted.astype(BF16)
            low = (weighted - hi.astype(F32)).astype(BF16)
            res = k_col(jnp.concatenate([hi, low, split_rows(u)], axis=0), k_ref[s, :, lanes])
            part = jnp.sum(res[2 * classes :], axis=0, keepdims=True)
            at = pl.ds(slots.col[s], 1)
            sums[at, :] = sums[at, :] + part
            acc[slots.col[s]] = acc[slots.col[s]] + (res[:classes] + res[classes : 2 * classes])
            note_stat(stat, part, u)

    l_ref[...] = to_log(sums[...], slots.shift)

    @pl.when(jnp.logical_not(sums_fine(stat, slots.high)))
    def _():
        chunks = width // 128
        slow_lse(slots, cost_hbm, cost_v, sem, other8, out8, f, l_ref, False, half * chunks)
        acc[...] = jnp.zeros(acc.shape, F32)
        sums[...] = jnp.ones(sums.shape, F32)
        for s in range(slots.total):

            @pl.when(slots.live[s])
            def _():
                copy = pltpu.make_async_copy(cost_hbm.at[0, s], cost_v, sem)
                copy.start()
                copy.wait()
                chunked(f[pl.ds(slots.row[s], 1), :], other8)
                chunked(l_ref[pl.ds(slots.col[s], 1), :], out8)
                for p in range(INNER):
                    lab_v[p] = label_piece(slots.row[s], p)

                @pl.loop(0, chunks * INNER)
                def _(ij):
                    i, j = ij // INNER, ij % INNER
                    here = pl.ds(pl.multiple_of(i * 128, 128), 128)
                    z = tile_z(cost_v, slots.scale[s], other8, half * chunks + i, j, False)
                    p = jnp.exp(z - out8[pl.ds(i, 1), :]).astype(BF16)
                    term = jnp.dot(lab_v[j], p, preferred_element_type=F32)
                    acc[slots.col[s], :, here] = acc[slots.col[s], :, here] + term

    for c in range(acc.shape[0]):
        mass = sums[c : c + 1, :]
        out[c, :classes] = acc[c] * jnp.where(mass > 0, 1.0 / jnp.maximum(mass, 1e-38), 0.0)
        out[c, classes:] = jnp.broadcast_to(l_ref[c : c + 1, :], (8, width))


def merge_kernel(keep, got, *outs):
    src = lax.axis_index("src")
    classes = keep.shape[1] - 8
    for q, out in enumerate(outs):
        block = (src // 2) ^ q
        mine, other = keep[block], got[block]
        first, second = mine[classes : classes + 1], other[classes : classes + 1]
        both = lse([first, second])
        mean = mine[:classes] * jnp.exp(first - both) + other[:classes] * jnp.exp(second - both)
        out[:classes] = mean.astype(BF16)
        out[classes:] = split_rows(both)


def tail_row(piece):
    return jnp.sum(piece[piece.shape[0] - 16 :].astype(F32), axis=0, keepdims=True)


def combine_kernel(log_b, *rest):
    pieces, out = rest[:-1], rest[-1]
    src = lax.axis_index("src")
    classes, width = out.shape[0] - 16, out.shape[1]
    ls = [tail_row(p[...]) for p in pieces]
    total = lse(ls)
    mass = piece_of(log_b, src, width)
    top = total - mass
    out[:classes] = tree_sum([p[:classes].astype(F32) * jnp.exp(l - top) for p, l in zip(pieces, ls)]).astype(BF16)
    out[classes:] = split_rows(EPS * mass - EPS * total)


def assemble_kernel(order, f, *refs):
    pieces, (f_out, g_out, out, row, f_row) = refs[: len(order)], refs[len(order) :]
    src = lax.axis_index("src")
    classes, width = out.shape[0], pieces[0].shape[1]
    for k, piece in zip(order, pieces):
        here = pl.ds(pl.multiple_of((src ^ k) * width, width), width)
        out[:, here] = piece[:classes]
        row[:, here] = tail_row(piece[...])
    g_out[...] = row[...].reshape(g_out.shape)
    tile = f.shape[1]
    for r in range(f.shape[0]):
        f_row[:, r * tile : (r + 1) * tile] = f[r : r + 1, :]
    f_out[...] = f_row[...].reshape(f_out.shape)


VM = pl.BlockSpec(memory_space=pltpu.VMEM)
SM = pl.BlockSpec(memory_space=pltpu.SMEM)
HB = pl.BlockSpec(memory_space=pltpu.HBM)
PARAMS = pltpu.CompilerParams(vmem_limit_bytes=LIMIT)


def local(cost, cost_scale, slot_block_row, slot_block_column, device_block_count, log_a, log_b, labels):
    n_src, n_tgt = lax.axis_size("src"), lax.axis_size("tgt")
    slots, tile = cost.shape[1], cost.shape[2]
    rb, cb = log_a.shape[0] // tile, log_b.shape[0] // tile
    classes = labels.shape[1]
    dims = (rb, cb, slots)
    in_hbm = functools.partial(pltpu.with_memory_space_constraint, memory_space=pltpu.HBM)
    in_vmem = functools.partial(pltpu.with_memory_space_constraint, memory_space=pltpu.VMEM)
    in_smem = functools.partial(pltpu.with_memory_space_constraint, memory_space=pltpu.SMEM)

    def xor(x, axis, k):
        return lax.ppermute(x, axis, [(i, i ^ k) for i in range(lax.axis_size(axis))])

    def doubled(part, axis):
        k = 1
        while 2 * k < lax.axis_size(axis):
            part = lse([part, xor(part, axis, k)])
            k *= 2
        return [part, xor(part, axis, k)]

    outer = n_tgt // INNER
    along_z = [[x * INNER + z for z in range(INNER)] for x in range(outer)]
    along_x = [[x * INNER + z for x in range(outer)] for z in range(INNER)]

    def everyone(copies, axis, groups=None):
        return lax.all_to_all(copies, axis, 0, 0, axis_index_groups=groups, tiled=True)

    cost = in_hbm(cost)
    vec = functools.partial(jax.ShapeDtypeStruct, dtype=F32)
    sent = functools.partial(jax.ShapeDtypeStruct, dtype=BF16)
    chunks = pltpu.VMEM((tile // 128, 128), F32)
    work = [pltpu.VMEM((3, tile), F32), pltpu.VMEM((tile, tile), BF16), chunks, chunks, pltpu.SemaphoreType.DMA]
    rows, cols = pltpu.VMEM((rb, tile), F32), pltpu.VMEM((cb, tile), F32)

    k_all, row_l, ints, floats, log_a, log_b = pl.pallas_call(
        functools.partial(build_kernel, dims),
        out_shape=(
            pltpu.VMEM((slots, tile, tile), BF16),
            sent((n_tgt,) + FLAT),
            pltpu.SMEM((1, 2 * slots + 1), jnp.int32),
            pltpu.SMEM((1, slots + 2), F32),
            pltpu.VMEM((rb, tile), F32),
            pltpu.VMEM((cb, tile), F32),
        ),
        in_specs=[SM] + [HB] * 6,
        out_specs=(VM, VM, SM, SM, VM, VM),
        scratch_shapes=[
            rows,
            pltpu.VMEM((slots, tile, tile), BF16),
            rows,
            cols,
            chunks,
            chunks,
            pltpu.VMEM((3, tile), F32),
            pltpu.SemaphoreType.DMA((slots, tile // PART)),
            pltpu.SMEM((1, slots), F32),
            pltpu.SMEM((1, slots), jnp.int32),
            pltpu.SMEM((1, slots), jnp.int32),
            pltpu.VMEM((rb * tile,), F32),
            pltpu.VMEM((cb * tile,), F32),
            pltpu.SemaphoreType.DMA((5,)),
            pltpu.VMEM((tile, 128), F32),
            pltpu.VMEM(FLAT, F32),
        ],
        compiler_params=PARAMS,
    )(
        device_block_count,
        in_hbm(cost_scale),
        in_hbm(slot_block_row),
        in_hbm(slot_block_column),
        in_hbm(log_a),
        in_hbm(log_b),
        cost,
    )
    k_all, log_a, log_b = in_vmem(k_all), in_vmem(log_a), in_vmem(log_b)
    scalars = (in_smem(ints), in_smem(floats))
    common = [SM] * 2 + [VM, HB, VM]

    flat = pltpu.VMEM(FLAT, F32)
    lab_t = labels.T
    f_pot = g_pot = box = None
    for step in range(ITERS):
        if step == 1:
            along = everyone(row_l, "tgt", along_z)
            high = FLAT[0] + INNER * (along.shape[1] - FLAT[0])
            copies = pl.pallas_call(
                relay_kernel,
                out_shape=sent((outer, high, FLAT[1])),
                in_specs=[VM],
                out_specs=VM,
                compiler_params=PARAMS,
            )(along)
            row_parts = box = everyone(copies, "tgt", along_x)
        else:
            row_parts = everyone(row_l, "tgt")
        if step == ITERS - 1:
            break
        first = step == 0
        col_l, f_pot = pl.pallas_call(
            functools.partial(col_kernel, slots, first),
            out_shape=(sent((n_src,) + FLAT), vec((rb, tile))),
            in_specs=common + [VM] * (1 if first else 4),
            out_specs=(VM, VM),
            scratch_shapes=[cols, flat, cols] + work,
            compiler_params=PARAMS,
        )(*scalars, log_a, cost, k_all, row_parts, *(() if first else (f_pot, log_b, g_pot)))
        col_parts = everyone(col_l, "src")
        extra = FLAT[0] * lab_t.size // (FLAT[0] * FLAT[1]) if first else 0
        last = step == ITERS - 2
        row_l, *g_out = pl.pallas_call(
            functools.partial(row_kernel, slots, first),
            out_shape=(sent((INNER if first else n_tgt, FLAT[0] + extra, FLAT[1])), vec((cb, tile)))[: 1 if last else 2],
            in_specs=common + [VM] * 4,
            out_specs=(VM, VM)[: 1 if last else 2],
            scratch_shapes=[cols] * last + [rows, flat, rows] + work,
            compiler_params=PARAMS,
        )(*scalars, log_b, cost, k_all, col_parts, log_a, f_pot, lab_t if first else g_pot)
        g_pot = g_out[0] if g_out else None

    width = cb * tile // n_src
    piece = jax.ShapeDtypeStruct((classes + 16, width), BF16)
    half = vec((cb, classes + 8, width))
    half_cols = pltpu.VMEM((cb, width), F32)

    def label_call(own):
        return pl.pallas_call(
            functools.partial(label_kernel, slots, own),
            out_shape=(vec((rb, tile)), half) if own else (half,),
            in_specs=common + [VM] * 3,
            out_specs=(VM,) * (1 + own),
            scratch_shapes=[rows] * (not own)
            + [
                pltpu.VMEM((cb, classes, width), F32),
                half_cols,
                flat,
                pltpu.VMEM((INNER, classes, 128), BF16),
                half_cols,
            ]
            + work[:3]
            + [pltpu.VMEM((width // 128, 128), F32), work[4]],
            cost_estimate=pl.CostEstimate(
                flops=slots * tile * tile * 150, bytes_accessed=slots * tile * tile, transcendentals=slots * tile
            ),
            compiler_params=PARAMS,
        )(*scalars, log_a, cost, k_all, f_pot, row_parts, box)

    got = xor(label_call(False)[0], "src", 1)
    f_pot, keep = label_call(True)
    n_y = n_src // 2
    pieces = pl.pallas_call(
        merge_kernel,
        out_shape=(piece,) * n_y,
        in_specs=[VM] * 2,
        out_specs=(VM,) * n_y,
        compiler_params=PARAMS,
    )(keep, got)
    far_first = (2, 1, 3)
    pieces = [pieces[0]] + [xor(pieces[q], "src", 2 * q) for q in far_first]
    done = pl.pallas_call(
        combine_kernel,
        out_shape=piece,
        in_specs=[VM] * (1 + n_y),
        out_specs=VM,
        compiler_params=PARAMS,
    )(log_b, *pieces)
    pieces = [done] + [xor(done, "src", 2 * q) for q in far_first]
    pieces = pieces + [xor(p, "src", 1) for p in pieces]
    order = (0,) + tuple(2 * q for q in far_first)
    order = order + tuple(k + 1 for k in order)
    f_pot, g_pot, out = pl.pallas_call(
        functools.partial(assemble_kernel, order),
        out_shape=(vec((rb * tile,)), vec((cb * tile,)), jax.ShapeDtypeStruct((classes, cb * tile), BF16)),
        in_specs=[VM] * (1 + n_src),
        out_specs=(VM,) * 3,
        scratch_shapes=[pltpu.VMEM((1, cb * tile), F32), pltpu.VMEM((1, rb * tile), F32)],
        compiler_params=PARAMS,
    )(f_pot, *pieces)
    return f_pot, g_pot, out.T


def solution(mesh):
    in_specs = (
        P("src", "tgt", None, None),
        P("src", "tgt"),
        P("src", "tgt"),
        P("src", "tgt"),
        P("src", "tgt"),
        P("src"),
        P("tgt"),
        P(("src", "tgt"), None),
    )
    out_specs = (P("src"), P("tgt"), P("tgt", None))
    return jax.shard_map(local, mesh=mesh, in_specs=in_specs, out_specs=out_specs, check_vma=False)
```
